32 devices in a mesh: rows: 8 (over z, y), cols: 4 (over x, core).
Axes of the slice: x: 2, y: 2, z: 4, core: 2. Of those that a mesh axis runs over, the one named last changes fastest.
Arguments:
- image_full: bfloat16 [32, 512, 512], P('rows', 'cols'), may hold values from -6 to 6
- image_half: bfloat16 [16, 256, 512], P('rows', 'cols'), may hold values from -6 to 6
- image_quarter: bfloat16 [8, 128, 512], P('rows', 'cols'), may hold values from -6 to 6
- row_pads: int32 [3], replicated, may hold values from 0 to 4
- tile_mask: int32 [8, 128], P('rows', 'cols'), may hold values 0 or 1
- aff_scale: float32 [512], replicated, may hold values from 0.1 to 1.9
- aff_shift: float32 [512], replicated, may hold values from -3 to 3
- conv_copy: bfloat16 [512, 9, 512], P(('rows', 'cols')), may hold values from -0.09375 to 0.09375
- heads_copy: bfloat16 [512, 7, 256], P(('rows', 'cols')), may hold values from -0.25 to 0.25
- gain: float32 [7, 256], replicated, may hold values from 0.1 to 1.9
- grad_out: bfloat16 [32, 512, 1792], P('rows', 'cols'), may hold values from -6 to 6
- step_count: int32 [1], replicated, may hold values from 1 to 20
- conv_master: float32 [512, 9, 512], P(('rows', 'cols')), may hold values from -0.09375 to 0.09375
- conv_first: float32 [512, 9, 512], P(('rows', 'cols')), may hold values from -64 to 64
- conv_second: float32 [512, 9, 512], P(('rows', 'cols')), may hold values from 2580.48 to 10321.92
- conv_left: float32 [512, 512], replicated, may hold values from -0.25 to 0.25
- conv_right: float32 [512, 512], replicated, may hold values from -0.25 to 0.25
- heads_master: float32 [512, 7, 256], P(('rows', 'cols')), may hold values from -0.25 to 0.25
- heads_first: float32 [512, 7, 256], P(('rows', 'cols')), may hold values from -64 to 64
- heads_second: float32 [512, 7, 256], P(('rows', 'cols')), may hold values from 2580.48 to 10321.92
- heads_left: float32 [7, 512, 512], replicated, may hold values from -0.25 to 0.25
- heads_right: float32 [7, 256, 256], replicated, may hold values from -0.375 to 0.375
- gain_first: float32 [7, 256], replicated, may hold values from -64 to 64
- gain_second: float32 [7, 256], replicated, may hold values from 2580.48 to 10321.92
Outputs:
- merged: bfloat16 [32, 512, 1792], P('rows', 'cols')
- grad_full: float32 [32, 512, 512], P('rows', 'cols')
- grad_half: float32 [16, 256, 512], P('rows', 'cols')
- grad_quarter: float32 [8, 128, 512], P('rows', 'cols')
- conv_grad: float32 [512, 9, 512], P(('rows', 'cols'))
- heads_grad: float32 [512, 7, 256], P(('rows', 'cols'))
- conv_first_new: float32 [512, 9, 512], P(('rows', 'cols'))
- conv_second_new: float32 [512, 9, 512], P(('rows', 'cols'))
- conv_master_new: float32 [512, 9, 512], P(('rows', 'cols'))
- conv_copy_new: bfloat16 [512, 9, 512], P(('rows', 'cols'))
- heads_first_new: float32 [512, 7, 256], P(('rows', 'cols'))
- heads_second_new: float32 [512, 7, 256], P(('rows', 'cols'))
- heads_master_new: float32 [512, 7, 256], P(('rows', 'cols'))
- heads_copy_new: bfloat16 [512, 7, 256], P(('rows', 'cols'))
- gain_grad: float32 [7, 256], replicated
- gain_first_new: float32 [7, 256], replicated
- gain_second_new: float32 [7, 256], replicated
- gain_new: float32 [7, 256], replicated
The draws below stay inside these ranges and needn't reach their ends.
Inputs may be any that keep to these rules, and one draw needn't show every extreme that they name: `row_pads`: each scale's padded rows lie at its bottom.
All inputs are finite; a program needn't handle non-finite values. No bound on the sum of `tile_mask` on one device may be relied on, other than what follows from the above.
Results may differ from the reference program's by a relative error of at most 0.014.
Values may be sent and summed in bfloat16 or wider, within the bound.
A program may use at most 192 MiB of HBM per device.

```python
import math
import jax
import jax.numpy as jnp
from jax import lax

C = 512
HD = 256
HEADS = 7
TILE = 4
H0 = 32
W0 = 512
NPIX = 21504


def touch_ends(array, stream_key, low, top_value):
    dims = array.shape
    place = [jax.random.randint(jax.random.fold_in(stream_key, axis), (), 0, dims[axis]) for axis in range(len(dims))]
    array = array.at[tuple(place)].set(low)
    longest = dims.index(max(dims))
    place[longest] = (place[longest] + 1) % dims[longest]
    return array.at[tuple(place)].set(top_value)


def steps_of(own_key, shape, shards, smallest, top_value):
    def one(dim, parts):
        steps = jax.random.uniform(jax.random.fold_in(jax.random.fold_in(own_key, 6), dim), (parts,), jnp.float32, smallest / len(shards), top_value / len(shards))
        return jnp.repeat(jnp.exp(steps), shape[dim] // parts).reshape((-1,) + (1,) * (len(shape) - dim - 1))

    loudness = one(*shards[0])
    for cut in shards[1:]:
        loudness = loudness * one(*cut)
    return loudness


def scatter_about(own_key, dims, deviation, bound, split=(), held_as=jnp.bfloat16):
    entries = deviation * jax.random.normal(own_key, dims, jnp.float32)
    if split:
        entries = entries * steps_of(own_key, dims, split, -0.22, 0.18)
    return jnp.clip(entries, -bound, bound).astype(held_as)


def setup_inputs(seed: int = 0) -> dict:
    streams_of = jax.random.split(jax.random.key(seed), 25)
    image_full = scatter_about(streams_of[0], (H0, W0, C), 1.0, 6.0, ((0, 8), (1, 4)))
    image_half = scatter_about(streams_of[1], (H0 // 2, W0 // 2, C), 1.0, 6.0, ((0, 8), (1, 4)))
    image_quarter = scatter_about(streams_of[2], (H0 // 4, W0 // 4, C), 1.0, 6.0, ((0, 8), (1, 4)))
    row_pads = jax.random.randint(streams_of[3], (3,), 0, H0 // 8 + 1).astype(jnp.int32)
    tile_mask = touch_ends((jax.random.randint(streams_of[4], (H0 // TILE, W0 // TILE), 0, 4) < 3).astype(jnp.int32), jax.random.fold_in(streams_of[4], 1), 0, 1)
    aff_scale = jnp.clip(1.0 + 0.18 * jax.random.normal(streams_of[5], (C,), jnp.float32), 0.1, 1.9)
    aff_shift = scatter_about(streams_of[6], (C,), 0.5, 3.0, (), jnp.float32)
    conv_copy = scatter_about(streams_of[7], (C, 9, C), (9 * C) ** -0.5, 0.09375, ((0, 32),))
    heads_copy = scatter_about(streams_of[8], (C, HEADS, HD), C ** -0.5, 0.25, ((0, 32),))
    gain = jnp.clip(1.0 + 0.18 * jax.random.normal(streams_of[9], (HEADS, HD), jnp.float32), 0.1, 1.9)
    grad_out = scatter_about(streams_of[10], (H0, W0, HEADS * HD), 1.0, 6.0, ((0, 8), (1, 4)))
    step_count = jax.random.randint(streams_of[11], (1,), 1, 21).astype(jnp.int32)
    conv_master = scatter_about(streams_of[12], (C, 9, C), (9 * C) ** -0.5, 0.09375, ((0, 32),), jnp.float32)
    conv_first = scatter_about(streams_of[13], (C, 9, C), (0.08 * NPIX ** 0.5), 64.0, ((0, 32),), jnp.float32)
    conv_second = jnp.clip(jnp.exp(math.log(10321.92) - 1.3862944 * jax.random.uniform(streams_of[14], (C, 9, C), jnp.float32) ** steps_of(streams_of[14], (C, 9, C), ((0, 32),), -0.2, 0.2)), 2580.48, 10321.92)
    conv_left = scatter_about(streams_of[15], (C, C), C ** -0.5, 0.25, (), jnp.float32)
    conv_right = scatter_about(streams_of[16], (C, C), C ** -0.5, 0.25, (), jnp.float32)
    heads_master = scatter_about(streams_of[17], (C, HEADS, HD), C ** -0.5, 0.25, ((0, 32),), jnp.float32)
    heads_first = scatter_about(streams_of[18], (C, HEADS, HD), (0.08 * NPIX ** 0.5), 64.0, ((0, 32),), jnp.float32)
    heads_second = jnp.clip(jnp.exp(math.log(10321.92) - 1.3862944 * jax.random.uniform(streams_of[19], (C, HEADS, HD), jnp.float32) ** steps_of(streams_of[19], (C, HEADS, HD), ((0, 32),), -0.2, 0.2)), 2580.48, 10321.92)
    heads_left = scatter_about(streams_of[20], (HEADS, C, C), C ** -0.5, 0.25, (), jnp.float32)
    heads_right = scatter_about(streams_of[21], (HEADS, HD, HD), HD ** -0.5, 0.375, (), jnp.float32)
    gain_first = scatter_about(streams_of[22], (HEADS, HD), (0.08 * NPIX ** 0.5), 64.0, (), jnp.float32)
    gain_second = jnp.clip(jnp.exp(jax.random.uniform(streams_of[23], (HEADS, HD), jnp.float32, math.log(2580.48), math.log(10321.92))), 2580.48, 10321.92)
    return {"image_full": image_full, "image_half": image_half, "image_quarter": image_quarter, "row_pads": row_pads, "tile_mask": tile_mask, "aff_scale": aff_scale, "aff_shift": aff_shift, "conv_copy": conv_copy, "heads_copy": heads_copy, "gain": gain, "grad_out": grad_out, "step_count": step_count, "conv_master": conv_master, "conv_first": conv_first, "conv_second": conv_second, "conv_left": conv_left, "conv_right": conv_right, "heads_master": heads_master, "heads_first": heads_first, "heads_second": heads_second, "heads_left": heads_left, "heads_right": heads_right, "gain_first": gain_first, "gain_second": gain_second}


beta_one = 0.95
beta_two = 0.95
adam_eps = 1e-08
norm_eps = 1e-06
learn_rate = 0.02
gain_rate = 1.0
weight_decay = 0.01

@jax.custom_vjp
def low(v):
    return lax.optimization_barrier(v.astype(jnp.bfloat16)).astype(jnp.float32)

@jax.custom_vjp
def low_back(v):
    return v

def low_keep(v):
    return (low(v), None)

def low_pass(kept, grad):
    return (grad,)

def back_keep(v):
    return (v, None)

def back_low(kept, grad):
    return (low(grad),)
low.defvjp(low_keep, low_pass)
low_back.defvjp(back_keep, back_low)

def conv_same(values, kernel):
    width = kernel.shape[0]
    shaped = kernel.reshape(width, 3, 3, kernel.shape[2]).transpose(1, 2, 0, 3)
    result = lax.conv_general_dilated(values[None], shaped, (1, 1), 'SAME', dimension_numbers=('NHWC', 'HWIO', 'NHWC'), precision=lax.Precision.HIGHEST)
    return result[0]

def enlarge(values, factor):
    return jnp.repeat(jnp.repeat(values, factor, axis=0), factor, axis=1)

def adam_parts(grad, first, second, step):
    first_new = beta_one * first + (1.0 - beta_one) * grad
    second_new = beta_two * second + (1.0 - beta_two) * grad * grad
    count = step[0].astype(jnp.float32)
    corr_one = 1.0 - jnp.power(jnp.float32(beta_one), count)
    corr_two = 1.0 - jnp.power(jnp.float32(beta_two), count)
    direction = first_new / corr_one / (jnp.sqrt(second_new / corr_two) + adam_eps)
    return (first_new, second_new, direction)

def reference(image_full, image_half, image_quarter, row_pads, tile_mask, aff_scale, aff_shift, conv_copy, heads_copy, gain, grad_out, step_count, conv_master, conv_first, conv_second, conv_left, conv_right, heads_master, heads_first, heads_second, heads_left, heads_right, gain_first, gain_second):
    high = lax.Precision.HIGHEST
    mask_up = enlarge(tile_mask.astype(jnp.float32), TILE)

    def forward(pic_full, pic_half, pic_quarter, kernel, heads_weight, gain_value):
        summed = jnp.zeros((H0, W0, HEADS, HD), jnp.float32)
        pictures = (pic_full, pic_half, pic_quarter)
        for scale_index in range(3):
            picture = pictures[scale_index]
            height = picture.shape[0]
            valid = (jnp.arange(height, dtype=jnp.int32) < height - row_pads[scale_index]).astype(jnp.float32)
            valid = valid[:, None, None]
            masked = low(picture * valid)
            pre_act = low_back(conv_same(masked, kernel))
            biased = pre_act * aff_scale + aff_shift
            active = low(jax.nn.relu(biased) * valid)
            hidden = low_back(jnp.einsum('hwc,ctd->hwtd', active, heads_weight, precision=high))
            inverse = lax.rsqrt(lax.optimization_barrier(jnp.mean(hidden * hidden, axis=-1, keepdims=True)) + norm_eps)
            normed = gain_value * (hidden * inverse)
            summed = summed + enlarge(normed, 2 ** scale_index)
        return (mask_up[:, :, None, None] * summed).reshape(H0, W0, HEADS * HD)
    inputs = (image_full.astype(jnp.float32), image_half.astype(jnp.float32), image_quarter.astype(jnp.float32), conv_copy.astype(jnp.float32), heads_copy.astype(jnp.float32), gain)
    merged, pull = jax.vjp(forward, *inputs)
    grads = pull(grad_out.astype(jnp.float32))
    grad_full, grad_half, grad_quarter, conv_grad, heads_grad, gain_grad = grads
    conv_rot = jnp.einsum('ci,ckj->ikj', conv_left, conv_grad, precision=high)
    conv_rot = jnp.einsum('ikj,jl->ikl', conv_rot, conv_right, precision=high)
    conv_first_new, conv_second_new, conv_dir = adam_parts(conv_rot, conv_first, conv_second, step_count)
    conv_update = jnp.einsum('ci,ikl->ckl', conv_left, conv_dir, precision=high)
    conv_update = jnp.einsum('ckl,jl->ckj', conv_update, conv_right, precision=high)
    conv_master_new = conv_master - learn_rate * (conv_update + weight_decay * conv_master)
    heads_rot = jnp.einsum('tci,ctj->itj', heads_left, heads_grad, precision=high)
    heads_rot = jnp.einsum('itj,tjl->itl', heads_rot, heads_right, precision=high)
    heads_first_new, heads_second_new, heads_dir = adam_parts(heads_rot, heads_first, heads_second, step_count)
    heads_update = jnp.einsum('tci,itl->ctl', heads_left, heads_dir, precision=high)
    heads_update = jnp.einsum('ctl,tjl->ctj', heads_update, heads_right, precision=high)
    heads_master_new = heads_master - learn_rate * (heads_update + weight_decay * heads_master)
    gain_first_new, gain_second_new, gain_dir = adam_parts(gain_grad, gain_first, gain_second, step_count)
    gain_new = gain - gain_rate * (gain_dir + weight_decay * gain)
    return (merged.astype(jnp.bfloat16), grad_full, grad_half, grad_quarter, conv_grad, heads_grad, conv_first_new, conv_second_new, conv_master_new, conv_master_new.astype(jnp.bfloat16), heads_first_new, heads_second_new, heads_master_new, heads_master_new.astype(jnp.bfloat16), gain_grad, gain_first_new, gain_second_new, gain_new)
```

```python
import functools

import jax
import jax.numpy as jnp
from jax import lax
from jax.experimental import pallas as pl
from jax.experimental.pallas import tpu as pltpu
from jax.sharding import PartitionSpec as P

beta_one = 0.95
beta_two = 0.95
adam_eps = 1e-08
norm_eps = 1e-06
learn_rate = 0.02
gain_rate = 1.0
weight_decay = 0.01

MESH = pl.DeviceIdType.MESH
BF16 = jnp.bfloat16
F32 = jnp.float32
GROUP = 16
CHUNKS = 5
TAPS = 9


def nn(a, b):
    return jnp.dot(a, b, preferred_element_type=F32)


def nt(a, b):
    return lax.dot_general(a, b, (((1,), (1,)), ((), ())), preferred_element_type=F32)


def tn(a, b):
    return lax.dot_general(a, b, (((0,), (0,)), ((), ())), preferred_element_type=F32)


class Dim:
    def __init__(self, size, row_step, col_step):
        self.size, self.row_step, self.col_step = size, row_step, col_step

    def coord(self, r, c):
        if self.row_step:
            return lax.rem(lax.div(r, self.row_step), self.size)
        return lax.rem(lax.div(c, self.col_step), self.size)


class Slice:
    def __init__(self, mesh, rows_per_device):
        self.rows, self.cols = mesh.devices.shape
        self.share = max(1, GROUP // rows_per_device)
        place = {}
        try:
            for r in range(self.rows):
                for c in range(self.cols):
                    device = mesh.devices[r, c]
                    place[(*device.coords, device.core_on_chip)] = (r, c)
        except AttributeError:
            place = {}
            for r in range(self.rows):
                for c in range(self.cols):
                    if self.rows == 8:
                        key = (c // 2, r % 2, r // 2, c % 2)
                    else:
                        key = (c, r // 8, r // 2 % 4, r % 2)
                    place[key] = (r, c)
        origin = tuple(min(k[a] for k in place) for a in range(4))
        dims = []
        for axis in range(4):
            size = max(k[axis] for k in place) - origin[axis] + 1
            step = list(origin)
            step[axis] += 1
            there = place[tuple(step)]
            dims.append(Dim(size, *there))
        self.core = dims[3]
        chips = dims[:3]
        inside = [d for d in chips if d.row_step == 0 and d.col_step < self.share]
        lines = [d for d in chips if d not in inside]
        lines.sort(key=lambda d: -d.size)
        self.lines = lines
        self.chips = lines + inside
        self.groups = self.rows * self.cols // self.share


class Here:
    def __init__(self, s):
        self.s = s
        self.r = lax.axis_index("rows")
        self.c = lax.axis_index("cols")
        self.place = {d: d.coord(self.r, self.c) for d in [*s.chips, s.core]}

    def at(self, dim):
        return self.place[dim]

    def moved(self, steps):
        r, c = self.r, self.c
        for dim, there in steps:
            delta = there - self.at(dim)
            r = r + delta * dim.row_step
            c = c + delta * dim.col_step
        return r, c

    def ahead(self, dim, step):
        return lax.rem(self.at(dim) + step, dim.size)

    def behind(self, dim, step):
        return lax.rem(self.at(dim) + dim.size - step, dim.size)

    def group(self, place):
        r, c = place
        return lax.div(r * self.s.cols + c, self.s.share)


def remote(src, dst, send, recv, where):
    return pltpu.make_async_remote_copy(
        src_ref=src, dst_ref=dst, send_sem=send, recv_sem=recv, device_id=where, device_id_type=MESH
    )


def gather_plan(s):
    lines = s.lines
    first = lines[0]
    plans = []
    for s0 in range(first.size):
        rest = list(lines[1:])
        if s0 >= (first.size + 1) // 2:
            rest.reverse()
        onward = [(d, st) for d in rest for st in range(1, d.size)]
        if s0 == 0:
            own = [(first, st) for st in range(1, first.size)] + onward
        else:
            plans.append((0, ((first, s0),), (first, s0), onward))
        if rest:
            for s1 in range(1, rest[0].size):
                on = [(d, st) for d in rest[1:] for st in range(1, d.size)]
                plans.append((1, ((first, s0), (rest[0], s1)), (rest[0], s1), on))
            for d in rest[1:]:
                for s2 in range(1, d.size):
                    for s1 in range(rest[0].size):
                        plans.append((2, ((first, s0), (rest[0], s1), (d, s2)), (d, s2), []))
    plans.sort(key=lambda p: p[0])
    return own, plans


def log2(n):
    return n.bit_length() - 1


def train_kernel(s, shapes, refs):
    (conv_w, head_w, full_ref, half_ref, quarter_ref, pads, tile_ref, scale_ref, shift_ref, gain_ref, go_ref,
     merged_ref, gfull_ref, ghalf_ref, gquarter_ref, unit_ref, gainsum_ref,
     W, Z, MK, HR, HC, TS, CS, HR2, HC2, TS2, CS2, MKF, U, UT, PRE, GA, ACT, GP, GG, GX,
     A, AH, SC, SCH, RC, RCH, SB, SBH, R1, R2, R3,
     ag_send, ag_recv, halo_send, halo_recv, core_send, core_recv, rs_send, rs1_recv, rs2_recv, rs3_recv,
     gx_send, gx_recv) = refs
    here = Here(s)
    C, HD, HEADS = shapes["C"], shapes["HD"], shapes["HEADS"]
    sizes = shapes["sizes"]
    counts = [a * b for a, b in sizes]
    offs = [0, counts[0], counts[0] + counts[1]]
    n_pix = sum(counts)
    n_rest = n_pix - counts[0]
    half = C // 2
    r, c = here.r, here.c
    core = here.at(s.core)
    sibling = here.moved([(s.core, 1 - core)])

    for ref in (HR, HC, HR2, HC2, CS, CS2):
        ref[...] = jnp.zeros_like(ref)
    own_group = here.group((r, c))
    for k in range(TAPS):
        W[own_group, :, k * C : (k + 1) * C] = conv_w[k]
    for t in range(HEADS):
        W[own_group, :, TAPS * C + t * HD : TAPS * C + (t + 1) * HD] = head_w[t]

    barrier = pltpu.get_barrier_semaphore()
    greeted = [sibling]
    for d in s.chips:
        greeted += [here.moved([(d, here.ahead(d, st))]) for st in range(1, d.size)]
    greeted += [
        (lax.rem(r + 1, s.rows), c), (lax.rem(r + s.rows - 1, s.rows), c),
        (r, lax.rem(c + 1, s.cols)), (r, lax.rem(c + s.cols - 1, s.cols)),
    ]
    for g in greeted:
        pl.semaphore_signal(barrier, inc=1, device_id=g, device_id_type=MESH)

    def valid_of(scale, row):
        rows_here = sizes[scale][0]
        limit = rows_here * s.rows - pads[scale]
        return jnp.where(r * rows_here + row < limit, 1.0, 0.0).astype(F32)

    pictures = (full_ref, half_ref, quarter_ref)
    segments = [(sc, row, offs[sc] + row * sizes[sc][1], sizes[sc][1]) for sc in range(3) for row in range(sizes[sc][0])]
    for sc, row, start, count in segments:
        MK[start : start + count, :] = (pictures[sc][row].astype(F32) * valid_of(sc, row)).astype(BF16)

    strip_at = [0, sizes[0][1], sizes[0][1] + sizes[1][1]]
    padded_rows = [(sc, j) for sc in range(3) for j in range(sizes[sc][0] + 2)]

    def pixel_row(pixels, sc, row):
        start = offs[sc] + row * sizes[sc][1]
        return pixels[start : start + sizes[sc][1], :]

    def stage_strips(pixels, strips):
        for sc in range(3):
            lanes = slice(strip_at[sc], strip_at[sc] + sizes[sc][1])
            strips[0, lanes, :] = pixel_row(pixels, sc, 0)
            strips[1, lanes, :] = pixel_row(pixels, sc, sizes[sc][0] - 1)

    sides = [
        (r > 0, (r - 1, c)), (r < s.rows - 1, (r + 1, c)),
        (c > 0, (r, c - 1)), (c < s.cols - 1, (r, c + 1)),
    ]

    def side_copy(which, side, staged, landing):
        there, where = sides[side]
        end = side % 2
        return there, remote(staged.at[end], landing.at[1 - end], halo_send.at[which, side], halo_recv.at[which, side ^ 1], where)

    def send_sides(which, pair, staged, landing):
        for side in pair:
            there, copy = side_copy(which, side, staged, landing)
            pl.when(there)(copy.start)

    def wait_sides(which, pair, staged, landing, do):
        for side in pair:
            there, where = sides[side]
            end = side % 2
            copy = remote(staged.at[end], landing.at[end], halo_send.at[which, side], halo_recv.at[which, side], where)
            pl.when(there)(copy.wait_recv if do == "recv" else copy.wait_send)

    def padded(pixels, rims, sc, j):
        lanes = slice(strip_at[sc], strip_at[sc] + sizes[sc][1])
        if j == 0:
            return rims[0, lanes, :]
        if j == sizes[sc][0] + 1:
            return rims[1, lanes, :]
        return pixel_row(pixels, sc, j - 1)

    def stage_columns(pixels, rims, columns):
        for index, (sc, j) in enumerate(padded_rows):
            x = padded(pixels, rims, sc, j).astype(F32)
            columns[0, index : index + 1, :] = x[0:1]
            columns[1, index : index + 1, :] = x[sizes[sc][1] - 1 :]

    def put_windows(sc, j, b, value):
        for a in range(3):
            row = j - a
            if 0 <= row < sizes[sc][0]:
                start = offs[sc] + row * sizes[sc][1]
                Z[3 * a + b, start : start + sizes[sc][1], :] = value

    def windows_middle(pixels, rims):
        for sc, j in padded_rows:
            put_windows(sc, j, 1, padded(pixels, rims, sc, j))

    def windows_sides(pixels, rims, ends):
        for index, (sc, j) in enumerate(padded_rows):
            count = sizes[sc][1]
            x = padded(pixels, rims, sc, j).astype(F32)
            place = lax.broadcasted_iota(jnp.int32, (count, C), 0)
            before = jnp.where(place == 0, ends[0, index : index + 1, :], pltpu.roll(x, 1, 0))
            after = jnp.where(place == count - 1, ends[1, index : index + 1, :], pltpu.roll(x, count - 1, 0))
            put_windows(sc, j, 0, before.astype(BF16))
            put_windows(sc, j, 2, after.astype(BF16))

    stage_strips(MK, TS)
    pl.semaphore_wait(barrier, len(greeted))
    send_sides(0, (0, 1), TS, HR)

    own_sends, plan = gather_plan(s)
    lanes_all = TAPS * C + HEADS * HD
    width = lanes_all // CHUNKS
    n_arrive = len(plan)

    def block_of(offsets):
        return here.moved([(d, here.behind(d, st)) for d, st in offsets if st])

    arrival_key = {}
    for index, (_, offsets, along, _) in enumerate(plan):
        full = tuple(sum(st for dd, st in offsets if dd is d) for d in s.lines)
        arrival_key[full] = index
    sends = []
    for d, st in own_sends:
        full = tuple(st if dd is d else 0 for dd in s.lines)
        sends.append((-1, d, st, arrival_key[full]))
    for index, (_, offsets, _, onward) in enumerate(plan):
        for d, st in onward:
            full = tuple(sum(s2 for dd, s2 in offsets if dd is e) + (st if e is d else 0) for e in s.lines)
            sends.append((index, d, st, arrival_key[full]))
    n_sends = len(sends)

    def lanes_of(ch):
        return pl.ds(pl.multiple_of(ch * width, width), width)

    def place_of(index):
        return (r, c) if index < 0 else block_of(plan[index][1])

    def pass_on(ch, index):
        group = here.group(place_of(index))
        block = W.at[group, :, lanes_of(ch)]
        for number, (source, d, st, lands) in enumerate(sends):
            if source == index:
                remote(block, block, ag_send.at[ch, number], ag_recv.at[ch, lands],
                       here.moved([(d, here.ahead(d, st))])).start()
        remote(block, block, ag_send.at[ch, n_sends + index + 1],
               ag_recv.at[ch, n_arrive + index + 1], sibling).start()

    def arrive(ch, index):
        block = W.at[here.group(place_of(index)), :, lanes_of(ch)]
        remote(block, block, ag_send.at[ch, 0], ag_recv.at[ch, index], sibling).wait_recv()

    def arrive_sibling(ch, index):
        place = place_of(index)
        moved = (place[0] + (1 - 2 * core) * s.core.row_step, place[1] + (1 - 2 * core) * s.core.col_step)
        block = W.at[here.group(moved), :, lanes_of(ch)]
        remote(block, block, ag_send.at[ch, 0], ag_recv.at[ch, n_arrive + index + 1], sibling).wait_recv()

    pass_on(0, -1)

    def taps_of(ch):
        done = lambda n: jnp.minimum(lax.div(n * width, C), TAPS)
        return done(ch), done(ch + 1)

    def conv_tap(k, carry):
        kernel = W[:, :, pl.ds(pl.multiple_of(k * C, C), C)].reshape(C, C)
        PRE[...] += nn(Z[k], kernel)
        return carry

    PRE[...] = jnp.zeros_like(PRE)

    tile_rows = sizes[0][0]
    tile_cols = sizes[0][1] // tile_ref.shape[1]
    per_tile = log2(tile_cols)
    cell = (sizes[0][1], tile_ref.shape[1])
    column = lax.broadcasted_iota(jnp.int32, cell, 0)
    tile = lax.broadcasted_iota(jnp.int32, cell, 1)
    picked = jnp.where((column >> per_tile) == tile, tile_ref[...].astype(F32), 0.0)
    mask_row = jnp.sum(picked, axis=1, keepdims=True)
    mask_row = jnp.broadcast_to(mask_row, (sizes[0][1], HD))
    for row in range(tile_rows):
        MKF[row * sizes[0][1] : (row + 1) * sizes[0][1], :] = mask_row

    def coarse(full_pixel):
        row = full_pixel >> log2(sizes[0][1])
        col = full_pixel & (sizes[0][1] - 1)
        one = (row >> 1) * sizes[1][1] + (col >> 1)
        two = counts[1] + (row >> 2) * sizes[2][1] + (col >> 2)
        return one, two

    one, two = coarse(lax.broadcasted_iota(jnp.int32, (counts[0], n_rest), 0))
    rest = lax.broadcasted_iota(jnp.int32, (counts[0], n_rest), 1)
    U[...] = jnp.where((one == rest) | (two == rest), 1.0, 0.0).astype(BF16)
    one, two = coarse(lax.broadcasted_iota(jnp.int32, (n_rest, counts[0]), 1))
    rest = lax.broadcasted_iota(jnp.int32, (n_rest, counts[0]), 0)
    UT[...] = jnp.where((one == rest) | (two == rest), 1.0, 0.0).astype(BF16)

    early = [i for i, p in enumerate(plan) if p[0] < 2]
    late = [i for i, p in enumerate(plan) if p[0] == 2]

    def chunk(ch, carry):
        for index in early:
            arrive(ch, index)
            pass_on(ch, index)

        @pl.when(ch < CHUNKS - 1)
        def _():
            pass_on(ch + 1, -1)

        @pl.when(ch == 0)
        def _():
            wait_sides(0, (0, 1), TS, HR, "recv")
            stage_columns(MK, HR, CS)
            send_sides(0, (2, 3), CS, HC)
            windows_middle(MK, HR)

        @pl.when(ch == 1)
        def _():
            wait_sides(0, (2, 3), CS, HC, "recv")
            windows_sides(MK, HR, HC)

        @pl.when(ch > 0)
        def _():
            low, high = taps_of(ch - 1)
            lax.fori_loop(low, high, conv_tap, 0)

        for index in late:
            arrive(ch, index)
            pass_on(ch, index)
        for index in range(-1, n_arrive):
            arrive_sibling(ch, index)
        return carry

    lax.fori_loop(0, CHUNKS, chunk, 0)
    wait_sides(0, (0, 1), TS, HR, "send")
    wait_sides(0, (2, 3), CS, HC, "send")

    for sc, row, start, count in segments:
        biased = PRE[start : start + count, :] * scale_ref[...] + shift_ref[...]
        ACT[start : start + count, :] = (jnp.maximum(biased, 0.0) * valid_of(sc, row)).astype(BF16)

    own_half = pl.ds(pl.multiple_of(core * half, half), half)
    other_half = pl.ds(pl.multiple_of((1 - core) * half, half), half)
    GA[...] = jnp.zeros_like(GA)
    GG[...] = jnp.zeros_like(GG)

    def core_copy(b, staged, landing):
        return remote(staged, landing, core_send.at[b], core_recv.at[b], sibling)

    def head(t, carry):
        weights = W[:, :, pl.ds(pl.multiple_of(TAPS * C + t * HD, HD), HD)].reshape(C, HD)
        hidden = nn(ACT[...], weights)
        inverse = lax.rsqrt(jnp.mean(hidden * hidden, axis=-1, keepdims=True) + norm_eps)
        unit = hidden * inverse
        gain = gain_ref[pl.ds(t, 1), :]
        normed = gain * unit
        small = normed[counts[0] :]
        small_high = small.astype(BF16)
        small_low = (small - small_high.astype(F32)).astype(BF16)
        lifted = nn(U[...], small_high) + nn(U[...], small_low)
        lanes = pl.ds(pl.multiple_of(t * HD, HD), HD)
        merged_ref[:, lanes] = (MKF[...] * (normed[: counts[0]] + lifted)).astype(BF16)
        back = go_ref[:, lanes].astype(F32) * MKF[...]
        pooled = jnp.concatenate([back, nn(UT[...], back.astype(BF16))], axis=0)
        product = pooled * unit
        GG[pl.ds(t, 1), :] = jnp.sum(product, axis=0, keepdims=True)
        middle = jnp.mean(gain * product, axis=-1, keepdims=True)
        grad_hidden = (inverse * (gain * pooled - unit * middle)).astype(BF16)
        SCH[t] = tn(ACT[:, other_half], grad_hidden).astype(BF16)
        core_copy(TAPS + t, SCH.at[t], RCH.at[t]).start()
        AH[t] = tn(ACT[:, own_half], grad_hidden)
        GA[...] += nt(grad_hidden, weights)
        return carry

    lax.fori_loop(0, HEADS, head, 0)

    sum_dims = [s.core] + list(reversed(s.chips))

    def gain_send(stage):
        d = sum_dims[stage]
        mine = here.at(d)
        GX[stage, mine] = GG[...]
        for st in range(1, d.size):
            remote(GX.at[stage, mine], GX.at[stage, mine], gx_send.at[stage, st], gx_recv.at[stage, st],
                   here.moved([(d, here.ahead(d, st))])).start()

    def gain_add(stage):
        d = sum_dims[stage]
        for st in range(1, d.size):
            slot = here.behind(d, st)
            remote(GX.at[stage, slot], GX.at[stage, slot], gx_send.at[stage, st], gx_recv.at[stage, st], sibling).wait_recv()
        total = GX[stage, 0]
        for i in range(1, d.size):
            total = total + GX[stage, i]
        GG[...] = total

    gain_send(0)

    for sc, row, start, count in segments:
        pre = PRE[start : start + count, :]
        biased = pre * scale_ref[...] + shift_ref[...]
        grad = jnp.where(biased > 0.0, GA[start : start + count, :], 0.0)
        GP[start : start + count, :] = (scale_ref[...] * grad * valid_of(sc, row)).astype(BF16)
    stage_strips(GP, TS2)
    send_sides(1, (0, 1), TS2, HR2)

    d0, d1, d2 = s.chips
    quarter = half // 2

    def home(b):
        return {d0: lax.div(b, 4), d1: lax.rem(lax.div(b, 2), 2), d2: lax.rem(b, 2)}

    conv_set = (A, SC, RC, SB, C)
    head_set = (AH, SCH, RCH, SBH, HD)

    def rows_of(part):
        return slice(part * quarter, (part + 1) * quarter)

    def ways(part):
        return (d1, d2) if part == 0 else (d2, d1)

    def landing(stage, b, part, slot, lanes):
        place = home(b)
        if stage == 1:
            which = place[d0] * 2 + place[ways(part)[1]]
            return R1.at[part, which, slot, :, 0:lanes], rs1_recv.at[part, which, slot]
        if stage == 2:
            return R2.at[part, place[d0], slot, :, 0:lanes], rs2_recv.at[part, place[d0], slot]
        return R3.at[part, slot, :, 0:lanes], rs3_recv.at[part, slot]

    def ship(stage, b, i, group, part, dim):
        total, _, _, staged, lanes = group
        place = home(b)
        staged[i, rows_of(part), :] = total[i, rows_of(part), :].astype(BF16)
        for st in range(1, dim.size):
            @pl.when(lax.rem(place[dim] + st, dim.size) == here.at(dim))
            def _():
                buffer, sem = landing(stage, b, part, st - 1, lanes)
                remote(staged.at[i, rows_of(part), :], buffer, rs_send.at[b, part], sem,
                       here.moved([(dim, place[dim])])).start()

    def take(stage, b, i, group, part, dim):
        total, _, _, staged, lanes = group
        for st in range(1, dim.size):
            buffer, sem = landing(stage, b, part, st - 1, lanes)
            remote(staged.at[i, rows_of(part), :], buffer, rs_send.at[b, part], sem, sibling).wait_recv()
            total[i, rows_of(part), :] += buffer[...].astype(F32)

    def first_ship(b, i, group):
        total, staged, landed, _, _ = group
        core_copy(b, staged.at[i], landed.at[i]).wait_recv()
        total[i] += landed[i].astype(F32)
        place = home(b)
        for part in (0, 1):
            dim = ways(part)[0]

            @pl.when(here.at(dim) != place[dim])
            def _():
                ship(1, b, i, group, part, dim)

    def second_ship(b, i, group):
        place = home(b)
        for part in (0, 1):
            dim, then = ways(part)

            @pl.when(here.at(dim) == place[dim])
            def _():
                take(1, b, i, group, part, dim)

                @pl.when(here.at(then) != place[then])
                def _():
                    ship(2, b, i, group, part, then)

    def third_ship(b, i, group):
        place = home(b)
        for part in (0, 1):
            @pl.when((here.at(d1) == place[d1]) & (here.at(d2) == place[d2]))
            def _():
                take(2, b, i, group, part, ways(part)[1])

                @pl.when(here.at(d0) != place[d0])
                def _():
                    ship(3, b, i, group, part, d0)

    def is_home(b):
        place = home(b)
        return (here.at(d0) == place[d0]) & (here.at(d1) == place[d1]) & (here.at(d2) == place[d2])

    def last_take(b, i, group):
        @pl.when(is_home(b))
        def _():
            for part in (0, 1):
                take(3, b, i, group, part, d0)
            unit_ref[:, 0 : group[4]] = group[0][i]

    def over_heads(step):
        def body(t, carry):
            step(TAPS + t, t, head_set)
            return carry
        lax.fori_loop(0, HEADS, body, 0)

    over_heads(first_ship)
    gain_add(0)
    gain_send(1)

    def conv_grad(k, carry):
        SC[k] = tn(Z[k, :, other_half], GP[...]).astype(BF16)
        core_copy(k, SC.at[k], RC.at[k]).start()
        A[k] = tn(Z[k, :, own_half], GP[...])

        @pl.when(k > 0)
        def _():
            first_ship(k - 1, k - 1, conv_set)
        return carry

    lax.fori_loop(0, TAPS, conv_grad, 0)
    first_ship(TAPS - 1, TAPS - 1, conv_set)
    wait_sides(1, (0, 1), TS2, HR2, "recv")
    stage_columns(GP, HR2, CS2)
    send_sides(1, (2, 3), CS2, HC2)
    over_heads(second_ship)
    gain_add(1)
    gain_send(2)
    windows_middle(GP, HR2)
    wait_sides(1, (2, 3), CS2, HC2, "recv")
    windows_sides(GP, HR2, HC2)
    PRE[...] = jnp.zeros_like(PRE)

    def image_grad(k, carry):
        second_ship(k, k, conv_set)
        kernel = W[:, :, pl.ds(pl.multiple_of(k * C, C), C)].reshape(C, C)
        PRE[...] += nt(Z[TAPS - 1 - k], kernel)
        return carry

    lax.fori_loop(0, TAPS, image_grad, 0)
    over_heads(third_ship)
    gain_add(2)
    gain_send(3)
    outs = (gfull_ref, ghalf_ref, gquarter_ref)
    for sc, row, start, count in segments:
        outs[sc][row] = PRE[start : start + count, :] * valid_of(sc, row)

    def conv_third(k, carry):
        third_ship(k, k, conv_set)
        return carry

    lax.fori_loop(0, TAPS, conv_third, 0)
    over_heads(last_take)

    def conv_last(k, carry):
        last_take(k, k, conv_set)
        return carry

    lax.fori_loop(0, TAPS, conv_last, 0)
    gain_add(3)
    gainsum_ref[...] = GG[...]

    def sent_chunk(ch, carry):
        block = W.at[0, :, lanes_of(ch)]
        for number in range(n_sends + n_arrive + 1):
            remote(block, block, ag_send.at[ch, number], ag_recv.at[ch, 0], sibling).wait_send()
        return carry

    lax.fori_loop(0, CHUNKS, sent_chunk, 0)
    wait_sides(1, (0, 1), TS2, HR2, "send")
    wait_sides(1, (2, 3), CS2, HC2, "send")
    for stage, d in enumerate(sum_dims):
        for st in range(1, d.size):
            remote(GX.at[stage, 0], GX.at[stage, 0], gx_send.at[stage, st], gx_recv.at[stage, st], sibling).wait_send()

    def sent_block(b, i, group):
        _, staged, landed, sb, _ = group
        core_copy(b, staged.at[i], landed.at[i]).wait_send()
        gone = jnp.logical_not(is_home(b))
        for part in (0, 1):
            @pl.when(gone)
            def _():
                piece = sb.at[i, rows_of(part), :]
                remote(piece, piece, rs_send.at[b, part], rs_send.at[b, part], sibling).wait_send()

    over_heads(sent_block)

    def conv_sent(k, carry):
        sent_block(k, k, conv_set)
        return carry

    lax.fori_loop(0, TAPS, conv_sent, 0)


def train_call(s, shapes, args):
    C, HD, HEADS, sizes = shapes["C"], shapes["HD"], shapes["HEADS"], shapes["sizes"]
    counts = [a * b for a, b in sizes]
    n_pix = sum(counts)
    half = C // 2
    strip = sum(b for _, b in sizes)
    padded = -(-sum(a + 2 for a, _ in sizes) // 8) * 8
    own_sends, plan = gather_plan(s)
    n_arrive = len(plan)
    n_sends = len(own_sends) + sum(len(p[3]) for p in plan)
    d0, d1, d2 = s.chips
    most = max(d1.size, d2.size) - 1
    lanes_all = TAPS * C + HEADS * HD
    heads_pad = -(-HEADS // 8) * 8
    dma = pltpu.SemaphoreType.DMA
    vm = pltpu.VMEM
    longest = max(s.core.size, *(d.size for d in s.chips))
    scratch = [
        vm((s.groups, GROUP, lanes_all), BF16),
        vm((TAPS, n_pix, C), BF16),
        vm((n_pix, C), BF16),
        vm((2, strip, C), BF16), vm((2, padded, C), F32), vm((2, strip, C), BF16), vm((2, padded, C), F32),
        vm((2, strip, C), BF16), vm((2, padded, C), F32), vm((2, strip, C), BF16), vm((2, padded, C), F32),
        vm((counts[0], HD), F32),
        vm((counts[0], n_pix - counts[0]), BF16), vm((n_pix - counts[0], counts[0]), BF16),
        vm((n_pix, C), F32), vm((n_pix, C), F32),
        vm((n_pix, C), BF16), vm((n_pix, C), BF16),
        vm((heads_pad, HD), F32), vm((4, longest, heads_pad, HD), F32),
        vm((TAPS, half, C), F32), vm((HEADS, half, HD), F32),
        vm((TAPS, half, C), BF16), vm((HEADS, half, HD), BF16),
        vm((TAPS, half, C), BF16), vm((HEADS, half, HD), BF16),
        vm((TAPS, half, C), BF16), vm((HEADS, half, HD), BF16),
        vm((2, 8, most, half // 2, C), BF16), vm((2, 4, most, half // 2, C), BF16),
        vm((2, d0.size - 1, half // 2, C), BF16),
        dma((CHUNKS, n_sends + n_arrive + 1)), dma((CHUNKS, 2 * n_arrive + 1)),
        dma((2, 4)), dma((2, 4)),
        dma((TAPS + HEADS,)), dma((TAPS + HEADS,)),
        dma((TAPS + HEADS, 2)), dma((2, 8, most)), dma((2, 4, most)), dma((2, d0.size - 1)),
        dma((4, longest)), dma((4, longest)),
    ]
    out_shape = (
        jax.ShapeDtypeStruct((counts[0], HEADS * HD), BF16),
        *(jax.ShapeDtypeStruct((a, b, C), F32) for a, b in sizes),
        jax.ShapeDtypeStruct((half, C), F32),
        jax.ShapeDtypeStruct((heads_pad, HD), F32),
    )
    vmem = pl.BlockSpec(memory_space=pltpu.VMEM)
    smem = pl.BlockSpec(memory_space=pltpu.SMEM)

    def kernel(*refs):
        train_kernel(s, shapes, refs)

    return pl.pallas_call(
        kernel,
        name="train",
        out_shape=out_shape,
        in_specs=[vmem] * 5 + [smem] + [vmem] * 5,
        out_specs=[vmem] * 6,
        scratch_shapes=scratch,
        compiler_params=pltpu.CompilerParams(collective_id=0, has_side_effects=True, vmem_limit_bytes=62 << 20),
        cost_estimate=pl.CostEstimate(flops=13 * 10**9, bytes_accessed=10**7, transcendentals=0),
    )(*args)


def soap_kernel(s, shapes, refs):
    (unit_ref, cfirst, csecond, hfirst, hsecond, step_ref, cleft, cright, hleft, hright,
     got_ref, goth_ref,
     FT, FTH, FB, LV, RV, LB, RB, TB, VB, ROT, OUT,
     first_send, first_recv, base_sem, core_send, core_recv, out_send, out_recv) = refs
    here = Here(s)
    C, HD, HEADS = shapes["C"], shapes["HD"], shapes["HEADS"]
    half = C // 2
    r, c = here.r, here.c
    core = here.at(s.core)
    d0, d1, d2 = s.chips
    blocks = TAPS + HEADS
    tiles = half // GROUP
    mine = here.group((r, c))
    my_half = lax.div(mine, tiles)
    my_tile = lax.rem(mine, tiles)
    block = here.at(d0) * 4 + here.at(d1) * 2 + here.at(d2)
    at_home = (here.at(d1) < 2) & (here.at(d2) < 2)
    is_conv = at_home & (block < TAPS)
    is_head = at_home & (block >= TAPS)
    sibling = here.moved([(s.core, 1 - core)])

    def owner(b):
        return here.moved([(d0, lax.div(b, 4)), (d1, lax.rem(lax.div(b, 2), 2)), (d2, lax.rem(b, 2)), (s.core, my_half)])

    def holder(i, copy):
        device = (core * tiles + i) * s.share + copy
        return lax.div(device, s.cols), lax.rem(device, s.cols)

    def is_me(where):
        return (where[0] == r) & (where[1] == c)

    barrier = pltpu.get_barrier_semaphore()

    def greet(where):
        @pl.when(jnp.logical_not(is_me(where)))
        def _():
            pl.semaphore_signal(barrier, inc=1, device_id=where, device_id_type=MESH)

    def greet_owner(b, carry):
        greet(owner(b))
        return carry

    lax.fori_loop(0, blocks, greet_owner, 0)

    @pl.when(at_home)
    def _():
        def greet_holder(i, carry):
            for copy in range(s.share):
                greet(holder(i, copy))
            return carry
        lax.fori_loop(0, tiles, greet_holder, 0)

    def bases(conv, t, do):
        if conv:
            copies = [pltpu.make_async_copy(cleft, LV, base_sem.at[0]), pltpu.make_async_copy(cright, RV, base_sem.at[1])]
        else:
            copies = [pltpu.make_async_copy(hleft.at[t], LV, base_sem.at[0]),
                      pltpu.make_async_copy(hright.at[t], RV.at[0:HD, 0:HD], base_sem.at[1])]
        for copy in copies:
            copy.start() if do == "start" else copy.wait()

    pl.when(is_conv)(lambda: bases(True, 0, "start"))
    pl.when(is_head)(lambda: bases(False, block - TAPS, "start"))

    for k in range(TAPS):
        FT[k, 0] = cfirst[k].astype(BF16)
        FT[k, 1] = csecond[k].astype(BF16)
    for t in range(HEADS):
        FTH[t, 0] = hfirst[t].astype(BF16)
        FTH[t, 1] = hsecond[t].astype(BF16)

    same = my_half == core
    n_greets = blocks - same.astype(jnp.int32)
    n_home = s.share * tiles - same.astype(jnp.int32)
    pl.semaphore_wait(barrier, jnp.where(at_home, n_greets + n_home, blocks))

    sends_rows = (lax.rem(r * s.cols + c, s.share) == 0) if s.share > 1 else None

    def moments(b, staged, lanes, do):
        where = owner(b)
        there = FB.at[:, my_tile, :, 0:lanes]
        me = is_me(where)
        away = jnp.logical_not(me)
        if sends_rows is not None:
            me, away = me & sends_rows, away & sends_rows

        @pl.when(me)
        def _():
            copy = pltpu.make_async_copy(staged, there, first_recv.at[my_tile])
            if do == "start":
                copy.start()

        @pl.when(away)
        def _():
            copy = remote(staged, there, first_send.at[b], first_recv.at[my_tile], where)
            copy.start() if do == "start" else copy.wait_send()

    def over_blocks(do):
        def conv_block(k, carry):
            moments(k, FT.at[k], C, do)
            return carry

        def head_block(t, carry):
            moments(TAPS + t, FTH.at[t], HD, do)
            return carry
        lax.fori_loop(0, TAPS, conv_block, 0)
        lax.fori_loop(0, HEADS, head_block, 0)

    over_blocks("start")

    own_rows = pl.ds(pl.multiple_of(core * half, half), half)

    def results(array, b, lanes, conv, do):
        def to_holder(i, carry):
            piece = OUT.at[array, pl.ds(pl.multiple_of(i * GROUP, GROUP), GROUP), 0:lanes]
            there = got_ref.at[array, b] if conv else goth_ref.at[array, b - TAPS]
            for copy_number in range(s.share):
                where = holder(i, copy_number)
                sent = out_send.at[array, i * s.share + copy_number]
                me = is_me(where)

                @pl.when(me)
                def _():
                    copy = pltpu.make_async_copy(piece, there, out_recv.at[array, b])
                    if do == "start":
                        copy.start()

                @pl.when(jnp.logical_not(me))
                def _():
                    copy = remote(piece, there, sent, out_recv.at[array, b], where)
                    copy.start() if do == "start" else copy.wait_send()
            return carry
        lax.fori_loop(0, tiles, to_holder, 0)

    def swap(buffer, lanes, which, do):
        rows = buffer.at[own_rows, 0:lanes]
        copy = remote(rows, rows, core_send.at[which], core_recv.at[which], sibling)
        copy.start() if do == "start" else copy.wait()

    def rotate(conv):
        lanes = C if conv else HD
        width = slice(0, lanes)
        OUT[0, :, width] = unit_ref[:, width].astype(BF16)
        results(0, block, lanes, conv, "start")
        bases(conv, block - TAPS, "wait")
        LB[...] = LV[...].astype(BF16)
        RB[width, width] = RV[width, width].astype(BF16)
        TB[own_rows, width] = nn(OUT[0, :, width], RB[width, width]).astype(BF16)
        swap(TB, lanes, 0, "start")
        swap(TB, lanes, 0, "wait")
        rot = tn(LB[:, own_rows], TB[:, width])
        OUT[1, :, width] = rot.astype(BF16)
        results(1, block, lanes, conv, "start")
        ROT[:, width] = rot

        def moments_in(i, carry):
            there = FB.at[:, i, :, width]
            remote(there, there, first_send.at[0], first_recv.at[i], sibling).wait_recv()
            return carry
        lax.fori_loop(0, tiles, moments_in, 0)
        first = FB[0].reshape(half, C)[:, width].astype(F32)
        second = FB[1].reshape(half, C)[:, width].astype(F32)
        _, _, direction = adam_parts(ROT[:, width], first, second, step_ref, lanes)
        VB[own_rows, width] = nt(direction.astype(BF16), RB[width, width]).astype(BF16)
        swap(VB, lanes, 1, "start")
        swap(VB, lanes, 1, "wait")
        OUT[2, :, width] = nn(LB[own_rows, :], VB[:, width]).astype(BF16)
        results(2, block, lanes, conv, "start")
        for array in range(3):
            results(array, block, lanes, conv, "wait")

    pl.when(is_conv)(lambda: rotate(True))
    pl.when(is_head)(lambda: rotate(False))

    for array in range(3):
        def conv_in(k, carry):
            there = got_ref.at[array, k]
            remote(there, there, out_send.at[0, 0], out_recv.at[array, k], sibling).wait_recv()
            return carry

        def head_in(t, carry):
            there = goth_ref.at[array, t]
            remote(there, there, out_send.at[0, 0], out_recv.at[array, TAPS + t], sibling).wait_recv()
            return carry
        lax.fori_loop(0, TAPS, conv_in, 0)
        lax.fori_loop(0, HEADS, head_in, 0)
    over_blocks("wait")


def adam_parts(grad, first, second, step_ref, lanes):
    first_new = beta_one * first + (1.0 - beta_one) * grad
    second_new = beta_two * second + (1.0 - beta_two) * grad * grad
    count = jnp.full((1, lanes), step_ref[0].astype(F32), F32)
    corr_one = 1.0 - jnp.exp(count * jnp.log(jnp.full((1, lanes), beta_one, F32)))
    corr_two = 1.0 - jnp.exp(count * jnp.log(jnp.full((1, lanes), beta_two, F32)))
    direction = first_new / corr_one / (jnp.sqrt(second_new / corr_two) + adam_eps)
    return first_new, second_new, direction


def soap_call(s, shapes, args):
    C, HD, HEADS = shapes["C"], shapes["HD"], shapes["HEADS"]
    half = C // 2
    tiles = half // GROUP
    blocks = TAPS + HEADS
    vm, dma = pltpu.VMEM, pltpu.SemaphoreType.DMA
    vmem = pl.BlockSpec(memory_space=pltpu.VMEM)
    smem = pl.BlockSpec(memory_space=pltpu.SMEM)
    hbm = pl.BlockSpec(memory_space=pl.ANY)
    scratch = [
        vm((TAPS, 2, GROUP, C), BF16), vm((HEADS, 2, GROUP, HD), BF16), vm((2, tiles, GROUP, C), BF16),
        vm((C, C), F32), vm((C, C), F32), vm((C, C), BF16), vm((C, C), BF16), vm((C, C), BF16), vm((C, C), BF16),
        vm((half, C), F32), vm((3, half, C), BF16),
        dma((blocks,)), dma((tiles,)), dma((2,)), dma((2,)), dma((2,)), dma((3, tiles * s.share)), dma((3, blocks)),
    ]

    def kernel(*refs):
        soap_kernel(s, shapes, refs)

    return pl.pallas_call(
        kernel,
        name="rotate",
        out_shape=(jax.ShapeDtypeStruct((3, TAPS, GROUP, C), BF16), jax.ShapeDtypeStruct((3, HEADS, GROUP, HD), BF16)),
        in_specs=[vmem] * 5 + [smem] + [hbm] * 4,
        out_specs=[vmem] * 2,
        scratch_shapes=scratch,
        compiler_params=pltpu.CompilerParams(collective_id=1, has_side_effects=True, vmem_limit_bytes=60 << 20),
    )(*args)


def finish_kernel(shapes, refs):
    (got, goth, cfirst, csecond, cmaster, hfirst, hsecond, hmaster, gains, gain, gfirst, gsecond, step_ref,
     merged_in, full_in, half_in, quarter_in,
     merged, gfull, ghalf, gquarter, cgrad, hgrad, cfirst_new, csecond_new, cmaster_new, ccopy,
     hfirst_new, hsecond_new, hmaster_new, hcopy, ggrad, gfirst_new, gsecond_new, gain_new,
     stage_a, stage_b, stage_c, stage_d, load_sem, store_sem) = refs
    HEADS = shapes["HEADS"]
    passed = [(merged_in, stage_a, merged), (full_in, stage_b, gfull), (half_in, stage_c, ghalf), (quarter_in, stage_d, gquarter)]
    loads = [pltpu.make_async_copy(a, b, load_sem.at[i]) for i, (a, b, _) in enumerate(passed)]
    stores = [pltpu.make_async_copy(b, o, store_sem.at[i]) for i, (_, b, o) in enumerate(passed)]
    for copy in loads:
        copy.start()

    def rows(arrays, count, first, second, master, outs):
        grad_out, first_out, second_out, master_out, copy_out = outs
        for k in range(count):
            grad_out[k] = arrays[0, k].astype(F32)
            rot = arrays[1, k].astype(F32)
            first_out[k] = beta_one * first[k] + (1.0 - beta_one) * rot
            second_out[k] = beta_two * second[k] + (1.0 - beta_two) * rot * rot
            old = master[k]
            new = old - learn_rate * (arrays[2, k].astype(F32) + weight_decay * old)
            master_out[k] = new
            copy_out[k] = new.astype(BF16)

    for load, store in zip(loads, stores):
        load.wait()
        store.start()
    rows(got, TAPS, cfirst, csecond, cmaster, (cgrad, cfirst_new, csecond_new, cmaster_new, ccopy))
    rows(goth, HEADS, hfirst, hsecond, hmaster, (hgrad, hfirst_new, hsecond_new, hmaster_new, hcopy))
    total = gains[0:HEADS, :]
    first_new, second_new, direction = adam_parts(total, gfirst[...], gsecond[...], step_ref, total.shape[1])
    ggrad[...] = total
    gfirst_new[...] = first_new
    gsecond_new[...] = second_new
    gain_new[...] = gain[...] - gain_rate * (direction + weight_decay * gain[...])
    for store in stores:
        store.wait()


def finish_call(shapes, args, like):
    vmem = pl.BlockSpec(memory_space=pltpu.VMEM)
    smem = pl.BlockSpec(memory_space=pltpu.SMEM)
    hbm = pl.BlockSpec(memory_space=pl.ANY)

    def kernel(*refs):
        finish_kernel(shapes, refs)

    return pl.pallas_call(
        kernel,
        name="finish",
        out_shape=like,
        in_specs=[vmem] * 12 + [smem] + [hbm] * 4,
        out_specs=[hbm] * 4 + [vmem] * 14,
        scratch_shapes=[*(pltpu.VMEM(x.shape, x.dtype) for x in like[:4]), pltpu.SemaphoreType.DMA((4,)), pltpu.SemaphoreType.DMA((4,))],
        compiler_params=pltpu.CompilerParams(vmem_limit_bytes=60 << 20),
    )(*args)


def shapes_of(image_full, image_half, image_quarter, heads_copy):
    return {
        "C": image_full.shape[2], "HD": heads_copy.shape[2], "HEADS": heads_copy.shape[1],
        "sizes": [p.shape[:2] for p in (image_full, image_half, image_quarter)],
    }


def per_device(
    s, image_full, image_half, image_quarter, row_pads, tile_mask, aff_scale, aff_shift, conv_copy, heads_copy, gain,
    grad_out, step_count, conv_master, conv_first, conv_second, conv_left, conv_right, heads_master, heads_first,
    heads_second, heads_left, heads_right, gain_first, gain_second,
):
    shapes = shapes_of(image_full, image_half, image_quarter, heads_copy)
    C, HEADS, HD = shapes["C"], shapes["HEADS"], shapes["HD"]

    def grouped(x):
        x = x if s.share == 1 else lax.all_gather(x, "cols", axis=0, tiled=True)
        return turned(x)

    def turned(x):
        return x.transpose(1, 0, 2)

    merged, gfull, ghalf, gquarter, unit, gains = train_call(s, shapes, (
        grouped(conv_copy), grouped(heads_copy),
        image_full, image_half, image_quarter, row_pads, tile_mask, aff_scale.reshape(1, C), aff_shift.reshape(1, C),
        gain, grad_out.reshape(-1, HEADS * HD)))
    got, goth = soap_call(s, shapes, (
        unit, grouped(conv_first), grouped(conv_second), grouped(heads_first), grouped(heads_second), step_count,
        conv_left, conv_right, heads_left, heads_right))
    if s.share > 1:
        rows = conv_first.shape[0]
        start = lax.rem(lax.axis_index("cols"), s.share) * rows
        got, goth = (lax.dynamic_slice_in_dim(x, start, rows, 2) for x in (got, goth))
    states = [turned(x) for x in (conv_first, conv_second, conv_master, heads_first, heads_second, heads_master)]
    conv = jax.ShapeDtypeStruct(states[0].shape, F32)
    head = jax.ShapeDtypeStruct(states[3].shape, F32)
    conv_low = jax.ShapeDtypeStruct(conv.shape, BF16)
    head_low = jax.ShapeDtypeStruct(head.shape, BF16)
    small = jax.ShapeDtypeStruct(gain.shape, F32)
    like = tuple(jax.ShapeDtypeStruct(x.shape, x.dtype) for x in (merged, gfull, ghalf, gquarter)) + (
        conv, head, conv, conv, conv, conv_low, head, head, head, head_low, small, small, small, small)
    outs = finish_call(shapes, (
        got, goth, *states, gains, gain, gain_first, gain_second, step_count, merged, gfull, ghalf, gquarter), like)
    return (outs[0].reshape(grad_out.shape), *outs[1:4], *[turned(x) for x in outs[4:14]], *outs[14:])


def solution(mesh):
    s = Slice(mesh, 512 // mesh.devices.size)
    pixels, rows, all_ = P("rows", "cols", None), P(("rows", "cols"), None, None), P()
    return jax.shard_map(
        functools.partial(per_device, s),
        mesh=mesh,
        in_specs=(
            pixels, pixels, pixels, all_, P("rows", "cols"), all_, all_, rows, rows, all_, pixels, all_,
            rows, rows, rows, all_, all_, rows, rows, rows, all_, all_, all_, all_,
        ),
        out_specs=(pixels,) * 4 + (rows,) * 10 + (all_,) * 4,
        check_vma=False,
    )
```

```python
import functools

import jax
import jax.numpy as jnp
from jax import lax
from jax.experimental import pallas as pl
from jax.experimental.pallas import tpu as pltpu
from jax.sharding import PartitionSpec as P

beta_one = 0.95
beta_two = 0.95
adam_eps = 1e-08
norm_eps = 1e-06
learn_rate = 0.02
gain_rate = 1.0
weight_decay = 0.01

MESH = pl.DeviceIdType.MESH
BF16 = jnp.bfloat16
F32 = jnp.float32
GROUP = 16
CHUNK_TAPS = (3, 3, 3)
CHUNK_HEADS = (4, 3)
VMEM_LIMIT = 63 << 20
TAPS = 9


def nn(a, b):
    return jnp.dot(a, b, preferred_element_type=F32)


def nt(a, b):
    return lax.dot_general(a, b, (((1,), (1,)), ((), ())), preferred_element_type=F32)


def tn(a, b):
    return lax.dot_general(a, b, (((0,), (0,)), ((), ())), preferred_element_type=F32)


class Dim:
    def __init__(self, size, row_step, col_step):
        self.size, self.row_step, self.col_step = size, row_step, col_step

    def coord(self, r, c):
        if self.row_step:
            return lax.rem(lax.div(r, self.row_step), self.size)
        return lax.rem(lax.div(c, self.col_step), self.size)


class Slice:
    def __init__(self, mesh, rows_per_device):
        self.rows, self.cols = mesh.devices.shape
        self.share = max(1, GROUP // rows_per_device)
        place = {}
        try:
            for r in range(self.rows):
                for c in range(self.cols):
                    device = mesh.devices[r, c]
                    place[(*device.coords, device.core_on_chip)] = (r, c)
        except AttributeError:
            place = {}
            for r in range(self.rows):
                for c in range(self.cols):
                    if self.rows == 8:
                        key = (c // 2, r % 2, r // 2, c % 2)
                    else:
                        key = (c, r // 8, r // 2 % 4, r % 2)
                    place[key] = (r, c)
        origin = tuple(min(k[a] for k in place) for a in range(4))
        dims = []
        for axis in range(4):
            size = max(k[axis] for k in place) - origin[axis] + 1
            step = list(origin)
            step[axis] += 1
            there = place[tuple(step)]
            dims.append(Dim(size, *there))
        self.core = dims[3]
        chips = dims[:3]
        inside = [d for d in chips if d.row_step == 0 and d.col_step < self.share]
        lines = [d for d in chips if d not in inside]
        lines.sort(key=lambda d: -d.size)
        self.lines = lines
        self.chips = lines + inside
        self.groups = self.rows * self.cols // self.share


class Here:
    def __init__(self, s):
        self.s = s
        self.r = lax.axis_index("rows")
        self.c = lax.axis_index("cols")
        self.place = {d: d.coord(self.r, self.c) for d in [*s.chips, s.core]}

    def at(self, dim):
        return self.place[dim]

    def moved(self, steps):
        r, c = self.r, self.c
        for dim, there in steps:
            delta = there - self.at(dim)
            r = r + delta * dim.row_step
            c = c + delta * dim.col_step
        return r, c

    def ahead(self, dim, step):
        return lax.rem(self.at(dim) + step, dim.size)

    def behind(self, dim, step):
        return lax.rem(self.at(dim) + dim.size - step, dim.size)

    def group(self, place):
        r, c = place
        return lax.div(r * self.s.cols + c, self.s.share)


def remote(src, dst, send, recv, where):
    return pltpu.make_async_remote_copy(
        src_ref=src, dst_ref=dst, send_sem=send, recv_sem=recv, device_id=where, device_id_type=MESH
    )


def gather_plan(s):
    lines = s.lines
    first = lines[0]
    plans = []
    own = []
    for s0 in range(first.size):
        rest = list(lines[1:])
        if s0 >= 1:
            rest.reverse()
        onward = [(d, st) for d in rest for st in range(1, d.size)]
        if s0 == 0:
            own = [(first, st) for st in range(1, first.size)] + onward
        else:
            plans.append((0, ((first, s0),), onward))
        if rest:
            for s1 in range(1, rest[0].size):
                on = [(d, st) for d in rest[1:] for st in range(1, d.size)]
                plans.append((1, ((first, s0), (rest[0], s1)), on))
            for d in rest[1:]:
                for s2 in range(1, d.size):
                    for s1 in range(rest[0].size):
                        plans.append((2, ((first, s0), (rest[0], s1), (d, s2)), []))
    plans.sort(key=lambda p: p[0])
    return own, plans


def log2(n):
    return n.bit_length() - 1


def home_of(s, b):
    d0, d1, d2 = s.chips
    t = b - TAPS
    tap = b < TAPS
    column = jnp.where(tap, lax.rem(b, 4), jnp.where(t < 3, t + 1, t - 3))
    along = jnp.where(tap, jnp.where(b < 4, 0, jnp.where(b < 8, 1, 3)), jnp.where(t < 3, 3, 2))
    return {d0: along, d1: lax.div(column, 2), d2: lax.rem(column, 2)}


def block_at(along, column):
    last = jnp.where(column == 0, TAPS - 1, TAPS + column - 1)
    return jnp.where(along < 2, along * 4 + column, jnp.where(along == 2, TAPS + 3 + column, last))


def adam_parts(grad, first, second, step_ref, lanes):
    first_new = beta_one * first + (1.0 - beta_one) * grad
    second_new = beta_two * second + (1.0 - beta_two) * grad * grad
    count = jnp.full((1, lanes), step_ref[0].astype(F32), F32)
    corr_one = 1.0 - jnp.exp(count * jnp.log(jnp.full((1, lanes), beta_one, F32)))
    corr_two = 1.0 - jnp.exp(count * jnp.log(jnp.full((1, lanes), beta_two, F32)))
    direction = first_new / corr_one / (jnp.sqrt(second_new / corr_two) + adam_eps)
    return first_new, second_new, direction


def train_kernel(s, shapes, refs):
    (conv_w, head_w, full_ref, half_ref, quarter_ref, pads, step_ref, tile_ref, scale_ref, shift_ref, gain_ref,
     go_hbm, cfirst_hbm, csecond_hbm, hfirst_hbm, hsecond_hbm, cleft, cright, hleft, hright,
     merged_hbm, gfull_hbm, ghalf_hbm, gquarter_hbm, gainsum_ref, got_ref, goth_ref,
     W, Z, MK, HR, HC, TS, CS, HR2, HC2, TS2, CS2, MKF, U, UT, PRE, GA, ACT, GP, GG, GX,
     A, AH, SC, SCH, RC, RCH, SB, SBH, R1A, R1B, R2A, R2B, R3A, R3B,
     GO, MERGED, CF, CS_, HF, HS, FT, FTH, FB, LV, RV, LB, RB, TB, VB, OUT,
     ag_send, ag_recv, halo_send, halo_recv, core_send, core_recv, rs_send, rs1_recv, rs2_recv, rs3_recv,
     gx_send, gx_recv, load_sem, store_sem, first_send, first_recv, base_sem, swap_send, swap_recv,
     out_send, out_recv) = refs
    here = Here(s)
    C, HD, HEADS = shapes["C"], shapes["HD"], shapes["HEADS"]
    sizes = shapes["sizes"]
    counts = [a * b for a, b in sizes]
    offs = [0, counts[0], counts[0] + counts[1]]
    n_pix = sum(counts)
    n_rest = n_pix - counts[0]
    half = C // 2
    blocks = TAPS + HEADS
    tiles = half // GROUP
    r, c = here.r, here.c
    core = here.at(s.core)
    sibling = here.moved([(s.core, 1 - core)])
    d0, d1, d2 = s.chips
    own_group = here.group((r, c))
    my_half = lax.div(own_group, tiles)
    my_tile = lax.rem(own_group, tiles)
    at_home = (here.at(d1) < 2) & (here.at(d2) < 2)
    block = block_at(here.at(d0), here.at(d1) * 2 + here.at(d2))
    is_conv = at_home & (block < TAPS)
    is_head = at_home & (block >= TAPS)

    loads = [(go_hbm, GO), (cfirst_hbm, CF), (csecond_hbm, CS_), (hfirst_hbm, HF), (hsecond_hbm, HS)]
    loads = [pltpu.make_async_copy(a, b, load_sem.at[i]) for i, (a, b) in enumerate(loads)]

    def bases(conv, do):
        if conv:
            pairs = [(cleft, LV), (cright, RV)]
        else:
            t = jnp.maximum(block - TAPS, 0)
            pairs = [(hleft.at[t], LV), (hright.at[t], RV.at[0:HD, 0:HD])]
        for i, (a, b) in enumerate(pairs):
            copy = pltpu.make_async_copy(a, b, base_sem.at[i])
            copy.start() if do == "start" else copy.wait()

    for ref in (HR, HC, HR2, HC2, CS, CS2):
        ref[...] = jnp.zeros_like(ref)

    def owner(b):
        return here.moved([*home_of(s, b).items(), (s.core, my_half)])

    def holder(i, copy):
        device = (core * tiles + i) * s.share + copy
        return lax.div(device, s.cols), lax.rem(device, s.cols)

    def is_me(where):
        return (where[0] == r) & (where[1] == c)

    barrier = pltpu.get_barrier_semaphore()

    def greet(where):
        pl.semaphore_signal(barrier, inc=1, device_id=where, device_id_type=MESH)

    greeted = [sibling]
    for d in s.chips:
        greeted += [here.moved([(d, here.ahead(d, st))]) for st in range(1, d.size)]
    greeted += [
        (lax.rem(r + 1, s.rows), c), (lax.rem(r + s.rows - 1, s.rows), c),
        (r, lax.rem(c + 1, s.cols)), (r, lax.rem(c + s.cols - 1, s.cols)),
    ]
    for g in greeted:
        greet(g)

    def greet_owner(b, carry):
        where = owner(b)
        pl.when(jnp.logical_not(is_me(where)))(lambda: greet(where))
        return carry

    lax.fori_loop(0, blocks, greet_owner, 0)

    @pl.when(at_home)
    def _():
        def greet_holder(i, carry):
            for copy in range(s.share):
                where = holder(i, copy)
                pl.when(jnp.logical_not(is_me(where)))(lambda: greet(where))
            return carry
        lax.fori_loop(0, tiles, greet_holder, 0)

    same = (at_home & (my_half == core)).astype(jnp.int32)
    n_greets = len(greeted) + blocks - same + jnp.where(at_home, s.share * tiles - same, 0)

    for load in loads:
        load.start()
    pl.when(is_conv)(lambda: bases(True, "start"))
    pl.when(is_head)(lambda: bases(False, "start"))

    for k in range(TAPS):
        W[own_group, :, k * C : (k + 1) * C] = conv_w[k]
    for t in range(HEADS):
        W[own_group, :, TAPS * C + t * HD : TAPS * C + (t + 1) * HD] = head_w[t]

    def valid_of(scale, row):
        rows_here = sizes[scale][0]
        limit = rows_here * s.rows - pads[scale]
        return jnp.where(r * rows_here + row < limit, 1.0, 0.0).astype(F32)

    pictures = (full_ref, half_ref, quarter_ref)
    segments = [(sc, row, offs[sc] + row * sizes[sc][1], sizes[sc][1]) for sc in range(3) for row in range(sizes[sc][0])]
    for sc, row, start, count in segments:
        MK[start : start + count, :] = (pictures[sc][row].astype(F32) * valid_of(sc, row)).astype(BF16)

    strip_at = [0, sizes[0][1], sizes[0][1] + sizes[1][1]]
    padded_rows = [(sc, j) for sc in range(3) for j in range(sizes[sc][0] + 2)]

    def pixel_row(pixels, sc, row):
        start = offs[sc] + row * sizes[sc][1]
        return pixels[start : start + sizes[sc][1], :]

    def stage_strips(pixels, strips):
        for sc in range(3):
            lanes = slice(strip_at[sc], strip_at[sc] + sizes[sc][1])
            strips[0, lanes, :] = pixel_row(pixels, sc, 0)
            strips[1, lanes, :] = pixel_row(pixels, sc, sizes[sc][0] - 1)

    sides = [
        (r > 0, (r - 1, c)), (r < s.rows - 1, (r + 1, c)),
        (c > 0, (r, c - 1)), (c < s.cols - 1, (r, c + 1)),
    ]

    def send_sides(which, pair, staged, landing):
        for side in pair:
            there, where = sides[side]
            end = side % 2
            copy = remote(staged.at[end], landing.at[1 - end], halo_send.at[which, side], halo_recv.at[which, side ^ 1], where)
            pl.when(there)(copy.start)

    def wait_sides(which, pair, staged, landing, do):
        for side in pair:
            there, where = sides[side]
            end = side % 2
            copy = remote(staged.at[end], landing.at[end], halo_send.at[which, side], halo_recv.at[which, side], where)
            pl.when(there)(copy.wait_recv if do == "recv" else copy.wait_send)

    def padded(pixels, rims, sc, j):
        lanes = slice(strip_at[sc], strip_at[sc] + sizes[sc][1])
        if j == 0:
            return rims[0, lanes, :]
        if j == sizes[sc][0] + 1:
            return rims[1, lanes, :]
        return pixel_row(pixels, sc, j - 1)

    def stage_columns(pixels, rims, columns):
        for index, (sc, j) in enumerate(padded_rows):
            x = padded(pixels, rims, sc, j).astype(F32)
            columns[0, index : index + 1, :] = x[0:1]
            columns[1, index : index + 1, :] = x[sizes[sc][1] - 1 :]

    def put_windows(sc, j, b, value):
        for a in range(3):
            row = j - a
            if 0 <= row < sizes[sc][0]:
                start = offs[sc] + row * sizes[sc][1]
                Z[3 * a + b, start : start + sizes[sc][1], :] = value

    def windows_middle(pixels, rims):
        for sc, j in padded_rows:
            put_windows(sc, j, 1, padded(pixels, rims, sc, j))

    def windows_sides(pixels, rims, ends):
        for index, (sc, j) in enumerate(padded_rows):
            count = sizes[sc][1]
            x = padded(pixels, rims, sc, j).astype(F32)
            place = lax.broadcasted_iota(jnp.int32, (count, C), 0)
            before = jnp.where(place == 0, ends[0, index : index + 1, :], pltpu.roll(x, 1, 0))
            after = jnp.where(place == count - 1, ends[1, index : index + 1, :], pltpu.roll(x, count - 1, 0))
            put_windows(sc, j, 0, before.astype(BF16))
            put_windows(sc, j, 2, after.astype(BF16))

    stage_strips(MK, TS)
    pl.semaphore_wait(barrier, n_greets)

    own_sends, plan = gather_plan(s)
    chunk_lanes = []
    for count, unit in [*((n, C) for n in CHUNK_TAPS), *((n, HD) for n in CHUNK_HEADS)]:
        start = chunk_lanes[-1].stop if chunk_lanes else 0
        chunk_lanes.append(slice(start, start + count * unit))
    chunks = len(chunk_lanes)
    n_arrive = len(plan)

    def block_of(offsets):
        return here.moved([(d, here.behind(d, st)) for d, st in offsets if st])

    def steps_of(offsets):
        return tuple(sum(st for dd, st in offsets if dd is d) for d in s.lines)

    arrival = {steps_of(offsets): index for index, (_, offsets, _) in enumerate(plan)}
    sends = [(-1, d, st, arrival[steps_of([(d, st)])]) for d, st in own_sends]
    for index, (_, offsets, onward) in enumerate(plan):
        sends += [(index, d, st, arrival[steps_of([*offsets, (d, st)])]) for d, st in onward]
    n_sends = len(sends)

    def place_of(index):
        return (r, c) if index < 0 else block_of(plan[index][1])

    def pass_on(ch, index):
        rows = W.at[here.group(place_of(index)), :, chunk_lanes[ch]]
        for number, (source, d, st, lands) in enumerate(sends):
            if source == index:
                remote(rows, rows, ag_send.at[ch], ag_recv.at[ch, lands],
                       here.moved([(d, here.ahead(d, st))])).start()
        remote(rows, rows, ag_send.at[ch], ag_recv.at[ch, n_arrive], sibling).start()

    def arrive(ch, index):
        rows = W.at[here.group(place_of(index)), :, chunk_lanes[ch]]
        remote(rows, rows, ag_send.at[ch], ag_recv.at[ch, index], sibling).wait_recv()

    def arrive_sibling(ch):
        rows = W.at[0 : n_arrive + 1, :, chunk_lanes[ch]]
        remote(rows, rows, ag_send.at[ch], ag_recv.at[ch, n_arrive], sibling).wait_recv()

    pass_on(0, -1)
    send_sides(0, (0, 1), TS, HR)
    pass_on(1, -1)

    def conv_tap(k, carry):
        kernel = W[:, :, pl.ds(pl.multiple_of(k * C, C), C)].reshape(C, C)
        PRE[...] += nn(Z[k], kernel)
        return carry

    PRE[...] = jnp.zeros_like(PRE)
    GA[...] = jnp.zeros_like(GA)
    GG[...] = jnp.zeros_like(GG)

    def constants():
        tile_cols = sizes[0][1] // tile_ref.shape[1]
        cell = (sizes[0][1], tile_ref.shape[1])
        column = lax.broadcasted_iota(jnp.int32, cell, 0)
        tile = lax.broadcasted_iota(jnp.int32, cell, 1)
        picked = jnp.where((column >> log2(tile_cols)) == tile, tile_ref[...].astype(F32), 0.0)
        mask_row = jnp.broadcast_to(jnp.sum(picked, axis=1, keepdims=True), (sizes[0][1], HD))
        for row in range(sizes[0][0]):
            MKF[row * sizes[0][1] : (row + 1) * sizes[0][1], :] = mask_row

        def coarse(full_pixel):
            row = full_pixel >> log2(sizes[0][1])
            col = full_pixel & (sizes[0][1] - 1)
            one = (row >> 1) * sizes[1][1] + (col >> 1)
            two = counts[1] + (row >> 2) * sizes[2][1] + (col >> 2)
            return one, two

        one, two = coarse(lax.broadcasted_iota(jnp.int32, (counts[0], n_rest), 0))
        rest = lax.broadcasted_iota(jnp.int32, (counts[0], n_rest), 1)
        U[...] = jnp.where((one == rest) | (two == rest), 1.0, 0.0).astype(BF16)
        one, two = coarse(lax.broadcasted_iota(jnp.int32, (n_rest, counts[0]), 1))
        rest = lax.broadcasted_iota(jnp.int32, (n_rest, counts[0]), 0)
        UT[...] = jnp.where((one == rest) | (two == rest), 1.0, 0.0).astype(BF16)

    def stage_moments():
        for load in loads[1:]:
            load.wait()
        for k in range(TAPS):
            FT[k, 0] = CF[k].astype(BF16)
            FT[k, 1] = CS_[k].astype(BF16)
        for t in range(HEADS):
            FTH[t, 0] = HF[t].astype(BF16)
            FTH[t, 1] = HS[t].astype(BF16)

    sends_rows = (lax.rem(r * s.cols + c, s.share) == 0) if s.share > 1 else None

    def moments(b, staged, lanes, do):
        where = owner(b)
        there = FB.at[:, my_tile, :, 0:lanes]
        me = is_me(where)
        away = jnp.logical_not(me)
        if sends_rows is not None:
            me, away = me & sends_rows, away & sends_rows
        if do == "start":
            @pl.when(me)
            def _():
                pltpu.make_async_copy(staged, there, first_recv.at[my_tile]).start()

        @pl.when(away)
        def _():
            copy = remote(staged, there, first_send.at[b], first_recv.at[my_tile], where)
            copy.start() if do == "start" else copy.wait_send()

    def over_blocks(step):
        def conv_block(k, carry):
            step(k, k, True)
            return carry

        def head_block(t, carry):
            step(TAPS + t, t, False)
            return carry
        lax.fori_loop(0, TAPS, conv_block, 0)
        lax.fori_loop(0, HEADS, head_block, 0)

    def all_moments(do):
        over_blocks(lambda b, i, conv: moments(b, FT.at[i] if conv else FTH.at[i], C if conv else HD, do))

    def base_casts():
        def cast(conv):
            bases(conv, "wait")
            n = C if conv else HD
            LB[...] = LV[...].astype(BF16)
            RB[0:n, 0:n] = RV[0:n, 0:n].astype(BF16)
        pl.when(is_conv)(lambda: cast(True))
        pl.when(is_head)(lambda: cast(False))

    def activation():
        for sc, row, start, count in segments:
            biased = PRE[start : start + count, :] * scale_ref[...] + shift_ref[...]
            ACT[start : start + count, :] = (jnp.maximum(biased, 0.0) * valid_of(sc, row)).astype(BF16)
        loads[0].wait()

    own_half = pl.ds(pl.multiple_of(core * half, half), half)
    other_half = pl.ds(pl.multiple_of((1 - core) * half, half), half)

    def core_copy(b, staged, landing):
        return remote(staged, landing, core_send.at[b], core_recv.at[b], sibling)

    def merged_store(t):
        lanes = pl.ds(pl.multiple_of(t * HD, HD), HD)
        return pltpu.make_async_copy(MERGED.at[:, lanes], merged_hbm.at[:, lanes], store_sem.at[t])

    def head(t, carry):
        weights = W[:, :, pl.ds(pl.multiple_of(TAPS * C + t * HD, HD), HD)].reshape(C, HD)
        hidden = nn(ACT[...], weights)
        inverse = lax.rsqrt(jnp.mean(hidden * hidden, axis=-1, keepdims=True) + norm_eps)
        unit = hidden * inverse
        gain = gain_ref[pl.ds(t, 1), :]
        normed = gain * unit
        small = normed[counts[0] :]
        small_high = small.astype(BF16)
        small_low = (small - small_high.astype(F32)).astype(BF16)
        lifted = nn(U[...], small_high) + nn(U[...], small_low)
        lanes = pl.ds(pl.multiple_of(t * HD, HD), HD)
        MERGED[:, lanes] = (MKF[...] * (normed[: counts[0]] + lifted)).astype(BF16)
        merged_store(t).start()
        back = GO[:, lanes].astype(F32) * MKF[...]
        pooled = jnp.concatenate([back, nn(UT[...], back.astype(BF16))], axis=0)
        product = pooled * unit
        GG[pl.ds(t, 1), :] = jnp.sum(product, axis=0, keepdims=True)
        middle = jnp.mean(gain * product, axis=-1, keepdims=True)
        grad_hidden = (inverse * (gain * pooled - unit * middle)).astype(BF16)
        SCH[t] = tn(ACT[:, other_half], grad_hidden).astype(BF16)
        core_copy(TAPS + t, SCH.at[t], RCH.at[t]).start()
        AH[t] = tn(ACT[:, own_half], grad_hidden)
        GA[...] += nt(grad_hidden, weights)
        return carry

    conv_set = (A, SC, RC, SB, C)
    head_set = (AH, SCH, RCH, SBH, HD)
    cut = shapes["cut"]
    part_rows = (slice(0, cut), slice(cut, half))
    part_ways = ((d1, d2), (d2, d1))
    firsts, seconds, thirds = (R1A, R1B), (R2A, R2B), (R3A, R3B)

    def landing(stage, place, part, slot, lanes):
        if stage == 1:
            which = place[d0] * 2 + place[part_ways[part][1]]
            return firsts[part].at[which, slot, :, 0:lanes], rs1_recv.at[part, which, slot]
        if stage == 2:
            return seconds[part].at[place[d0], slot, :, 0:lanes], rs2_recv.at[part, place[d0], slot]
        return thirds[part].at[slot, :, 0:lanes], rs3_recv.at[part, slot]

    def ship(stage, b, i, group, part, dim):
        total, _, _, staged, lanes = group
        place = home_of(s, b)
        rows = part_rows[part]
        staged[i, rows, :] = total[i, rows, :].astype(BF16)
        for st in range(1, dim.size):
            @pl.when(lax.rem(place[dim] + st, dim.size) == here.at(dim))
            def _():
                buffer, sem = landing(stage, place, part, st - 1, lanes)
                remote(staged.at[i, rows, :], buffer, rs_send.at[b, part], sem, here.moved([(dim, place[dim])])).start()

    def take(stage, b, i, group, part, dim):
        total, _, _, staged, lanes = group
        place = home_of(s, b)
        rows = part_rows[part]
        for st in range(1, dim.size):
            buffer, sem = landing(stage, place, part, st - 1, lanes)
            remote(staged.at[i, rows, :], buffer, rs_send.at[b, part], sem, sibling).wait_recv()
            total[i, rows, :] += buffer[...].astype(F32)

    def first_ship(b, i, group):
        total, staged, landed, _, _ = group
        core_copy(b, staged.at[i], landed.at[i]).wait_recv()
        total[i] += landed[i].astype(F32)
        place = home_of(s, b)
        for part in (0, 1):
            dim = part_ways[part][0]

            @pl.when(here.at(dim) != place[dim])
            def _():
                ship(1, b, i, group, part, dim)

    def second_ship(b, i, group):
        place = home_of(s, b)
        for part in (0, 1):
            dim, then = part_ways[part]

            @pl.when(here.at(dim) == place[dim])
            def _():
                take(1, b, i, group, part, dim)

                @pl.when(here.at(then) != place[then])
                def _():
                    ship(2, b, i, group, part, then)

    def third_ship(b, i, group):
        place = home_of(s, b)
        for part in (0, 1):
            @pl.when((here.at(d1) == place[d1]) & (here.at(d2) == place[d2]))
            def _():
                take(2, b, i, group, part, part_ways[part][1])

                @pl.when(here.at(d0) != place[d0])
                def _():
                    ship(3, b, i, group, part, d0)

    def head_first(t):
        first_ship(TAPS + t, t, head_set)

    tiers = [[i for i, p in enumerate(plan) if p[0] == tier] for tier in range(3)]
    constants()
    heads_done = 0
    for turn in range(chunks + 2):
        for tier in range(3):
            ch = turn - tier
            if 0 <= ch < chunks:
                for index in tiers[tier]:
                    arrive(ch, index)
                    pass_on(ch, index)
        if turn + 2 < chunks:
            pass_on(turn + 2, -1)
        if turn == 0:
            wait_sides(0, (0, 1), TS, HR, "recv")
            stage_columns(MK, HR, CS)
            send_sides(0, (2, 3), CS, HC)
            windows_middle(MK, HR)
        if turn == 1:
            stage_moments()
            wait_sides(0, (2, 3), CS, HC, "recv")
            windows_sides(MK, HR, HC)
        if turn == chunks:
            all_moments("start")
        ch = turn - 2
        if ch < 0:
            continue
        arrive_sibling(ch)
        if ch < len(CHUNK_TAPS):
            low = sum(CHUNK_TAPS[:ch])
            lax.fori_loop(low, low + CHUNK_TAPS[ch], conv_tap, 0)
            if ch == len(CHUNK_TAPS) - 1:
                activation()
        else:
            if ch == len(CHUNK_TAPS):
                base_casts()
            count = CHUNK_HEADS[ch - len(CHUNK_TAPS)]
            lax.fori_loop(heads_done, heads_done + count, head, 0)
            heads_done += count
    wait_sides(0, (0, 1), TS, HR, "send")
    wait_sides(0, (2, 3), CS, HC, "send")

    sum_dims = [s.core] + list(reversed(s.chips))

    def gain_send(stage):
        d = sum_dims[stage]
        mine = here.at(d)
        GX[stage, mine] = GG[...]
        for st in range(1, d.size):
            remote(GX.at[stage, mine], GX.at[stage, mine], gx_send.at[stage, st], gx_recv.at[stage, st],
                   here.moved([(d, here.ahead(d, st))])).start()

    def gain_add(stage):
        d = sum_dims[stage]
        for st in range(1, d.size):
            slot = here.behind(d, st)
            remote(GX.at[stage, slot], GX.at[stage, slot], gx_send.at[stage, st], gx_recv.at[stage, st], sibling).wait_recv()
        total = GX[stage, 0]
        for i in range(1, d.size):
            total = total + GX[stage, i]
        GG[...] = total

    gain_send(0)

    def heads_in(low, high, step):
        def body(t, carry):
            step(TAPS + t, t, head_set)
            return carry
        lax.fori_loop(low, high, body, 0)

    early_heads = (0, 3)
    late_heads = (3, HEADS)
    heads_in(*early_heads, first_ship)

    for sc, row, start, count in segments:
        pre = PRE[start : start + count, :]
        biased = pre * scale_ref[...] + shift_ref[...]
        grad = jnp.where(biased > 0.0, GA[start : start + count, :], 0.0)
        GP[start : start + count, :] = (scale_ref[...] * grad * valid_of(sc, row)).astype(BF16)
    stage_strips(GP, TS2)
    gain_add(0)
    gain_send(1)

    lag_two, lag_three = 4, 7
    turns = TAPS + lag_three

    def tap_at(turn):
        return jnp.where(turn == 0, TAPS - 1, turn - 1)

    def conv_stage(step, turn):
        @pl.when((turn >= 0) & (turn < TAPS))
        def _():
            k = tap_at(turn)
            step(k, k, conv_set)

    def produce(k, i, group):
        SC[k] = tn(Z[k, :, other_half], GP[...]).astype(BF16)
        core_copy(k, SC.at[k], RC.at[k]).start()
        A[k] = tn(Z[k, :, own_half], GP[...])

    def image_tap(k, carry):
        kernel = W[:, :, pl.ds(pl.multiple_of(k * C, C), C)].reshape(C, C)
        PRE[...] += nt(Z[TAPS - 1 - k], kernel)
        return carry

    def gradient_turn(turn, carry):
        conv_stage(produce, turn)
        conv_stage(first_ship, turn - 1)

        @pl.when(turn == 1)
        def _():
            send_sides(1, (0, 1), TS2, HR2)
            heads_in(*early_heads, second_ship)

        @pl.when(turn == 4)
        def _():
            heads_in(*early_heads, third_ship)
            gain_add(1)
            gain_send(2)

        pl.when(turn == TAPS + 1)(lambda: heads_in(*late_heads, first_ship))
        conv_stage(second_ship, turn - lag_two)
        conv_stage(third_ship, turn - lag_three)

        @pl.when(turn == TAPS - 2)
        def _():
            wait_sides(1, (0, 1), TS2, HR2, "recv")
            stage_columns(GP, HR2, CS2)
            send_sides(1, (2, 3), CS2, HC2)

        @pl.when(turn == TAPS)
        def _():
            windows_middle(GP, HR2)
            wait_sides(1, (2, 3), CS2, HC2, "recv")
            windows_sides(GP, HR2, HC2)
            PRE[...] = jnp.zeros_like(PRE)

        @pl.when(turn > TAPS)
        def _():
            low = (turn - TAPS - 1) * 2
            lax.fori_loop(low, jnp.minimum(low + 2, TAPS), image_tap, 0)
        return carry

    lax.fori_loop(0, turns, gradient_turn, 0)
    heads_in(*late_heads, second_ship)
    gain_add(2)
    gain_send(3)
    outs = (gfull_hbm, ghalf_hbm, gquarter_hbm)
    picture_stores = []
    for index, (sc, row, start, count) in enumerate(segments):
        PRE[start : start + count, :] = PRE[start : start + count, :] * valid_of(sc, row)
        picture_stores.append(pltpu.make_async_copy(
            PRE.at[start : start + count, :], outs[sc].at[row], store_sem.at[HEADS + index]))
        picture_stores[-1].start()
    heads_in(*late_heads, third_ship)
    own_rows = own_half

    def results(array, lanes, conv, do):
        def to_holder(i, carry):
            piece = OUT.at[array, pl.ds(pl.multiple_of(i * GROUP, GROUP), GROUP), 0:lanes]
            there = got_ref.at[array, block] if conv else goth_ref.at[array, block - TAPS]
            for number in range(s.share):
                where = holder(i, number)
                me = is_me(where)
                if do == "start":
                    @pl.when(me)
                    def _():
                        pltpu.make_async_copy(piece, there, out_recv.at[array, block]).start()

                @pl.when(jnp.logical_not(me))
                def _():
                    copy = remote(piece, there, out_send.at[array, i * s.share + number], out_recv.at[array, block], where)
                    copy.start() if do == "start" else copy.wait_send()
            return carry
        lax.fori_loop(0, tiles, to_holder, 0)

    def swap(buffer, lanes, which):
        rows = buffer.at[own_rows, 0:lanes]
        return remote(rows, rows, swap_send.at[which], swap_recv.at[which], sibling)

    def rotate(conv):
        group = conv_set if conv else head_set
        i = block if conv else block - TAPS
        lanes = group[4]
        n = slice(0, lanes)
        for part in (0, 1):
            take(3, block, i, group, part, d0)
        OUT[0, :, n] = group[0][i].astype(BF16)
        TB[own_rows, n] = nn(OUT[0, :, n], RB[n, n]).astype(BF16)
        swap(TB, lanes, 0).start()
        results(0, lanes, conv, "start")
        swap(TB, lanes, 0).wait()
        rot = tn(LB[:, own_rows], TB[:, n])
        OUT[1, :, n] = rot.astype(BF16)

        def moments_in(j, carry):
            there = FB.at[:, j, :, n]
            remote(there, there, first_send.at[0], first_recv.at[j], sibling).wait_recv()
            return carry
        lax.fori_loop(0, tiles, moments_in, 0)
        first = FB[0].reshape(half, C)[:, n].astype(F32)
        second = FB[1].reshape(half, C)[:, n].astype(F32)
        _, _, direction = adam_parts(rot, first, second, step_ref, lanes)
        VB[own_rows, n] = nt(direction.astype(BF16), RB[n, n]).astype(BF16)
        swap(VB, lanes, 1).start()
        results(1, lanes, conv, "start")
        swap(VB, lanes, 1).wait()
        OUT[2, :, n] = nn(LB[own_rows, :], VB[:, n]).astype(BF16)
        results(2, lanes, conv, "start")
        for array in range(3):
            results(array, lanes, conv, "wait")

    pl.when(is_conv)(lambda: rotate(True))
    pl.when(is_head)(lambda: rotate(False))
    gain_add(3)
    gainsum_ref[...] = GG[...]

    for array in range(3):
        def result_in(b, i, conv):
            there = got_ref.at[array, i] if conv else goth_ref.at[array, i]
            remote(there, there, out_send.at[0, 0], out_recv.at[array, b], sibling).wait_recv()
        over_blocks(result_in)

    for ch in range(chunks):
        rows = W.at[0 : n_sends + n_arrive + 1, :, chunk_lanes[ch]]
        remote(rows, rows, ag_send.at[ch], ag_recv.at[ch, 0], sibling).wait_send()
    all_moments("wait")
    wait_sides(1, (0, 1), TS2, HR2, "send")
    wait_sides(1, (2, 3), CS2, HC2, "send")
    for stage, d in enumerate(sum_dims):
        for st in range(1, d.size):
            remote(GX.at[stage, 0], GX.at[stage, 0], gx_send.at[stage, st], gx_recv.at[stage, st], sibling).wait_send()

    def sent_block(b, i, conv):
        _, staged, landed, sb, _ = conv_set if conv else head_set
        core_copy(b, staged.at[i], landed.at[i]).wait_send()
        place = home_of(s, b)
        gone = (here.at(d0) != place[d0]) | (here.at(d1) != place[d1]) | (here.at(d2) != place[d2])
        for part in (0, 1):
            @pl.when(gone)
            def _():
                piece = sb.at[i, part_rows[part], :]
                remote(piece, piece, rs_send.at[b, part], rs_send.at[b, part], sibling).wait_send()

    over_blocks(sent_block)

    def stored(t, carry):
        merged_store(t).wait()
        return carry

    lax.fori_loop(0, HEADS, stored, 0)
    for store in picture_stores:
        store.wait()


def train_call(s, shapes, args):
    C, HD, HEADS, sizes = shapes["C"], shapes["HD"], shapes["HEADS"], shapes["sizes"]
    counts = [a * b for a, b in sizes]
    n_pix = sum(counts)
    half = C // 2
    tiles = half // GROUP
    blocks = TAPS + HEADS
    strip = sum(b for _, b in sizes)
    padded = -(-sum(a + 2 for a, _ in sizes) // 8) * 8
    own_sends, plan = gather_plan(s)
    n_arrive = len(plan)
    n_sends = len(own_sends) + sum(len(p[2]) for p in plan)
    chunks = len(CHUNK_TAPS) + len(CHUNK_HEADS)
    d0, d1, d2 = s.chips
    most = max(d1.size, d2.size) - 1
    lanes_all = TAPS * C + HEADS * HD
    heads_pad = -(-HEADS // 8) * 8
    cut = half * 3 // 4
    shapes = {**shapes, "cut": cut}
    rest = half - cut
    dma = pltpu.SemaphoreType.DMA
    vm = pltpu.VMEM
    longest = max(s.core.size, *(d.size for d in s.chips))
    scratch = [
        vm((s.groups, GROUP, lanes_all), BF16),
        vm((TAPS, n_pix, C), BF16),
        vm((n_pix, C), BF16),
        vm((2, strip, C), BF16), vm((2, padded, C), F32), vm((2, strip, C), BF16), vm((2, padded, C), F32),
        vm((2, strip, C), BF16), vm((2, padded, C), F32), vm((2, strip, C), BF16), vm((2, padded, C), F32),
        vm((counts[0], HD), F32),
        vm((counts[0], n_pix - counts[0]), BF16), vm((n_pix - counts[0], counts[0]), BF16),
        vm((n_pix, C), F32), vm((n_pix, C), F32),
        vm((n_pix, C), BF16), vm((n_pix, C), BF16),
        vm((heads_pad, HD), F32), vm((4, longest, heads_pad, HD), F32),
        vm((TAPS, half, C), F32), vm((HEADS, half, HD), F32),
        vm((TAPS, half, C), BF16), vm((HEADS, half, HD), BF16),
        vm((TAPS, half, C), BF16), vm((HEADS, half, HD), BF16),
        vm((TAPS, half, C), BF16), vm((HEADS, half, HD), BF16),
        vm((8, most, cut, C), BF16), vm((8, most, rest, C), BF16),
        vm((4, most, cut, C), BF16), vm((4, most, rest, C), BF16),
        vm((d0.size - 1, cut, C), BF16), vm((d0.size - 1, rest, C), BF16),
        vm((counts[0], HEADS * HD), BF16), vm((counts[0], HEADS * HD), BF16),
        vm((TAPS, GROUP, C), F32), vm((TAPS, GROUP, C), F32), vm((HEADS, GROUP, HD), F32), vm((HEADS, GROUP, HD), F32),
        vm((TAPS, 2, GROUP, C), BF16), vm((HEADS, 2, GROUP, HD), BF16), vm((2, tiles, GROUP, C), BF16),
        vm((C, C), F32), vm((C, C), F32), vm((C, C), BF16), vm((C, C), BF16),
        vm((C, C), BF16), vm((C, C), BF16), vm((3, half, C), BF16),
        dma((chunks,)), dma((chunks, n_arrive + 1)),
        dma((2, 4)), dma((2, 4)),
        dma((blocks,)), dma((blocks,)),
        dma((blocks, 2)), dma((2, 8, most)), dma((2, 4, most)), dma((2, d0.size - 1)),
        dma((4, longest)), dma((4, longest)),
        dma((5,)), dma((HEADS + sum(a for a, _ in sizes),)),
        dma((blocks,)), dma((tiles,)), dma((2,)), dma((2,)), dma((2,)),
        dma((3, tiles * s.share)), dma((3, blocks)),
    ]
    out_shape = (
        jax.ShapeDtypeStruct((counts[0], HEADS * HD), BF16),
        *(jax.ShapeDtypeStruct((a, b, C), F32) for a, b in sizes),
        jax.ShapeDtypeStruct((heads_pad, HD), F32),
        jax.ShapeDtypeStruct((3, TAPS, GROUP, C), BF16),
        jax.ShapeDtypeStruct((3, HEADS, GROUP, HD), BF16),
    )
    vmem = pl.BlockSpec(memory_space=pltpu.VMEM)
    smem = pl.BlockSpec(memory_space=pltpu.SMEM)
    hbm = pl.BlockSpec(memory_space=pl.ANY)

    def kernel(*refs):
        train_kernel(s, shapes, refs)

    return pl.pallas_call(
        kernel,
        name="train",
        out_shape=out_shape,
        in_specs=[vmem] * 5 + [smem] * 2 + [vmem] * 4 + [hbm] * 9,
        out_specs=[hbm] * 4 + [vmem] * 3,
        scratch_shapes=scratch,
        compiler_params=pltpu.CompilerParams(collective_id=0, has_side_effects=True, vmem_limit_bytes=VMEM_LIMIT),
        cost_estimate=pl.CostEstimate(flops=13 * 10**9, bytes_accessed=10**7, transcendentals=0),
    )(*args)


def finish_kernel(shapes, refs):
    (got, goth, cfirst, csecond, cmaster, hfirst, hsecond, hmaster, gains, gain, gfirst, gsecond, step_ref,
     merged_in, full_in, half_in, quarter_in,
     merged, gfull, ghalf, gquarter, cgrad, hgrad, cfirst_new, csecond_new, cmaster_new, ccopy,
     hfirst_new, hsecond_new, hmaster_new, hcopy, ggrad, gfirst_new, gsecond_new, gain_new,
     stage_a, stage_b, stage_c, stage_d, load_sem, store_sem) = refs
    HEADS = shapes["HEADS"]
    passed = [(merged_in, stage_a, merged), (full_in, stage_b, gfull), (half_in, stage_c, ghalf), (quarter_in, stage_d, gquarter)]
    loads = [pltpu.make_async_copy(a, b, load_sem.at[i]) for i, (a, b, _) in enumerate(passed)]
    stores = [pltpu.make_async_copy(b, o, store_sem.at[i]) for i, (_, b, o) in enumerate(passed)]
    for copy in loads:
        copy.start()

    def rows(arrays, count, first, second, master, outs):
        grad_out, first_out, second_out, master_out, copy_out = outs
        for k in range(count):
            grad_out[k] = arrays[0, k].astype(F32)
            rot = arrays[1, k].astype(F32)
            first_out[k] = beta_one * first[k] + (1.0 - beta_one) * rot
            second_out[k] = beta_two * second[k] + (1.0 - beta_two) * rot * rot
            old = master[k]
            new = old - learn_rate * (arrays[2, k].astype(F32) + weight_decay * old)
            master_out[k] = new
            copy_out[k] = new.astype(BF16)

    for load, store in zip(loads, stores):
        load.wait()
        store.start()
    rows(got, TAPS, cfirst, csecond, cmaster, (cgrad, cfirst_new, csecond_new, cmaster_new, ccopy))
    rows(goth, HEADS, hfirst, hsecond, hmaster, (hgrad, hfirst_new, hsecond_new, hmaster_new, hcopy))
    total = gains[0:HEADS, :]
    first_new, second_new, direction = adam_parts(total, gfirst[...], gsecond[...], step_ref, total.shape[1])
    ggrad[...] = total
    gfirst_new[...] = first_new
    gsecond_new[...] = second_new
    gain_new[...] = gain[...] - gain_rate * (direction + weight_decay * gain[...])
    for store in stores:
        store.wait()


def finish_call(shapes, args, like):
    vmem = pl.BlockSpec(memory_space=pltpu.VMEM)
    smem = pl.BlockSpec(memory_space=pltpu.SMEM)
    hbm = pl.BlockSpec(memory_space=pl.ANY)

    def kernel(*refs):
        finish_kernel(shapes, refs)

    return pl.pallas_call(
        kernel,
        name="finish",
        out_shape=like,
        in_specs=[vmem] * 12 + [smem] + [hbm] * 4,
        out_specs=[hbm] * 4 + [vmem] * 14,
        scratch_shapes=[*(pltpu.VMEM(x.shape, x.dtype) for x in like[:4]), pltpu.SemaphoreType.DMA((4,)), pltpu.SemaphoreType.DMA((4,))],
        compiler_params=pltpu.CompilerParams(vmem_limit_bytes=60 << 20),
    )(*args)


def shapes_of(image_full, image_half, image_quarter, heads_copy):
    return {
        "C": image_full.shape[2], "HD": heads_copy.shape[2], "HEADS": heads_copy.shape[1],
        "sizes": [p.shape[:2] for p in (image_full, image_half, image_quarter)],
    }


def per_device(
    s, image_full, image_half, image_quarter, row_pads, tile_mask, aff_scale, aff_shift, conv_copy, heads_copy, gain,
    grad_out, step_count, conv_master, conv_first, conv_second, conv_left, conv_right, heads_master, heads_first,
    heads_second, heads_left, heads_right, gain_first, gain_second,
):
    shapes = shapes_of(image_full, image_half, image_quarter, heads_copy)
    C, HEADS, HD = shapes["C"], shapes["HEADS"], shapes["HD"]

    def grouped(x):
        x = x if s.share == 1 else lax.all_gather(x, "cols", axis=0, tiled=True)
        return turned(x)

    def turned(x):
        return x.transpose(1, 0, 2)

    merged, gfull, ghalf, gquarter, gains, got, goth = train_call(s, shapes, (
        grouped(conv_copy), grouped(heads_copy), image_full, image_half, image_quarter, row_pads, step_count,
        tile_mask, aff_scale.reshape(1, C), aff_shift.reshape(1, C), gain, grad_out.reshape(-1, HEADS * HD),
        grouped(conv_first), grouped(conv_second), grouped(heads_first), grouped(heads_second),
        conv_left, conv_right, heads_left, heads_right))
    if s.share > 1:
        rows = conv_first.shape[0]
        start = lax.rem(lax.axis_index("cols"), s.share) * rows
        got, goth = (lax.dynamic_slice_in_dim(x, start, rows, 2) for x in (got, goth))
    states = [turned(x) for x in (conv_first, conv_second, conv_master, heads_first, heads_second, heads_master)]
    conv = jax.ShapeDtypeStruct(states[0].shape, F32)
    head = jax.ShapeDtypeStruct(states[3].shape, F32)
    conv_low = jax.ShapeDtypeStruct(conv.shape, BF16)
    head_low = jax.ShapeDtypeStruct(head.shape, BF16)
    small = jax.ShapeDtypeStruct(gain.shape, F32)
    like = tuple(jax.ShapeDtypeStruct(x.shape, x.dtype) for x in (merged, gfull, ghalf, gquarter)) + (
        conv, head, conv, conv, conv, conv_low, head, head, head, head_low, small, small, small, small)
    outs = finish_call(shapes, (
        got, goth, *states, gains, gain, gain_first, gain_second, step_count, merged, gfull, ghalf, gquarter), like)
    return (outs[0].reshape(grad_out.shape), *outs[1:4], *[turned(x) for x in outs[4:14]], *outs[14:])


def solution(mesh):
    s = Slice(mesh, 512 // mesh.devices.size)
    pixels, rows, all_ = P("rows", "cols", None), P(("rows", "cols"), None, None), P()
    return jax.shard_map(
        functools.partial(per_device, s),
        mesh=mesh,
        in_specs=(
            pixels, pixels, pixels, all_, P("rows", "cols"), all_, all_, rows, rows, all_, pixels, all_,
            rows, rows, rows, all_, all_, rows, rows, rows, all_, all_, all_, all_,
        ),
        out_specs=(pixels,) * 4 + (rows,) * 10 + (all_,) * 4,
        check_vma=False,
    )
```

```python
import functools

import jax
import jax.numpy as jnp
from jax import lax
from jax.experimental import pallas as pl
from jax.experimental.pallas import tpu as pltpu
from jax.sharding import PartitionSpec as P

beta_one = 0.95
beta_two = 0.95
adam_eps = 1e-08
norm_eps = 1e-06
learn_rate = 0.02
gain_rate = 1.0
weight_decay = 0.01

MESH = pl.DeviceIdType.MESH
BF16 = jnp.bfloat16
F32 = jnp.float32
GROUP = 16
CHUNK_TAPS = (3, 3, 3)
CHUNK_HEADS = (3, 4)
PLAN = (
    ("own", 0), ("columns",), ("own", 1), ("own", 2), ("constants",), ("tier", 0, 0), ("wide",), ("cotangent",),
    ("tier", 0, 1), ("tier", 1, 0), ("own", 3), ("narrow",), ("moments",), ("bases",),
    ("tier", 0, 2), ("tier", 1, 1), ("tier", 2, 0), ("own", 4),
    ("tier", 0, 3), ("tier", 1, 2), ("tier", 2, 1), ("windows",), ("core", 0), ("conv", 0, 3), ("tier", 0, 4), ("core", 1), ("conv", 3, 6),
    ("tier", 1, 3), ("tier", 2, 2), ("core", 2), ("conv", 6, 9), ("tier", 1, 4), ("activation",),
    ("tier", 2, 3), ("core", 3), ("heads", 0, 2), ("tier", 2, 4), ("heads", 2, 3), ("share",), ("core", 4), ("ship", 0, 3), ("heads", 3, 7),
)
LAGS = (2, 7, 12)
IMAGE_TURN = 18
VMEM_LIMIT = 63 << 20
TAPS = 9


def nn(a, b):
    return jnp.dot(a, b, preferred_element_type=F32)


def nt(a, b):
    return lax.dot_general(a, b, (((1,), (1,)), ((), ())), preferred_element_type=F32)


def tn(a, b):
    return lax.dot_general(a, b, (((0,), (0,)), ((), ())), preferred_element_type=F32)


class Dim:
    def __init__(self, size, row_step, col_step):
        self.size, self.row_step, self.col_step = size, row_step, col_step

    def coord(self, r, c):
        if self.row_step:
            return lax.rem(lax.div(r, self.row_step), self.size)
        return lax.rem(lax.div(c, self.col_step), self.size)


class Slice:
    def __init__(self, mesh, rows_per_device):
        self.rows, self.cols = mesh.devices.shape
        self.share = max(1, GROUP // rows_per_device)
        place = {}
        try:
            for r in range(self.rows):
                for c in range(self.cols):
                    device = mesh.devices[r, c]
                    place[(*device.coords, device.core_on_chip)] = (r, c)
        except AttributeError:
            place = {}
            for r in range(self.rows):
                for c in range(self.cols):
                    if self.rows == 8:
                        key = (c // 2, r % 2, r // 2, c % 2)
                    else:
                        key = (c, r // 8, r // 2 % 4, r % 2)
                    place[key] = (r, c)
        origin = tuple(min(k[a] for k in place) for a in range(4))
        dims = []
        for axis in range(4):
            size = max(k[axis] for k in place) - origin[axis] + 1
            step = list(origin)
            step[axis] += 1
            there = place[tuple(step)]
            dims.append(Dim(size, *there))
        self.core = dims[3]
        chips = dims[:3]
        inside = [d for d in chips if d.row_step == 0 and d.col_step < self.share]
        lines = [d for d in chips if d not in inside]
        lines.sort(key=lambda d: -d.size)
        self.lines = lines
        self.chips = lines + inside
        self.groups = self.rows * self.cols // self.share


class Here:
    def __init__(self, s):
        self.s = s
        self.r = lax.axis_index("rows")
        self.c = lax.axis_index("cols")
        self.place = {d: d.coord(self.r, self.c) for d in [*s.chips, s.core]}

    def at(self, dim):
        return self.place[dim]

    def moved(self, steps):
        r, c = self.r, self.c
        for dim, there in steps:
            delta = there - self.at(dim)
            r = r + delta * dim.row_step
            c = c + delta * dim.col_step
        return r, c

    def ahead(self, dim, step):
        return lax.rem(self.at(dim) + step, dim.size)

    def behind(self, dim, step):
        return lax.rem(self.at(dim) + dim.size - step, dim.size)

    def group(self, place):
        r, c = place
        return lax.div(r * self.s.cols + c, self.s.share)


def remote(src, dst, send, recv, where):
    return pltpu.make_async_remote_copy(
        src_ref=src, dst_ref=dst, send_sem=send, recv_sem=recv, device_id=where, device_id_type=MESH
    )


def gather_plan(s):
    lines = s.lines
    first = lines[0]
    plans = []
    own = []
    for s0 in range(first.size):
        rest = list(lines[1:])
        if s0 >= 1:
            rest.reverse()
        onward = [(d, st) for d in rest for st in range(1, d.size)]
        if s0 == 0:
            own = [(first, st) for st in range(1, first.size)] + onward
        else:
            plans.append((0, ((first, s0),), onward))
        if rest:
            for s1 in range(1, rest[0].size):
                on = [(d, st) for d in rest[1:] for st in range(1, d.size)]
                plans.append((1, ((first, s0), (rest[0], s1)), on))
            for d in rest[1:]:
                for s2 in range(1, d.size):
                    for s1 in range(rest[0].size):
                        plans.append((2, ((first, s0), (rest[0], s1), (d, s2)), []))
    plans.sort(key=lambda p: p[0])
    return own, plans


def log2(n):
    return n.bit_length() - 1


def home_of(s, b):
    d0, d1, d2 = s.chips
    t = b - TAPS
    tap = b < TAPS
    column = jnp.where(tap, lax.rem(b, 4), jnp.where(t < 3, t + 1, t - 3))
    along = jnp.where(tap, jnp.where(b < 4, 2, jnp.where(b < 8, 1, 0)), jnp.where(t < 3, 0, 3))
    return {d0: along, d1: lax.div(column, 2), d2: lax.rem(column, 2)}


def block_at(along, column):
    early = jnp.where(column == 0, TAPS - 1, TAPS + column - 1)
    taps = jnp.where(along == 2, column, 4 + column)
    return jnp.where(along == 0, early, jnp.where(along == 3, TAPS + 3 + column, taps))


def adam_parts(grad, first, second, step_ref, lanes):
    first_new = beta_one * first + (1.0 - beta_one) * grad
    second_new = beta_two * second + (1.0 - beta_two) * grad * grad
    count = jnp.full((1, lanes), step_ref[0].astype(F32), F32)
    scale_one = 1.0 / (1.0 - jnp.exp(count * jnp.log(jnp.full((1, lanes), beta_one, F32))))
    scale_two = 1.0 / (1.0 - jnp.exp(count * jnp.log(jnp.full((1, lanes), beta_two, F32))))
    direction = first_new * scale_one / (jnp.sqrt(second_new * scale_two) + adam_eps)
    return first_new, second_new, direction


def train_kernel(s, shapes, refs):
    (conv_w, head_w, full_ref, half_ref, quarter_ref, pads, step_ref, tile_ref, scale_ref, shift_ref, gain_ref,
     go_hbm, cfirst_hbm, csecond_hbm, hfirst_hbm, hsecond_hbm, cleft, cright, hleft, hright,
     merged_hbm, gfull_hbm, ghalf_hbm, gquarter_hbm, gainsum_ref, got_ref, goth_ref,
     W, Z, MK, RIMS, ENDS, CORNERS, STRIPS, COLUMNS, POINTS, MKF, U, UT, PRE, GA, ACT, GP, GG, GX,
     A, AH, SC, SCH, RC, RCH, SB, SBH, R1A, R1B, R2A, R2B, R3A, R3B,
     GO, MERGED, CF, CS_, HF, HS, FT, FTH, FB, LV, RV, LB, RB, TB, VB, OUT,
     ag_send, ag_recv, halo_send, halo_recv, core_send, core_recv, rs_send, rs1_recv, rs2_recv, rs3_recv,
     gx_send, gx_recv, load_sem, store_sem, first_send, first_recv, base_sem, swap_send, swap_recv,
     out_send, out_recv) = refs
    here = Here(s)
    C, HD, HEADS = shapes["C"], shapes["HD"], shapes["HEADS"]
    sizes = shapes["sizes"]
    counts = [a * b for a, b in sizes]
    offs = [0, counts[0], counts[0] + counts[1]]
    n_pix = sum(counts)
    n_rest = n_pix - counts[0]
    half = C // 2
    blocks = TAPS + HEADS
    tiles = half // GROUP
    r, c = here.r, here.c
    core = here.at(s.core)
    sibling = here.moved([(s.core, 1 - core)])
    d0, d1, d2 = s.chips
    own_group = here.group((r, c))
    my_half = lax.div(own_group, tiles)
    my_tile = lax.rem(own_group, tiles)
    at_home = (here.at(d1) < 2) & (here.at(d2) < 2)
    block = block_at(here.at(d0), here.at(d1) * 2 + here.at(d2))
    is_conv = at_home & (block < TAPS)
    is_head = at_home & (block >= TAPS)

    loads = [(go_hbm, GO), (cfirst_hbm, CF), (csecond_hbm, CS_), (hfirst_hbm, HF), (hsecond_hbm, HS)]
    loads = [pltpu.make_async_copy(a, b, load_sem.at[i]) for i, (a, b) in enumerate(loads)]

    def bases(conv, do):
        if conv:
            pairs = [(cleft, LV), (cright, RV)]
        else:
            t = jnp.maximum(block - TAPS, 0)
            pairs = [(hleft.at[t], LV), (hright.at[t], RV.at[0:HD, 0:HD])]
        for i, (a, b) in enumerate(pairs):
            copy = pltpu.make_async_copy(a, b, base_sem.at[i])
            copy.start() if do == "start" else copy.wait()

    for ref in (RIMS, ENDS, CORNERS):
        ref[...] = jnp.zeros_like(ref)

    def owner(b):
        return here.moved([*home_of(s, b).items(), (s.core, my_half)])

    def holder(i, copy):
        device = (core * tiles + i) * s.share + copy
        return lax.div(device, s.cols), lax.rem(device, s.cols)

    def is_me(where):
        return (where[0] == r) & (where[1] == c)

    barrier = pltpu.get_barrier_semaphore()

    def greet(where):
        pl.semaphore_signal(barrier, inc=1, device_id=where, device_id_type=MESH)

    greeted = [sibling]
    for d in s.chips:
        greeted += [here.moved([(d, here.ahead(d, st))]) for st in range(1, d.size)]
    greeted += [
        (lax.rem(r + 1, s.rows), c), (lax.rem(r + s.rows - 1, s.rows), c),
        (r, lax.rem(c + 1, s.cols)), (r, lax.rem(c + s.cols - 1, s.cols)),
    ]
    greeted += [(lax.rem(r + s.rows + a, s.rows), lax.rem(c + s.cols + b, s.cols)) for a in (-1, 1) for b in (-1, 1)]
    for g in greeted:
        greet(g)

    def greet_owner(b, carry):
        where = owner(b)
        pl.when(jnp.logical_not(is_me(where)))(lambda: greet(where))
        return carry

    lax.fori_loop(0, blocks, greet_owner, 0)

    @pl.when(at_home)
    def _():
        def greet_holder(i, carry):
            for copy in range(s.share):
                where = holder(i, copy)
                pl.when(jnp.logical_not(is_me(where)))(lambda: greet(where))
            return carry
        lax.fori_loop(0, tiles, greet_holder, 0)

    same = (at_home & (my_half == core)).astype(jnp.int32)
    n_greets = len(greeted) + blocks - same + jnp.where(at_home, s.share * tiles - same, 0)

    for k in range(TAPS):
        W[own_group, :, k * C : (k + 1) * C] = conv_w[k]
    for t in range(HEADS):
        W[own_group, :, TAPS * C + t * HD : TAPS * C + (t + 1) * HD] = head_w[t]

    pl.semaphore_wait(barrier, n_greets)

    def valid_of(scale, row):
        rows_here = sizes[scale][0]
        limit = rows_here * s.rows - pads[scale]
        return jnp.where(r * rows_here + row < limit, 1.0, 0.0).astype(F32)

    pictures = (full_ref, half_ref, quarter_ref)
    segments = [(sc, row, offs[sc] + row * sizes[sc][1], sizes[sc][1]) for sc in range(3) for row in range(sizes[sc][0])]

    def mask_pixels():
        for sc, row, start, count in segments:
            MK[start : start + count, :] = (pictures[sc][row].astype(F32) * valid_of(sc, row)).astype(BF16)
        stage_borders(0, MK)

    strip_at = [0, sizes[0][1], sizes[0][1] + sizes[1][1]]
    padded_rows = [(sc, j) for sc in range(3) for j in range(sizes[sc][0] + 2)]

    def pixel_row(pixels, sc, row):
        start = offs[sc] + row * sizes[sc][1]
        return pixels[start : start + sizes[sc][1], :]

    def stage_borders(which, pixels):
        for sc in range(3):
            lanes = slice(strip_at[sc], strip_at[sc] + sizes[sc][1])
            last = sizes[sc][0] - 1
            STRIPS[which, 0, lanes, :] = pixel_row(pixels, sc, 0)
            STRIPS[which, 1, lanes, :] = pixel_row(pixels, sc, last)
        for index, (sc, row, start, count) in enumerate(segments):
            for end, at in ((0, start), (1, start + count - 1)):
                tile = at // 16 * 16
                x = pixels[tile : tile + 16, :].astype(F32)[at - tile : at - tile + 1]
                COLUMNS[which, end, index : index + 1, :] = x
                for side, edge in ((0, 0), (1, sizes[sc][0] - 1)):
                    if row == edge:
                        POINTS[which, 2 * side + end, sc : sc + 1, :] = x

    def beside(r_step, c_step):
        there = jnp.bool_(True)
        if r_step:
            there = there & ((r > 0) if r_step < 0 else (r < s.rows - 1))
        if c_step:
            there = there & ((c > 0) if c_step < 0 else (c < s.cols - 1))
        return there, (r + r_step, c + c_step)

    wide = slice(0, strip_at[1])
    narrow = slice(strip_at[1], strip_at[2] + sizes[2][1])
    wide_way, narrow_way = (
        [(beside(-1, 0), STRIPS, RIMS, 0, 1, number, rows), (beside(1, 0), STRIPS, RIMS, 1, 0, number + 1, rows)]
        for number, rows in ((0, wide), (8, narrow))
    )
    rows_way = wide_way + narrow_way
    every = slice(None)
    ends_way = [(beside(0, -1), COLUMNS, ENDS, 0, 1, 2, every), (beside(0, 1), COLUMNS, ENDS, 1, 0, 3, every)]
    ends_way += [
        (beside(2 * v - 1, 2 * h - 1), POINTS, CORNERS, 2 * v + h, 3 - 2 * v - h, 4 + 2 * v + h, every)
        for v in (0, 1) for h in (0, 1)
    ]

    def send_borders(which, ways):
        for (there, where), staged, landing, end, other, number, rows in ways:
            back = {0: 1, 1: 0, 2: 3, 3: 2, 4: 7, 5: 6, 6: 5, 7: 4, 8: 9, 9: 8}[number]
            copy = remote(staged.at[which, end, rows], landing.at[which, other, rows], halo_send.at[which, number],
                          halo_recv.at[which, back], where)
            pl.when(there)(copy.start)

    def wait_borders(which, ways, do):
        for (there, where), staged, landing, end, _, number, rows in ways:
            copy = remote(staged.at[which, end, rows], landing.at[which, end, rows], halo_send.at[which, number],
                          halo_recv.at[which, number], where)
            pl.when(there)(copy.wait_recv if do == "recv" else copy.wait_send)

    def shifted(which, x, sc, j):
        count = sizes[sc][1]

        def beyond(end):
            if 0 < j <= sizes[sc][0]:
                index = sum(a for a, _ in sizes[:sc]) + j - 1
                return ENDS[which, end, index : index + 1, :]
            return CORNERS[which, 2 * (j > 0) + end, sc : sc + 1, :]

        x = x.astype(F32)
        place = lax.broadcasted_iota(jnp.int32, (count, C), 0)
        before = jnp.where(place == 0, beyond(0), pltpu.roll(x, 1, 0))
        after = jnp.where(place == count - 1, beyond(1), pltpu.roll(x, count - 1, 0))
        return before.astype(BF16), after.astype(BF16)

    def put_windows(sc, j, b, value):
        for a in range(3):
            row = j - a
            if 0 <= row < sizes[sc][0]:
                start = offs[sc] + row * sizes[sc][1]
                Z[3 * a + b, start : start + sizes[sc][1], :] = value

    def windows(which, pixels, rims):
        for sc, j in padded_rows:
            lanes = slice(strip_at[sc], strip_at[sc] + sizes[sc][1])
            if 0 < j <= sizes[sc][0]:
                x = pixel_row(pixels, sc, j - 1)
            elif rims:
                x = RIMS[which, int(j > 0), lanes, :]
            else:
                zero = jnp.zeros((sizes[sc][1], C), BF16)
                for b in range(3):
                    put_windows(sc, j, b, zero)
                continue
            before, after = shifted(which, x, sc, j)
            for b, value in enumerate((before, x, after)):
                put_windows(sc, j, b, value)

    own_sends, plan = gather_plan(s)
    chunk_lanes = []
    for count, unit in [*((n, C) for n in CHUNK_TAPS), *((n, HD) for n in CHUNK_HEADS)]:
        start = chunk_lanes[-1].stop if chunk_lanes else 0
        chunk_lanes.append(slice(start, start + count * unit))
    chunks = len(chunk_lanes)
    n_arrive = len(plan)

    def block_of(offsets):
        return here.moved([(d, here.behind(d, st)) for d, st in offsets if st])

    def steps_of(offsets):
        return tuple(sum(st for dd, st in offsets if dd is d) for d in s.lines)

    arrival = {steps_of(offsets): index for index, (_, offsets, _) in enumerate(plan)}
    sends = [(-1, d, st, arrival[steps_of([(d, st)])]) for d, st in own_sends]
    for index, (_, offsets, onward) in enumerate(plan):
        sends += [(index, d, st, arrival[steps_of([*offsets, (d, st)])]) for d, st in onward]
    n_sends = len(sends)

    def place_of(index):
        return (r, c) if index < 0 else block_of(plan[index][1])

    def pass_on(ch, index):
        rows = W.at[here.group(place_of(index)), :, chunk_lanes[ch]]
        for number, (source, d, st, lands) in enumerate(sends):
            if source == index:
                remote(rows, rows, ag_send.at[ch], ag_recv.at[ch, lands],
                       here.moved([(d, here.ahead(d, st))])).start()
        remote(rows, rows, ag_send.at[ch], ag_recv.at[ch, n_arrive], sibling).start()

    def arrive(ch, index):
        rows = W.at[here.group(place_of(index)), :, chunk_lanes[ch]]
        remote(rows, rows, ag_send.at[ch], ag_recv.at[ch, index], sibling).wait_recv()

    def arrive_sibling(ch):
        rows = W.at[0 : n_arrive + 1, :, chunk_lanes[ch]]
        remote(rows, rows, ag_send.at[ch], ag_recv.at[ch, n_arrive], sibling).wait_recv()

    pass_on(0, -1)
    for load in loads:
        load.start()
    pl.when(is_conv)(lambda: bases(True, "start"))
    pl.when(is_head)(lambda: bases(False, "start"))
    mask_pixels()

    def conv_tap(k, carry):
        kernel = W[:, :, pl.ds(pl.multiple_of(k * C, C), C)].reshape(C, C)
        PRE[...] += nn(Z[k], kernel)
        return carry

    PRE[...] = jnp.zeros_like(PRE)
    GA[...] = jnp.zeros_like(GA)
    GG[...] = jnp.zeros_like(GG)

    def constants():
        tile_cols = sizes[0][1] // tile_ref.shape[1]
        cell = (sizes[0][1], tile_ref.shape[1])
        column = lax.broadcasted_iota(jnp.int32, cell, 0)
        tile = lax.broadcasted_iota(jnp.int32, cell, 1)
        picked = jnp.where((column >> log2(tile_cols)) == tile, tile_ref[...].astype(F32), 0.0)
        mask_row = jnp.broadcast_to(jnp.sum(picked, axis=1, keepdims=True), (sizes[0][1], HD))
        for row in range(sizes[0][0]):
            MKF[row * sizes[0][1] : (row + 1) * sizes[0][1], :] = mask_row

        def coarse(full_pixel):
            row = full_pixel >> log2(sizes[0][1])
            col = full_pixel & (sizes[0][1] - 1)
            one = (row >> 1) * sizes[1][1] + (col >> 1)
            two = counts[1] + (row >> 2) * sizes[2][1] + (col >> 2)
            return one, two

        one, two = coarse(lax.broadcasted_iota(jnp.int32, (counts[0], n_rest), 0))
        rest = lax.broadcasted_iota(jnp.int32, (counts[0], n_rest), 1)
        U[...] = jnp.where((one == rest) | (two == rest), 1.0, 0.0).astype(BF16)
        one, two = coarse(lax.broadcasted_iota(jnp.int32, (n_rest, counts[0]), 1))
        rest = lax.broadcasted_iota(jnp.int32, (n_rest, counts[0]), 0)
        UT[...] = jnp.where((one == rest) | (two == rest), 1.0, 0.0).astype(BF16)

    def stage_moments():
        for load in loads[1:]:
            load.wait()
        for k in range(TAPS):
            FT[k, 0] = CF[k].astype(BF16)
            FT[k, 1] = CS_[k].astype(BF16)
        for t in range(HEADS):
            FTH[t, 0] = HF[t].astype(BF16)
            FTH[t, 1] = HS[t].astype(BF16)

    sends_rows = (lax.rem(r * s.cols + c, s.share) == 0) if s.share > 1 else None

    def moments(b, staged, lanes, do):
        where = owner(b)
        there = FB.at[:, my_tile, :, 0:lanes]
        me = is_me(where)
        away = jnp.logical_not(me)
        if sends_rows is not None:
            me, away = me & sends_rows, away & sends_rows
        if do == "start":
            @pl.when(me)
            def _():
                pltpu.make_async_copy(staged, there, first_recv.at[my_tile]).start()

        @pl.when(away)
        def _():
            copy = remote(staged, there, first_send.at[b], first_recv.at[my_tile], where)
            copy.start() if do == "start" else copy.wait_send()

    def over_blocks(step):
        def conv_block(k, carry):
            step(k, k, True)
            return carry

        def head_block(t, carry):
            step(TAPS + t, t, False)
            return carry
        lax.fori_loop(0, TAPS, conv_block, 0)
        lax.fori_loop(0, HEADS, head_block, 0)

    def all_moments(do):
        over_blocks(lambda b, i, conv: moments(b, FT.at[i] if conv else FTH.at[i], C if conv else HD, do))

    def base_casts():
        def cast(conv):
            bases(conv, "wait")
            n = C if conv else HD
            LB[...] = LV[...].astype(BF16)
            RB[0:n, 0:n] = RV[0:n, 0:n].astype(BF16)
        pl.when(is_conv)(lambda: cast(True))
        pl.when(is_head)(lambda: cast(False))

    def activation():
        for sc, row, start, count in segments:
            biased = PRE[start : start + count, :] * scale_ref[...] + shift_ref[...]
            ACT[start : start + count, :] = (jnp.maximum(biased, 0.0) * valid_of(sc, row)).astype(BF16)

    def mask_cotangent():
        loads[0].wait()
        for t in range(HEADS):
            lanes = slice(t * HD, (t + 1) * HD)
            GO[:, lanes] = (GO[:, lanes].astype(F32) * MKF[...]).astype(BF16)

    own_half = pl.ds(pl.multiple_of(core * half, half), half)
    other_half = pl.ds(pl.multiple_of((1 - core) * half, half), half)

    def core_copy(b, staged, landing):
        return remote(staged, landing, core_send.at[b], core_recv.at[b], sibling)

    def merged_store(t):
        lanes = pl.ds(pl.multiple_of(t * HD, HD), HD)
        return pltpu.make_async_copy(MERGED.at[:, lanes], merged_hbm.at[:, lanes], store_sem.at[t])

    def head(t):
        weights = W[:, :, pl.ds(pl.multiple_of(TAPS * C + t * HD, HD), HD)].reshape(C, HD)
        hidden = nn(ACT[...], weights)
        inverse = lax.rsqrt(jnp.mean(hidden * hidden, axis=-1, keepdims=True) + norm_eps)
        unit = hidden * inverse
        gain = gain_ref[t : t + 1, :]
        normed = gain * unit
        lifted = nn(U[...], normed[counts[0] :].astype(BF16))
        lanes = pl.ds(pl.multiple_of(t * HD, HD), HD)
        MERGED[:, lanes] = (MKF[...] * (normed[: counts[0]] + lifted)).astype(BF16)
        merged_store(t).start()
        back = GO[:, lanes]
        pooled = jnp.concatenate([back.astype(F32), nn(UT[...], back)], axis=0)
        product = pooled * unit
        GG[t : t + 1, :] = jnp.sum(product, axis=0, keepdims=True)
        middle = jnp.mean(gain * product, axis=-1, keepdims=True)
        grad_hidden = (inverse * (gain * pooled - unit * middle)).astype(BF16)
        SCH[t] = tn(ACT[:, other_half], grad_hidden).astype(BF16)
        core_copy(TAPS + t, SCH.at[t], RCH.at[t]).start()
        AH[t] = tn(ACT[:, own_half], grad_hidden)
        GA[...] += nt(grad_hidden, weights)

    conv_set = (A, SC, RC, SB, C)
    head_set = (AH, SCH, RCH, SBH, HD)
    piece = half // 4
    part_ways = ((d1, d2), (d2, d1))
    firsts, seconds, thirds = (R1A, R1B), (R2A, R2B), (R3A, R3B)

    def rows_of_part(way, h):
        return pl.ds(pl.multiple_of((2 * way + h) * piece, piece), piece)

    def landing(stage, place, way, h, slot, lanes):
        rows = pl.ds(pl.multiple_of(h * piece, piece), piece)
        if stage == 1:
            which = place[d0] * 2 + place[part_ways[way][1]]
            return firsts[way].at[which, slot, rows, 0:lanes], rs1_recv.at[2 * way + h, which, slot]
        if stage == 2:
            return seconds[way].at[place[d0], slot, rows, 0:lanes], rs2_recv.at[2 * way + h, place[d0], slot]
        return thirds[way].at[slot, rows, 0:lanes], rs3_recv.at[2 * way + h, slot]

    def ship(stage, b, i, group, way, h, dim):
        total, _, _, staged, lanes = group
        place = home_of(s, b)
        rows = rows_of_part(way, h)
        staged[i, rows, :] = total[i, rows, :].astype(BF16)
        for st in range(1, dim.size):
            @pl.when(lax.rem(place[dim] + st, dim.size) == here.at(dim))
            def _():
                buffer, sem = landing(stage, place, way, h, st - 1, lanes)
                remote(staged.at[i, rows, :], buffer, rs_send.at[b, 2 * way + h], sem,
                       here.moved([(dim, place[dim])])).start()

    def take(stage, b, i, group, way, h, dim):
        total, _, _, staged, lanes = group
        place = home_of(s, b)
        rows = rows_of_part(way, h)
        for st in range(1, dim.size):
            buffer, sem = landing(stage, place, way, h, st - 1, lanes)
            remote(staged.at[i, rows, :], buffer, rs_send.at[b, 2 * way + h], sem, sibling).wait_recv()
            total[i, rows, :] += buffer[...].astype(F32)

    def first_ship(b, i, group, h):
        total, staged, landed, _, _ = group

        @pl.when(h == 0)
        def _():
            core_copy(b, staged.at[i], landed.at[i]).wait_recv()
            total[i] += landed[i].astype(F32)

        place = home_of(s, b)
        for way in (0, 1):
            dim = part_ways[way][0]
            pl.when(here.at(dim) != place[dim])(functools.partial(ship, 1, b, i, group, way, h, dim))

    def second_ship(b, i, group, h):
        place = home_of(s, b)
        for way in (0, 1):
            dim, then = part_ways[way]

            @pl.when(here.at(dim) == place[dim])
            def _():
                take(1, b, i, group, way, h, dim)
                pl.when(here.at(then) != place[then])(functools.partial(ship, 2, b, i, group, way, h, then))

    def third_ship(b, i, group, h):
        place = home_of(s, b)
        for way in (0, 1):
            @pl.when((here.at(d1) == place[d1]) & (here.at(d2) == place[d2]))
            def _():
                take(2, b, i, group, way, h, part_ways[way][1])
                pl.when(here.at(d0) != place[d0])(functools.partial(ship, 3, b, i, group, way, h, d0))

    def heads_in(low, high, step):
        def body(j, carry):
            t = lax.div(j, 2)
            step(TAPS + t, t, head_set, lax.rem(j, 2))
            return carry
        lax.fori_loop(2 * low, 2 * high, body, 0)

    tiers = [[i for i, p in enumerate(plan) if p[0] == tier] for tier in range(3)]

    def take_tier(tier, ch):
        for index in tiers[tier]:
            arrive(ch, index)
            pass_on(ch, index)

    def forward_windows():
        wait_borders(0, rows_way + ends_way, "recv")
        windows(0, MK, True)

    acts = {
        "own": lambda ch: pass_on(ch, -1) if ch else None,
        "tier": take_tier,
        "core": arrive_sibling,
        "columns": lambda: send_borders(0, ends_way),
        "wide": lambda: send_borders(0, wide_way),
        "narrow": lambda: send_borders(0, narrow_way),
        "constants": constants,
        "cotangent": mask_cotangent,
        "moments": stage_moments,
        "bases": base_casts,
        "windows": forward_windows,
        "conv": lambda low, high: lax.fori_loop(low, high, conv_tap, 0),
        "activation": activation,
        "heads": lambda low, high: [head(t) for t in range(low, high)],
        "ship": lambda low, high: heads_in(low, high, first_ship),
        "share": lambda: all_moments("start"),
    }
    for word, *numbers in PLAN:
        acts[word](*numbers)
    wait_borders(0, rows_way + ends_way, "send")

    sum_dims = [s.core] + list(reversed(s.chips))

    def gain_send(stage):
        d = sum_dims[stage]
        mine = here.at(d)
        GX[stage, mine] = GG[...]
        for st in range(1, d.size):
            remote(GX.at[stage, mine], GX.at[stage, mine], gx_send.at[stage, st], gx_recv.at[stage, st],
                   here.moved([(d, here.ahead(d, st))])).start()

    def gain_add(stage):
        d = sum_dims[stage]
        for st in range(1, d.size):
            slot = here.behind(d, st)
            remote(GX.at[stage, slot], GX.at[stage, slot], gx_send.at[stage, st], gx_recv.at[stage, st], sibling).wait_recv()
        total = GX[stage, 0]
        for i in range(1, d.size):
            total = total + GX[stage, i]
        GG[...] = total

    gain_send(0)

    for sc, row, start, count in segments:
        pre = PRE[start : start + count, :]
        biased = pre * scale_ref[...] + shift_ref[...]
        grad = jnp.where(biased > 0.0, GA[start : start + count, :], 0.0)
        GP[start : start + count, :] = (scale_ref[...] * grad * valid_of(sc, row)).astype(BF16)

    lag_one, lag_two, lag_three = LAGS
    whole_turns = 2 * (TAPS - 4)
    tap_turns = 2 * TAPS
    early_heads, late_heads = (0, 3), (3, HEADS)

    def conv_stage(step, turn):
        @pl.when((turn >= 0) & (turn < tap_turns))
        def _():
            at = lax.div(turn, 2)
            split = turn - whole_turns
            plain = turn < whole_turns
            k = jnp.where(turn < 2, TAPS - 1, jnp.where(plain, at - 1, 4 + lax.rem(split, 4)))
            step(k, k, conv_set, jnp.where(plain, lax.rem(turn, 2), lax.div(split, 4)))

    def produce(k):
        SC[k] = tn(Z[k, :, other_half], GP[...]).astype(BF16)
        core_copy(k, SC.at[k], RC.at[k]).start()
        A[k] = tn(Z[k, :, own_half], GP[...])

    def image_tap(k, carry):
        kernel = W[:, :, pl.ds(pl.multiple_of(k * C, C), C)].reshape(C, C)
        PRE[...] += nt(Z[TAPS - 1 - k], kernel)
        return carry

    def gradient_turn(turn, carry):
        conv_stage(first_ship, turn - lag_one)
        pl.when(turn < TAPS)(lambda: produce(jnp.where(turn == 0, TAPS - 1, turn - 1)))

        @pl.when(turn == 2)
        def _():
            stage_borders(1, GP)
            send_borders(1, ends_way)
            gain_add(0)
            gain_send(1)

        pl.when(turn == 3)(lambda: heads_in(*early_heads, second_ship))
        pl.when(turn == 8)(lambda: heads_in(*early_heads, third_ship))

        @pl.when(turn == 10)
        def _():
            gain_add(1)
            gain_send(2)

        pl.when(turn == tap_turns + lag_one)(lambda: heads_in(*late_heads, first_ship))
        conv_stage(second_ship, turn - lag_two)
        conv_stage(third_ship, turn - lag_three)

        @pl.when(turn == IMAGE_TURN)
        def _():
            wait_borders(1, ends_way, "recv")
            windows(1, GP, False)
            PRE[...] = jnp.zeros_like(PRE)

        @pl.when(turn > IMAGE_TURN)
        def _():
            low = (turn - IMAGE_TURN - 1) * 2
            lax.fori_loop(jnp.minimum(low, TAPS), jnp.minimum(low + 2, TAPS), image_tap, 0)
        return carry

    turns = max(tap_turns + lag_three, IMAGE_TURN + 6)
    lax.fori_loop(0, turns, gradient_turn, 0)
    heads_in(*late_heads, second_ship)
    heads_in(*late_heads, third_ship)
    send_borders(1, rows_way)
    gain_add(2)
    gain_send(3)

    own_rows = own_half

    def results(array, lanes, conv, do):
        def to_holder(i, carry):
            piece = OUT.at[array, pl.ds(pl.multiple_of(i * GROUP, GROUP), GROUP), 0:lanes]
            there = got_ref.at[array, block] if conv else goth_ref.at[array, block - TAPS]
            for number in range(s.share):
                where = holder(i, number)
                me = is_me(where)
                if do == "start":
                    @pl.when(me)
                    def _():
                        pltpu.make_async_copy(piece, there, out_recv.at[array, block]).start()

                @pl.when(jnp.logical_not(me))
                def _():
                    copy = remote(piece, there, out_send.at[array, i * s.share + number], out_recv.at[array, block], where)
                    copy.start() if do == "start" else copy.wait_send()
            return carry
        lax.fori_loop(0, tiles, to_holder, 0)

    def swap(buffer, lanes, which):
        rows = buffer.at[own_rows, 0:lanes]
        return remote(rows, rows, swap_send.at[which], swap_recv.at[which], sibling)

    def rotate(conv):
        group = conv_set if conv else head_set
        i = block if conv else block - TAPS
        lanes = group[4]
        n = slice(0, lanes)
        for way in (0, 1):
            for h in (0, 1):
                take(3, block, i, group, way, h, d0)
        OUT[0, :, n] = group[0][i].astype(BF16)
        TB[own_rows, n] = nn(OUT[0, :, n], RB[n, n]).astype(BF16)
        swap(TB, lanes, 0).start()
        results(0, lanes, conv, "start")
        swap(TB, lanes, 0).wait()
        rot = tn(LB[:, own_rows], TB[:, n])
        OUT[1, :, n] = rot.astype(BF16)

        def moments_in(j, carry):
            there = FB.at[:, j, :, n]
            remote(there, there, first_send.at[0], first_recv.at[j], sibling).wait_recv()
            return carry
        lax.fori_loop(0, tiles, moments_in, 0)
        first = FB[0].reshape(half, C)[:, n].astype(F32)
        second = FB[1].reshape(half, C)[:, n].astype(F32)
        _, _, direction = adam_parts(rot, first, second, step_ref, lanes)
        VB[own_rows, n] = nt(direction.astype(BF16), RB[n, n]).astype(BF16)
        swap(VB, lanes, 1).start()
        results(1, lanes, conv, "start")
        swap(VB, lanes, 1).wait()
        OUT[2, :, n] = nn(LB[own_rows, :], VB[:, n]).astype(BF16)
        results(2, lanes, conv, "start")

    pl.when(is_conv)(lambda: rotate(True))
    pl.when(is_head)(lambda: rotate(False))
    gain_add(3)
    gainsum_ref[...] = GG[...]

    wait_borders(1, rows_way, "recv")
    strip = sum(b for _, b in sizes)
    for side, a in ((0, 0), (1, 2)):
        for sc in range(3):
            lanes = slice(strip_at[sc], strip_at[sc] + sizes[sc][1])
            x = RIMS[1, side, lanes, :]
            before, after = shifted(1, x, sc, (sizes[sc][0] + 1) * side)
            for b, value in enumerate((before, x, after)):
                Z[3 * a + b, lanes, :] = value
        total = jnp.zeros((strip, C), F32)
        for b in range(3):
            k = TAPS - 1 - (3 * a + b)
            kernel = W[:, :, k * C : (k + 1) * C].reshape(C, C)
            total = total + nt(Z[3 * a + b, 0:strip, :], kernel)
        for sc in range(3):
            start = offs[sc] + side * (sizes[sc][0] - 1) * sizes[sc][1]
            lanes = slice(strip_at[sc], strip_at[sc] + sizes[sc][1])
            PRE[start : start + sizes[sc][1], :] += total[lanes]
    outs = (gfull_hbm, ghalf_hbm, gquarter_hbm)
    picture_stores = []
    for index, (sc, row, start, count) in enumerate(segments):
        PRE[start : start + count, :] = PRE[start : start + count, :] * valid_of(sc, row)
        picture_stores.append(pltpu.make_async_copy(
            PRE.at[start : start + count, :], outs[sc].at[row], store_sem.at[HEADS + index]))
        picture_stores[-1].start()

    for ch in range(chunks):
        rows = W.at[0 : n_sends + n_arrive + 1, :, chunk_lanes[ch]]
        remote(rows, rows, ag_send.at[ch], ag_recv.at[ch, 0], sibling).wait_send()
    all_moments("wait")
    wait_borders(1, rows_way + ends_way, "send")
    for stage, d in enumerate(sum_dims):
        for st in range(1, d.size):
            remote(GX.at[stage, 0], GX.at[stage, 0], gx_send.at[stage, st], gx_recv.at[stage, st], sibling).wait_send()

    def sent_block(b, i, conv):
        _, staged, landed, sb, _ = conv_set if conv else head_set
        core_copy(b, staged.at[i], landed.at[i]).wait_send()
        place = home_of(s, b)
        gone = (here.at(d0) != place[d0]) | (here.at(d1) != place[d1]) | (here.at(d2) != place[d2])
        for way in (0, 1):
            for h in (0, 1):
                @pl.when(gone)
                def _():
                    sent = sb.at[i, rows_of_part(way, h), :]
                    remote(sent, sent, rs_send.at[b, 2 * way + h], rs_send.at[b, 2 * way + h], sibling).wait_send()

    over_blocks(sent_block)

    def results_out(conv):
        for array in range(3):
            results(array, C if conv else HD, conv, "wait")

    pl.when(is_conv)(lambda: results_out(True))
    pl.when(is_head)(lambda: results_out(False))
    for array in range(3):
        def result_in(b, i, conv):
            there = got_ref.at[array, i] if conv else goth_ref.at[array, i]
            remote(there, there, out_send.at[0, 0], out_recv.at[array, b], sibling).wait_recv()
        over_blocks(result_in)

    def stored(t, carry):
        merged_store(t).wait()
        return carry

    lax.fori_loop(0, HEADS, stored, 0)
    for store in picture_stores:
        store.wait()


def train_call(s, shapes, args):
    C, HD, HEADS, sizes = shapes["C"], shapes["HD"], shapes["HEADS"], shapes["sizes"]
    counts = [a * b for a, b in sizes]
    n_pix = sum(counts)
    half = C // 2
    tiles = half // GROUP
    blocks = TAPS + HEADS
    strip = sum(b for _, b in sizes)
    own_sends, plan = gather_plan(s)
    n_arrive = len(plan)
    n_sends = len(own_sends) + sum(len(p[2]) for p in plan)
    chunks = len(CHUNK_TAPS) + len(CHUNK_HEADS)
    d0, d1, d2 = s.chips
    most = max(d1.size, d2.size) - 1
    lanes_all = TAPS * C + HEADS * HD
    heads_pad = -(-HEADS // 8) * 8
    cut = rest = half // 2
    eight = -(-sum(a for a, _ in sizes) // 8) * 8
    dma = pltpu.SemaphoreType.DMA
    vm = pltpu.VMEM
    longest = max(s.core.size, *(d.size for d in s.chips))
    scratch = [
        vm((s.groups, GROUP, lanes_all), BF16),
        vm((TAPS, n_pix, C), BF16),
        vm((n_pix, C), BF16),
        vm((2, 2, strip, C), BF16), vm((2, 2, eight, C), F32), vm((2, 4, 8, C), F32),
        vm((2, 2, strip, C), BF16), vm((2, 2, eight, C), F32), vm((2, 4, 8, C), F32),
        vm((counts[0], HD), F32),
        vm((counts[0], n_pix - counts[0]), BF16), vm((n_pix - counts[0], counts[0]), BF16),
        vm((n_pix, C), F32), vm((n_pix, C), F32),
        vm((n_pix, C), BF16), vm((n_pix, C), BF16),
        vm((heads_pad, HD), F32), vm((4, longest, heads_pad, HD), F32),
        vm((TAPS, half, C), F32), vm((HEADS, half, HD), F32),
        vm((TAPS, half, C), BF16), vm((HEADS, half, HD), BF16),
        vm((TAPS, half, C), BF16), vm((HEADS, half, HD), BF16),
        vm((TAPS, half, C), BF16), vm((HEADS, half, HD), BF16),
        vm((8, most, cut, C), BF16), vm((8, most, rest, C), BF16),
        vm((4, most, cut, C), BF16), vm((4, most, rest, C), BF16),
        vm((d0.size - 1, cut, C), BF16), vm((d0.size - 1, rest, C), BF16),
        vm((counts[0], HEADS * HD), BF16), vm((counts[0], HEADS * HD), BF16),
        vm((TAPS, GROUP, C), F32), vm((TAPS, GROUP, C), F32), vm((HEADS, GROUP, HD), F32), vm((HEADS, GROUP, HD), F32),
        vm((TAPS, 2, GROUP, C), BF16), vm((HEADS, 2, GROUP, HD), BF16), vm((2, tiles, GROUP, C), BF16),
        vm((C, C), F32), vm((C, C), F32), vm((C, C), BF16), vm((C, C), BF16),
        vm((C, C), BF16), vm((C, C), BF16), vm((3, half, C), BF16),
        dma((chunks,)), dma((chunks, n_arrive + 1)),
        dma((2, 10)), dma((2, 10)),
        dma((blocks,)), dma((blocks,)),
        dma((blocks, 4)), dma((4, 8, most)), dma((4, 4, most)), dma((4, d0.size - 1)),
        dma((4, longest)), dma((4, longest)),
        dma((5,)), dma((HEADS + sum(a for a, _ in sizes),)),
        dma((blocks,)), dma((tiles,)), dma((2,)), dma((2,)), dma((2,)),
        dma((3, tiles * s.share)), dma((3, blocks)),
    ]
    out_shape = (
        jax.ShapeDtypeStruct((counts[0], HEADS * HD), BF16),
        *(jax.ShapeDtypeStruct((a, b, C), F32) for a, b in sizes),
        jax.ShapeDtypeStruct((heads_pad, HD), F32),
        jax.ShapeDtypeStruct((3, TAPS, GROUP, C), BF16),
        jax.ShapeDtypeStruct((3, HEADS, GROUP, HD), BF16),
    )
    vmem = pl.BlockSpec(memory_space=pltpu.VMEM)
    smem = pl.BlockSpec(memory_space=pltpu.SMEM)
    hbm = pl.BlockSpec(memory_space=pl.ANY)

    def kernel(*refs):
        train_kernel(s, shapes, refs)

    return pl.pallas_call(
        kernel,
        name="train",
        out_shape=out_shape,
        in_specs=[vmem] * 5 + [smem] * 2 + [vmem] * 4 + [hbm] * 9,
        out_specs=[hbm] * 4 + [vmem] * 3,
        scratch_shapes=scratch,
        compiler_params=pltpu.CompilerParams(collective_id=0, has_side_effects=True, vmem_limit_bytes=VMEM_LIMIT),
        cost_estimate=pl.CostEstimate(flops=13 * 10**9, bytes_accessed=10**7, transcendentals=0),
    )(*args)


def finish_kernel(shapes, refs):
    inputs, outputs, rest = refs[:16], refs[16:34], refs[34:]
    step_ref, rest = rest[0], rest[1:]
    staged, made, load_sem, store_sem = rest[:16], rest[16:-2], rest[-2], rest[-1]
    HEADS = shapes["HEADS"]
    loads = [pltpu.make_async_copy(a, b, load_sem.at[i]) for i, (a, b) in enumerate(zip(inputs, staged))]
    for load in loads:
        load.start()
    held = (*staged[:4], *made)
    stores = [pltpu.make_async_copy(a, b, store_sem.at[i]) for i, (a, b) in enumerate(zip(held, outputs))]
    got, goth, cfirst, csecond, cmaster, hfirst, hsecond, hmaster, gains, gain, gfirst, gsecond = staged[4:]
    (cgrad, hgrad, cfirst_new, csecond_new, cmaster_new, ccopy, hfirst_new, hsecond_new, hmaster_new, hcopy,
     ggrad, gfirst_new, gsecond_new, gain_new) = made

    def rows(arrays, count, first, second, master, outs):
        grad_out, first_out, second_out, master_out, copy_out = outs
        for k in range(count):
            grad_out[k] = arrays[0, k].astype(F32)
            rot = arrays[1, k].astype(F32)
            first_out[k] = beta_one * first[k] + (1.0 - beta_one) * rot
            second_out[k] = beta_two * second[k] + (1.0 - beta_two) * rot * rot
            old = master[k]
            new = old - learn_rate * (arrays[2, k].astype(F32) + weight_decay * old)
            master_out[k] = new
            copy_out[k] = new.astype(BF16)

    def wait(*indices):
        for i in indices:
            loads[i].wait()

    def store(*indices):
        for i in indices:
            stores[i].start()

    wait(4, 6, 7, 8)
    rows(got, TAPS, cfirst, csecond, cmaster, (cgrad, cfirst_new, csecond_new, cmaster_new, ccopy))
    store(4, 6, 7, 8, 9)
    wait(5, 9, 10, 11)
    rows(goth, HEADS, hfirst, hsecond, hmaster, (hgrad, hfirst_new, hsecond_new, hmaster_new, hcopy))
    store(5, 10, 11, 12, 13)
    for i in range(4):
        wait(i)
        store(i)
    wait(12, 13, 14, 15)
    total = gains[0:HEADS, :]
    first_new, second_new, direction = adam_parts(total, gfirst[...], gsecond[...], step_ref, total.shape[1])
    ggrad[...] = total
    gfirst_new[...] = first_new
    gsecond_new[...] = second_new
    gain_new[...] = gain[...] - gain_rate * (direction + weight_decay * gain[...])
    store(14, 15, 16, 17)
    for copy in stores:
        copy.wait()


def finish_call(shapes, args, like):
    smem = pl.BlockSpec(memory_space=pltpu.SMEM)
    hbm = pl.BlockSpec(memory_space=pl.ANY)
    n = len(args) - 1

    def kernel(step_ref, *refs):
        finish_kernel(shapes, (*refs[: n + len(like)], step_ref, *refs[n + len(like) :]))

    return pl.pallas_call(
        kernel,
        name="finish",
        out_shape=like,
        in_specs=[smem] + [hbm] * n,
        out_specs=[hbm] * len(like),
        scratch_shapes=[
            *(pltpu.VMEM(x.shape, x.dtype) for x in args[1:]), *(pltpu.VMEM(x.shape, x.dtype) for x in like[4:]),
            pltpu.SemaphoreType.DMA((n,)), pltpu.SemaphoreType.DMA((len(like),)),
        ],
        compiler_params=pltpu.CompilerParams(vmem_limit_bytes=VMEM_LIMIT),
    )(*args)


def shapes_of(image_full, image_half, image_quarter, heads_copy):
    return {
        "C": image_full.shape[2], "HD": heads_copy.shape[2], "HEADS": heads_copy.shape[1],
        "sizes": [p.shape[:2] for p in (image_full, image_half, image_quarter)],
    }


def per_device(
    s, image_full, image_half, image_quarter, row_pads, tile_mask, aff_scale, aff_shift, conv_copy, heads_copy, gain,
    grad_out, step_count, conv_master, conv_first, conv_second, conv_left, conv_right, heads_master, heads_first,
    heads_second, heads_left, heads_right, gain_first, gain_second,
):
    shapes = shapes_of(image_full, image_half, image_quarter, heads_copy)
    C, HEADS, HD = shapes["C"], shapes["HEADS"], shapes["HD"]

    def grouped(x):
        x = x if s.share == 1 else lax.all_gather(x, "cols", axis=0, tiled=True)
        return turned(x)

    def turned(x):
        return x.transpose(1, 0, 2)

    merged, gfull, ghalf, gquarter, gains, got, goth = train_call(s, shapes, (
        grouped(conv_copy), grouped(heads_copy), image_full, image_half, image_quarter, row_pads, step_count,
        tile_mask, aff_scale.reshape(1, C), aff_shift.reshape(1, C), gain, grad_out.reshape(-1, HEADS * HD),
        grouped(conv_first), grouped(conv_second), grouped(heads_first), grouped(heads_second),
        conv_left, conv_right, heads_left, heads_right))
    if s.share > 1:
        rows = conv_first.shape[0]
        start = lax.rem(lax.axis_index("cols"), s.share) * rows
        got, goth = (lax.dynamic_slice_in_dim(x, start, rows, 2) for x in (got, goth))
    states = [turned(x) for x in (conv_first, conv_second, conv_master, heads_first, heads_second, heads_master)]
    conv = jax.ShapeDtypeStruct(states[0].shape, F32)
    head = jax.ShapeDtypeStruct(states[3].shape, F32)
    conv_low = jax.ShapeDtypeStruct(conv.shape, BF16)
    head_low = jax.ShapeDtypeStruct(head.shape, BF16)
    small = jax.ShapeDtypeStruct(gain.shape, F32)
    like = tuple(jax.ShapeDtypeStruct(x.shape, x.dtype) for x in (merged, gfull, ghalf, gquarter)) + (
        conv, head, conv, conv, conv, conv_low, head, head, head, head_low, small, small, small, small)
    outs = finish_call(shapes, (
        step_count, merged, gfull, ghalf, gquarter, got, goth, *states, gains, gain, gain_first, gain_second), like)
    return (outs[0].reshape(grad_out.shape), *outs[1:4], *[turned(x) for x in outs[4:14]], *outs[14:])


def solution(mesh):
    s = Slice(mesh, 512 // mesh.devices.size)
    pixels, rows, all_ = P("rows", "cols", None), P(("rows", "cols"), None, None), P()
    return jax.shard_map(
        functools.partial(per_device, s),
        mesh=mesh,
        in_specs=(
            pixels, pixels, pixels, all_, P("rows", "cols"), all_, all_, rows, rows, all_, pixels, all_,
            rows, rows, rows, all_, all_, rows, rows, rows, all_, all_, all_, all_,
        ),
        out_specs=(pixels,) * 4 + (rows,) * 10 + (all_,) * 4,
        check_vma=False,
    )
```

```python
import functools

import jax
import jax.numpy as jnp
from jax import lax
from jax.experimental import pallas as pl
from jax.experimental.pallas import tpu as pltpu
from jax.sharding import PartitionSpec as P

beta_one = 0.95
beta_two = 0.95
adam_eps = 1e-08
norm_eps = 1e-06
learn_rate = 0.02
gain_rate = 1.0
weight_decay = 0.01

MESH = pl.DeviceIdType.MESH
BF16 = jnp.bfloat16
F32 = jnp.float32
GROUP = 16
CHUNK_TAPS = (3, 3, 3)
CHUNK_HEADS = (3, 4)
PLAN = (
    ("own", 0), ("columns",), ("own", 1), ("own", 2), ("constants",), ("tier", 0, 0), ("wide",), ("cotangent",),
    ("tier", 0, 1), ("tier", 1, 0), ("own", 3), ("narrow",), ("moments",), ("bases",),
    ("tier", 0, 2), ("tier", 1, 1), ("tier", 2, 0), ("own", 4),
    ("tier", 0, 3), ("tier", 1, 2), ("tier", 2, 1), ("windows",), ("core", 0), ("conv", 0, 3), ("tier", 0, 4), ("core", 1), ("conv", 3, 6),
    ("tier", 1, 3), ("tier", 2, 2), ("core", 2), ("conv", 6, 9), ("tier", 1, 4), ("activation",),
    ("tier", 2, 3), ("core", 3), ("heads", 0, 2), ("tier", 2, 4), ("heads", 2, 3), ("share",), ("core", 4), ("ship", 0, 3), ("heads", 3, 7),
)
LAGS = (1, 6, 11)
IMAGE_TURN = 19
VMEM_LIMIT = 63 << 20
TAPS = 9


def nn(a, b):
    return jnp.dot(a, b, preferred_element_type=F32)


def nt(a, b):
    return lax.dot_general(a, b, (((1,), (1,)), ((), ())), preferred_element_type=F32)


def tn(a, b):
    return lax.dot_general(a, b, (((0,), (0,)), ((), ())), preferred_element_type=F32)


class Dim:
    def __init__(self, size, row_step, col_step):
        self.size, self.row_step, self.col_step = size, row_step, col_step

    def coord(self, r, c):
        if self.row_step:
            return lax.rem(lax.div(r, self.row_step), self.size)
        return lax.rem(lax.div(c, self.col_step), self.size)


class Slice:
    def __init__(self, mesh, rows_per_device):
        self.rows, self.cols = mesh.devices.shape
        self.share = max(1, GROUP // rows_per_device)
        place = {}
        try:
            for r in range(self.rows):
                for c in range(self.cols):
                    device = mesh.devices[r, c]
                    place[(*device.coords, device.core_on_chip)] = (r, c)
        except AttributeError:
            place = {}
            for r in range(self.rows):
                for c in range(self.cols):
                    if self.rows == 8:
                        key = (c // 2, r % 2, r // 2, c % 2)
                    else:
                        key = (c, r // 8, r // 2 % 4, r % 2)
                    place[key] = (r, c)
        origin = tuple(min(k[a] for k in place) for a in range(4))
        dims = []
        for axis in range(4):
            size = max(k[axis] for k in place) - origin[axis] + 1
            step = list(origin)
            step[axis] += 1
            there = place[tuple(step)]
            dims.append(Dim(size, *there))
        self.core = dims[3]
        chips = dims[:3]
        inside = [d for d in chips if d.row_step == 0 and d.col_step < self.share]
        lines = [d for d in chips if d not in inside]
        lines.sort(key=lambda d: -d.size)
        self.lines = lines
        self.chips = lines + inside
        self.groups = self.rows * self.cols // self.share


class Here:
    def __init__(self, s):
        self.s = s
        self.r = lax.axis_index("rows")
        self.c = lax.axis_index("cols")
        self.place = {d: d.coord(self.r, self.c) for d in [*s.chips, s.core]}

    def at(self, dim):
        return self.place[dim]

    def moved(self, steps):
        r, c = self.r, self.c
        for dim, there in steps:
            delta = there - self.at(dim)
            r = r + delta * dim.row_step
            c = c + delta * dim.col_step
        return r, c

    def ahead(self, dim, step):
        return lax.rem(self.at(dim) + step, dim.size)

    def behind(self, dim, step):
        return lax.rem(self.at(dim) + dim.size - step, dim.size)

    def group(self, place):
        r, c = place
        return lax.div(r * self.s.cols + c, self.s.share)


def remote(src, dst, send, recv, where):
    return pltpu.make_async_remote_copy(
        src_ref=src, dst_ref=dst, send_sem=send, recv_sem=recv, device_id=where, device_id_type=MESH
    )


def gather_plan(s):
    lines = s.lines
    first = lines[0]
    plans = []
    own = []
    for s0 in range(first.size):
        rest = list(lines[1:])
        if s0 >= 1:
            rest.reverse()
        onward = [(d, st) for d in rest for st in range(1, d.size)]
        if s0 == 0:
            own = [(first, st) for st in range(1, first.size)] + onward
        else:
            plans.append((0, ((first, s0),), onward))
        if rest:
            for s1 in range(1, rest[0].size):
                on = [(d, st) for d in rest[1:] for st in range(1, d.size)]
                plans.append((1, ((first, s0), (rest[0], s1)), on))
            for d in rest[1:]:
                for s2 in range(1, d.size):
                    for s1 in range(rest[0].size):
                        plans.append((2, ((first, s0), (rest[0], s1), (d, s2)), []))
    plans.sort(key=lambda p: p[0])
    return own, plans


def log2(n):
    return n.bit_length() - 1


def home_of(s, b):
    d0, d1, d2 = s.chips
    t = b - TAPS
    tap = b < TAPS
    column = jnp.where(tap, lax.rem(b, 4), jnp.where(t < 3, t + 1, t - 3))
    along = jnp.where(tap, jnp.where(b < 4, 2, jnp.where(b < 8, 1, 0)), jnp.where(t < 3, 0, 3))
    return {d0: along, d1: lax.div(column, 2), d2: lax.rem(column, 2)}


def block_at(along, column):
    early = jnp.where(column == 0, TAPS - 1, TAPS + column - 1)
    taps = jnp.where(along == 2, column, 4 + column)
    return jnp.where(along == 0, early, jnp.where(along == 3, TAPS + 3 + column, taps))


def adam_parts(grad, first, second, step_ref, lanes):
    first_new = beta_one * first + (1.0 - beta_one) * grad
    second_new = beta_two * second + (1.0 - beta_two) * grad * grad
    count = jnp.full((1, lanes), step_ref[0].astype(F32), F32)
    scale_one = 1.0 / (1.0 - jnp.exp(count * jnp.log(jnp.full((1, lanes), beta_one, F32))))
    scale_two = 1.0 / (1.0 - jnp.exp(count * jnp.log(jnp.full((1, lanes), beta_two, F32))))
    direction = first_new * scale_one / (jnp.sqrt(second_new * scale_two) + adam_eps)
    return first_new, second_new, direction


def train_kernel(s, shapes, refs):
    (conv_w, head_w, full_ref, half_ref, quarter_ref, pads, step_ref, tile_ref, scale_ref, shift_ref, gain_ref,
     go_hbm, cfirst_hbm, csecond_hbm, hfirst_hbm, hsecond_hbm, cleft, cright, hleft, hright,
     merged_hbm, gfull_hbm, ghalf_hbm, gquarter_hbm, gainsum_ref, got_ref, goth_ref,
     W, Z, MK, RIMS, ENDS, CORNERS, STRIPS, COLUMNS, POINTS, MKF, U, UT, PRE, GA, ACT, GP, GG, GX,
     A, AH, SC, SCH, RC, RCH, SB, SBH, R1A, R1B, R2A, R2B, R3A, R3B,
     GO, MERGED, CF, CS_, HF, HS, FT, FTH, FB, LV, RV, LB, RB, TB, VB, OUT,
     ag_send, ag_recv, halo_send, halo_recv, core_send, core_recv, rs_send, rs1_recv, rs2_recv, rs3_recv,
     gx_send, gx_recv, load_sem, store_sem, first_send, first_recv, base_sem, swap_send, swap_recv,
     out_send, out_recv) = refs
    here = Here(s)
    C, HD, HEADS = shapes["C"], shapes["HD"], shapes["HEADS"]
    sizes = shapes["sizes"]
    counts = [a * b for a, b in sizes]
    offs = [0, counts[0], counts[0] + counts[1]]
    n_pix = sum(counts)
    n_rest = n_pix - counts[0]
    half = C // 2
    blocks = TAPS + HEADS
    tiles = half // GROUP
    r, c = here.r, here.c
    core = here.at(s.core)
    sibling = here.moved([(s.core, 1 - core)])
    d0, d1, d2 = s.chips
    own_group = here.group((r, c))
    my_half = lax.div(own_group, tiles)
    my_tile = lax.rem(own_group, tiles)
    at_home = (here.at(d1) < 2) & (here.at(d2) < 2)
    block = block_at(here.at(d0), here.at(d1) * 2 + here.at(d2))
    is_conv = at_home & (block < TAPS)
    is_head = at_home & (block >= TAPS)

    loads = [(go_hbm, GO), (cfirst_hbm, CF), (csecond_hbm, CS_), (hfirst_hbm, HF), (hsecond_hbm, HS)]
    loads = [pltpu.make_async_copy(a, b, load_sem.at[i]) for i, (a, b) in enumerate(loads)]

    def bases(conv, do):
        if conv:
            pairs = [(cleft, LV), (cright, RV)]
        else:
            t = jnp.maximum(block - TAPS, 0)
            pairs = [(hleft.at[t], LV), (hright.at[t], RV.at[0:HD, 0:HD])]
        for i, (a, b) in enumerate(pairs):
            copy = pltpu.make_async_copy(a, b, base_sem.at[i])
            copy.start() if do == "start" else copy.wait()

    for ref in (RIMS, ENDS, CORNERS):
        ref[...] = jnp.zeros_like(ref)

    def owner(b):
        return here.moved([*home_of(s, b).items(), (s.core, my_half)])

    def holder(i, copy):
        device = (core * tiles + i) * s.share + copy
        return lax.div(device, s.cols), lax.rem(device, s.cols)

    def is_me(where):
        return (where[0] == r) & (where[1] == c)

    barrier = pltpu.get_barrier_semaphore()

    def greet(where):
        pl.semaphore_signal(barrier, inc=1, device_id=where, device_id_type=MESH)

    greeted = [sibling]
    for d in s.chips:
        greeted += [here.moved([(d, here.ahead(d, st))]) for st in range(1, d.size)]
    greeted += [
        (lax.rem(r + 1, s.rows), c), (lax.rem(r + s.rows - 1, s.rows), c),
        (r, lax.rem(c + 1, s.cols)), (r, lax.rem(c + s.cols - 1, s.cols)),
    ]
    greeted += [(lax.rem(r + s.rows + a, s.rows), lax.rem(c + s.cols + b, s.cols)) for a in (-1, 1) for b in (-1, 1)]
    for g in greeted:
        greet(g)

    def greet_owner(b, carry):
        where = owner(b)
        pl.when(jnp.logical_not(is_me(where)))(lambda: greet(where))
        return carry

    lax.fori_loop(0, blocks, greet_owner, 0)

    @pl.when(at_home)
    def _():
        def greet_holder(i, carry):
            for copy in range(s.share):
                where = holder(i, copy)
                pl.when(jnp.logical_not(is_me(where)))(lambda: greet(where))
            return carry
        lax.fori_loop(0, tiles, greet_holder, 0)

    same = (at_home & (my_half == core)).astype(jnp.int32)
    n_greets = len(greeted) + blocks - same + jnp.where(at_home, s.share * tiles - same, 0)

    for k in range(TAPS):
        W[own_group, :, k * C : (k + 1) * C] = conv_w[k]
    for t in range(HEADS):
        W[own_group, :, TAPS * C + t * HD : TAPS * C + (t + 1) * HD] = head_w[t]

    pl.semaphore_wait(barrier, n_greets)

    def valid_of(scale, row):
        rows_here = sizes[scale][0]
        limit = rows_here * s.rows - pads[scale]
        return jnp.where(r * rows_here + row < limit, 1.0, 0.0).astype(F32)

    pictures = (full_ref, half_ref, quarter_ref)
    segments = [(sc, row, offs[sc] + row * sizes[sc][1], sizes[sc][1]) for sc in range(3) for row in range(sizes[sc][0])]

    def mask_pixels():
        for sc, row, start, count in segments:
            MK[start : start + count, :] = (pictures[sc][row].astype(F32) * valid_of(sc, row)).astype(BF16)
        stage_borders(0, MK)

    strip_at = [0, sizes[0][1], sizes[0][1] + sizes[1][1]]
    padded_rows = [(sc, j) for sc in range(3) for j in range(sizes[sc][0] + 2)]

    def pixel_row(pixels, sc, row):
        start = offs[sc] + row * sizes[sc][1]
        return pixels[start : start + sizes[sc][1], :]

    def stage_borders(which, pixels):
        for sc in range(3):
            lanes = slice(strip_at[sc], strip_at[sc] + sizes[sc][1])
            last = sizes[sc][0] - 1
            STRIPS[which, 0, lanes, :] = pixel_row(pixels, sc, 0)
            STRIPS[which, 1, lanes, :] = pixel_row(pixels, sc, last)
        for index, (sc, row, start, count) in enumerate(segments):
            for end, at in ((0, start), (1, start + count - 1)):
                tile = at // 16 * 16
                x = pixels[tile : tile + 16, :].astype(F32)[at - tile : at - tile + 1]
                COLUMNS[which, end, index : index + 1, :] = x
                for side, edge in ((0, 0), (1, sizes[sc][0] - 1)):
                    if row == edge:
                        POINTS[which, 2 * side + end, sc : sc + 1, :] = x

    def beside(r_step, c_step):
        there = jnp.bool_(True)
        if r_step:
            there = there & ((r > 0) if r_step < 0 else (r < s.rows - 1))
        if c_step:
            there = there & ((c > 0) if c_step < 0 else (c < s.cols - 1))
        return there, (r + r_step, c + c_step)

    wide = slice(0, strip_at[1])
    narrow = slice(strip_at[1], strip_at[2] + sizes[2][1])
    wide_way, narrow_way = (
        [(beside(-1, 0), STRIPS, RIMS, 0, 1, number, rows), (beside(1, 0), STRIPS, RIMS, 1, 0, number + 1, rows)]
        for number, rows in ((0, wide), (8, narrow))
    )
    rows_way = wide_way + narrow_way
    every = slice(None)
    ends_way = [(beside(0, -1), COLUMNS, ENDS, 0, 1, 2, every), (beside(0, 1), COLUMNS, ENDS, 1, 0, 3, every)]
    ends_way += [
        (beside(2 * v - 1, 2 * h - 1), POINTS, CORNERS, 2 * v + h, 3 - 2 * v - h, 4 + 2 * v + h, every)
        for v in (0, 1) for h in (0, 1)
    ]

    def send_borders(which, ways):
        for (there, where), staged, landing, end, other, number, rows in ways:
            back = {0: 1, 1: 0, 2: 3, 3: 2, 4: 7, 5: 6, 6: 5, 7: 4, 8: 9, 9: 8}[number]
            copy = remote(staged.at[which, end, rows], landing.at[which, other, rows], halo_send.at[which, number],
                          halo_recv.at[which, back], where)
            pl.when(there)(copy.start)

    def wait_borders(which, ways, do):
        for (there, where), staged, landing, end, _, number, rows in ways:
            copy = remote(staged.at[which, end, rows], landing.at[which, end, rows], halo_send.at[which, number],
                          halo_recv.at[which, number], where)
            pl.when(there)(copy.wait_recv if do == "recv" else copy.wait_send)

    def shifted(which, x, sc, j):
        count = sizes[sc][1]

        def beyond(end):
            if 0 < j <= sizes[sc][0]:
                index = sum(a for a, _ in sizes[:sc]) + j - 1
                return ENDS[which, end, index : index + 1, :]
            return CORNERS[which, 2 * (j > 0) + end, sc : sc + 1, :]

        x = x.astype(F32)
        place = lax.broadcasted_iota(jnp.int32, (count, C), 0)
        before = jnp.where(place == 0, beyond(0), pltpu.roll(x, 1, 0))
        after = jnp.where(place == count - 1, beyond(1), pltpu.roll(x, count - 1, 0))
        return before.astype(BF16), after.astype(BF16)

    def put_windows(sc, j, b, value):
        for a in range(3):
            row = j - a
            if 0 <= row < sizes[sc][0]:
                start = offs[sc] + row * sizes[sc][1]
                Z[3 * a + b, start : start + sizes[sc][1], :] = value

    def windows(which, pixels, rims):
        for sc, j in padded_rows:
            lanes = slice(strip_at[sc], strip_at[sc] + sizes[sc][1])
            if 0 < j <= sizes[sc][0]:
                x = pixel_row(pixels, sc, j - 1)
            elif rims:
                x = RIMS[which, int(j > 0), lanes, :]
            else:
                zero = jnp.zeros((sizes[sc][1], C), BF16)
                for b in range(3):
                    put_windows(sc, j, b, zero)
                continue
            before, after = shifted(which, x, sc, j)
            for b, value in enumerate((before, x, after)):
                put_windows(sc, j, b, value)

    own_sends, plan = gather_plan(s)
    chunk_lanes = []
    for count, unit in [*((n, C) for n in CHUNK_TAPS), *((n, HD) for n in CHUNK_HEADS)]:
        start = chunk_lanes[-1].stop if chunk_lanes else 0
        chunk_lanes.append(slice(start, start + count * unit))
    chunks = len(chunk_lanes)
    n_arrive = len(plan)

    def block_of(offsets):
        return here.moved([(d, here.behind(d, st)) for d, st in offsets if st])

    def steps_of(offsets):
        return tuple(sum(st for dd, st in offsets if dd is d) for d in s.lines)

    arrival = {steps_of(offsets): index for index, (_, offsets, _) in enumerate(plan)}
    sends = [(-1, d, st, arrival[steps_of([(d, st)])]) for d, st in own_sends]
    for index, (_, offsets, onward) in enumerate(plan):
        sends += [(index, d, st, arrival[steps_of([*offsets, (d, st)])]) for d, st in onward]
    n_sends = len(sends)

    def place_of(index):
        return (r, c) if index < 0 else block_of(plan[index][1])

    def pass_on(ch, index):
        rows = W.at[here.group(place_of(index)), :, chunk_lanes[ch]]
        for number, (source, d, st, lands) in enumerate(sends):
            if source == index:
                remote(rows, rows, ag_send.at[ch], ag_recv.at[ch, lands],
                       here.moved([(d, here.ahead(d, st))])).start()
        remote(rows, rows, ag_send.at[ch], ag_recv.at[ch, n_arrive], sibling).start()

    def arrive(ch, index):
        rows = W.at[here.group(place_of(index)), :, chunk_lanes[ch]]
        remote(rows, rows, ag_send.at[ch], ag_recv.at[ch, index], sibling).wait_recv()

    def arrive_sibling(ch):
        rows = W.at[0 : n_arrive + 1, :, chunk_lanes[ch]]
        remote(rows, rows, ag_send.at[ch], ag_recv.at[ch, n_arrive], sibling).wait_recv()

    pass_on(0, -1)
    for load in loads:
        load.start()
    pl.when(is_conv)(lambda: bases(True, "start"))
    pl.when(is_head)(lambda: bases(False, "start"))
    mask_pixels()

    def conv_tap(k, carry):
        kernel = W[:, :, pl.ds(pl.multiple_of(k * C, C), C)].reshape(C, C)
        PRE[...] += nn(Z[k], kernel)
        return carry

    PRE[...] = jnp.zeros_like(PRE)
    GA[...] = jnp.zeros_like(GA)
    GG[...] = jnp.zeros_like(GG)

    def constants():
        tile_cols = sizes[0][1] // tile_ref.shape[1]
        cell = (sizes[0][1], tile_ref.shape[1])
        column = lax.broadcasted_iota(jnp.int32, cell, 0)
        tile = lax.broadcasted_iota(jnp.int32, cell, 1)
        picked = jnp.where((column >> log2(tile_cols)) == tile, tile_ref[...].astype(F32), 0.0)
        mask_row = jnp.broadcast_to(jnp.sum(picked, axis=1, keepdims=True), (sizes[0][1], HD))
        for row in range(sizes[0][0]):
            MKF[row * sizes[0][1] : (row + 1) * sizes[0][1], :] = mask_row

        def coarse(full_pixel):
            row = full_pixel >> log2(sizes[0][1])
            col = full_pixel & (sizes[0][1] - 1)
            one = (row >> 1) * sizes[1][1] + (col >> 1)
            two = counts[1] + (row >> 2) * sizes[2][1] + (col >> 2)
            return one, two

        one, two = coarse(lax.broadcasted_iota(jnp.int32, (counts[0], n_rest), 0))
        rest = lax.broadcasted_iota(jnp.int32, (counts[0], n_rest), 1)
        U[...] = jnp.where((one == rest) | (two == rest), 1.0, 0.0).astype(BF16)
        one, two = coarse(lax.broadcasted_iota(jnp.int32, (n_rest, counts[0]), 1))
        rest = lax.broadcasted_iota(jnp.int32, (n_rest, counts[0]), 0)
        UT[...] = jnp.where((one == rest) | (two == rest), 1.0, 0.0).astype(BF16)

    def stage_moments():
        for load in loads[1:]:
            load.wait()
        for k in range(TAPS):
            FT[k, 0] = CF[k].astype(BF16)
            FT[k, 1] = CS_[k].astype(BF16)
        for t in range(HEADS):
            FTH[t, 0] = HF[t].astype(BF16)
            FTH[t, 1] = HS[t].astype(BF16)

    sends_rows = (lax.rem(r * s.cols + c, s.share) == 0) if s.share > 1 else None

    def moments(b, staged, lanes, do):
        where = owner(b)
        there = FB.at[:, my_tile, :, 0:lanes]
        me = is_me(where)
        away = jnp.logical_not(me)
        if sends_rows is not None:
            me, away = me & sends_rows, away & sends_rows
        if do == "start":
            @pl.when(me)
            def _():
                pltpu.make_async_copy(staged, there, first_recv.at[my_tile]).start()

        @pl.when(away)
        def _():
            copy = remote(staged, there, first_send.at[b], first_recv.at[my_tile], where)
            copy.start() if do == "start" else copy.wait_send()

    def over_blocks(step):
        def conv_block(k, carry):
            step(k, k, True)
            return carry

        def head_block(t, carry):
            step(TAPS + t, t, False)
            return carry
        lax.fori_loop(0, TAPS, conv_block, 0)
        lax.fori_loop(0, HEADS, head_block, 0)

    def all_moments(do):
        over_blocks(lambda b, i, conv: moments(b, FT.at[i] if conv else FTH.at[i], C if conv else HD, do))

    def base_casts():
        def cast(conv):
            bases(conv, "wait")
            n = C if conv else HD
            LB[...] = LV[...].astype(BF16)
            RB[0:n, 0:n] = RV[0:n, 0:n].astype(BF16)
        pl.when(is_conv)(lambda: cast(True))
        pl.when(is_head)(lambda: cast(False))

    def activation():
        for sc, row, start, count in segments:
            biased = PRE[start : start + count, :] * scale_ref[...] + shift_ref[...]
            ACT[start : start + count, :] = (jnp.maximum(biased, 0.0) * valid_of(sc, row)).astype(BF16)

    def mask_cotangent():
        loads[0].wait()
        for t in range(HEADS):
            lanes = slice(t * HD, (t + 1) * HD)
            GO[:, lanes] = (GO[:, lanes].astype(F32) * MKF[...]).astype(BF16)

    own_half = pl.ds(pl.multiple_of(core * half, half), half)
    other_half = pl.ds(pl.multiple_of((1 - core) * half, half), half)

    def core_copy(b, staged, landing):
        return remote(staged, landing, core_send.at[b], core_recv.at[b], sibling)

    def merged_store(t):
        lanes = pl.ds(pl.multiple_of(t * HD, HD), HD)
        return pltpu.make_async_copy(MERGED.at[:, lanes], merged_hbm.at[:, lanes], store_sem.at[t])

    def head(t):
        weights = W[:, :, pl.ds(pl.multiple_of(TAPS * C + t * HD, HD), HD)].reshape(C, HD)
        hidden = nn(ACT[...], weights)
        inverse = lax.rsqrt(jnp.mean(hidden * hidden, axis=-1, keepdims=True) + norm_eps)
        unit = hidden * inverse
        gain = gain_ref[t : t + 1, :]
        normed = gain * unit
        lifted = nn(U[...], normed[counts[0] :].astype(BF16))
        lanes = pl.ds(pl.multiple_of(t * HD, HD), HD)
        MERGED[:, lanes] = (MKF[...] * (normed[: counts[0]] + lifted)).astype(BF16)
        merged_store(t).start()
        back = GO[:, lanes]
        pooled = jnp.concatenate([back.astype(F32), nn(UT[...], back)], axis=0)
        product = pooled * unit
        GG[t : t + 1, :] = jnp.sum(product, axis=0, keepdims=True)
        middle = jnp.mean(gain * product, axis=-1, keepdims=True)
        grad_hidden = (inverse * (gain * pooled - unit * middle)).astype(BF16)
        SCH[t] = tn(ACT[:, other_half], grad_hidden).astype(BF16)
        core_copy(TAPS + t, SCH.at[t], RCH.at[t]).start()
        AH[t] = tn(ACT[:, own_half], grad_hidden)
        GA[...] += nt(grad_hidden, weights)

    conv_set = (A, SC, RC, SB, C)
    head_set = (AH, SCH, RCH, SBH, HD)
    piece = half // 4
    part_ways = ((d1, d2), (d2, d1))
    firsts, seconds, thirds = (R1A, R1B), (R2A, R2B), (R3A, R3B)

    def rows_of_part(way, h):
        return pl.ds(pl.multiple_of((2 * way + h) * piece, piece), piece)

    def landing(stage, place, way, h, slot, lanes):
        rows = pl.ds(pl.multiple_of(h * piece, piece), piece)
        if stage == 1:
            which = place[d0] * 2 + place[part_ways[way][1]]
            return firsts[way].at[which, slot, rows, 0:lanes], rs1_recv.at[2 * way + h, which, slot]
        if stage == 2:
            return seconds[way].at[place[d0], slot, rows, 0:lanes], rs2_recv.at[2 * way + h, place[d0], slot]
        return thirds[way].at[slot, rows, 0:lanes], rs3_recv.at[2 * way + h, slot]

    def ship(stage, b, i, group, way, h, dim):
        total, _, _, staged, lanes = group
        place = home_of(s, b)
        rows = rows_of_part(way, h)
        staged[i, rows, :] = total[i, rows, :].astype(BF16)
        for st in range(1, dim.size):
            @pl.when(lax.rem(place[dim] + st, dim.size) == here.at(dim))
            def _():
                buffer, sem = landing(stage, place, way, h, st - 1, lanes)
                remote(staged.at[i, rows, :], buffer, rs_send.at[b, 2 * way + h], sem,
                       here.moved([(dim, place[dim])])).start()

    def take(stage, b, i, group, way, h, dim):
        total, _, _, staged, lanes = group
        place = home_of(s, b)
        rows = rows_of_part(way, h)
        for st in range(1, dim.size):
            buffer, sem = landing(stage, place, way, h, st - 1, lanes)
            remote(staged.at[i, rows, :], buffer, rs_send.at[b, 2 * way + h], sem, sibling).wait_recv()
            total[i, rows, :] += buffer[...].astype(F32)

    def first_ship(b, i, group, h):
        total, staged, landed, _, _ = group

        @pl.when(h == 0)
        def _():
            core_copy(b, staged.at[i], landed.at[i]).wait_recv()
            total[i] += landed[i].astype(F32)

        place = home_of(s, b)
        for way in (0, 1):
            dim = part_ways[way][0]
            pl.when(here.at(dim) != place[dim])(functools.partial(ship, 1, b, i, group, way, h, dim))

    def second_ship(b, i, group, h):
        place = home_of(s, b)
        for way in (0, 1):
            dim, then = part_ways[way]

            @pl.when(here.at(dim) == place[dim])
            def _():
                take(1, b, i, group, way, h, dim)
                pl.when(here.at(then) != place[then])(functools.partial(ship, 2, b, i, group, way, h, then))

    def third_ship(b, i, group, h):
        place = home_of(s, b)
        for way in (0, 1):
            @pl.when((here.at(d1) == place[d1]) & (here.at(d2) == place[d2]))
            def _():
                take(2, b, i, group, way, h, part_ways[way][1])
                pl.when(here.at(d0) != place[d0])(functools.partial(ship, 3, b, i, group, way, h, d0))

    def heads_in(low, high, step):
        def body(j, carry):
            t = lax.div(j, 2)
            step(TAPS + t, t, head_set, lax.rem(j, 2))
            return carry
        lax.fori_loop(2 * low, 2 * high, body, 0)

    tiers = [[i for i, p in enumerate(plan) if p[0] == tier] for tier in range(3)]

    def take_tier(tier, ch):
        for index in tiers[tier]:
            arrive(ch, index)
            pass_on(ch, index)

    def forward_windows():
        wait_borders(0, rows_way + ends_way, "recv")
        windows(0, MK, True)

    acts = {
        "own": lambda ch: pass_on(ch, -1) if ch else None,
        "tier": take_tier,
        "core": arrive_sibling,
        "columns": lambda: send_borders(0, ends_way),
        "wide": lambda: send_borders(0, wide_way),
        "narrow": lambda: send_borders(0, narrow_way),
        "constants": constants,
        "cotangent": mask_cotangent,
        "moments": stage_moments,
        "bases": base_casts,
        "windows": forward_windows,
        "conv": lambda low, high: lax.fori_loop(low, high, conv_tap, 0),
        "activation": activation,
        "heads": lambda low, high: [head(t) for t in range(low, high)],
        "ship": lambda low, high: heads_in(low, high, first_ship),
        "share": lambda: all_moments("start"),
    }
    for word, *numbers in PLAN:
        acts[word](*numbers)
    wait_borders(0, rows_way + ends_way, "send")

    sum_dims = [s.core] + list(reversed(s.chips))

    def gain_send(stage):
        d = sum_dims[stage]
        mine = here.at(d)
        GX[stage, mine] = GG[...]
        for st in range(1, d.size):
            remote(GX.at[stage, mine], GX.at[stage, mine], gx_send.at[stage, st], gx_recv.at[stage, st],
                   here.moved([(d, here.ahead(d, st))])).start()

    def gain_add(stage):
        d = sum_dims[stage]
        for st in range(1, d.size):
            slot = here.behind(d, st)
            remote(GX.at[stage, slot], GX.at[stage, slot], gx_send.at[stage, st], gx_recv.at[stage, st], sibling).wait_recv()
        total = GX[stage, 0]
        for i in range(1, d.size):
            total = total + GX[stage, i]
        GG[...] = total

    gain_send(0)

    for sc, row, start, count in segments:
        pre = PRE[start : start + count, :]
        biased = pre * scale_ref[...] + shift_ref[...]
        grad = jnp.where(biased > 0.0, GA[start : start + count, :], 0.0)
        GP[start : start + count, :] = (scale_ref[...] * grad * valid_of(sc, row)).astype(BF16)

    lag_one, lag_two, lag_three = LAGS
    whole_turns = 2 * (TAPS - 4)
    tap_turns = 2 * TAPS
    early_heads, late_heads = (0, 3), (3, HEADS)

    def conv_stage(step, turn):
        @pl.when((turn >= 0) & (turn < tap_turns))
        def _():
            at = lax.div(turn, 2)
            split = turn - whole_turns
            plain = turn < whole_turns
            k = jnp.where(turn < 2, TAPS - 1, jnp.where(plain, at - 1, 4 + lax.rem(split, 4)))
            step(k, k, conv_set, jnp.where(plain, lax.rem(turn, 2), lax.div(split, 4)))

    def produce(k):
        SC[k] = tn(Z[k, :, other_half], GP[...]).astype(BF16)
        core_copy(k, SC.at[k], RC.at[k]).start()
        A[k] = tn(Z[k, :, own_half], GP[...])

    def image_tap(k, carry):
        kernel = W[:, :, pl.ds(pl.multiple_of(k * C, C), C)].reshape(C, C)
        PRE[...] += nt(Z[TAPS - 1 - k], kernel)
        return carry

    def gradient_turn(turn, carry):
        conv_stage(first_ship, turn - lag_one)
        pl.when(turn < TAPS)(lambda: produce(jnp.where(turn == 0, TAPS - 1, turn - 1)))

        @pl.when(turn == 2)
        def _():
            stage_borders(1, GP)
            send_borders(1, ends_way)
            gain_add(0)
            gain_send(1)

        pl.when(turn == 3)(lambda: heads_in(*early_heads, second_ship))
        pl.when(turn == 8)(lambda: heads_in(*early_heads, third_ship))

        @pl.when(turn == 10)
        def _():
            gain_add(1)
            gain_send(2)

        pl.when(turn == tap_turns + lag_one)(lambda: heads_in(*late_heads, first_ship))
        conv_stage(second_ship, turn - lag_two)
        conv_stage(third_ship, turn - lag_three)

        @pl.when(turn == IMAGE_TURN)
        def _():
            wait_borders(1, ends_way, "recv")
            windows(1, GP, False)
            PRE[...] = jnp.zeros_like(PRE)

        @pl.when(turn > IMAGE_TURN)
        def _():
            low = (turn - IMAGE_TURN - 1) * 2
            lax.fori_loop(jnp.minimum(low, TAPS), jnp.minimum(low + 2, TAPS), image_tap, 0)
        return carry

    turns = max(tap_turns + lag_three, IMAGE_TURN + 6)
    lax.fori_loop(0, turns, gradient_turn, 0)
    heads_in(*late_heads, second_ship)
    heads_in(*late_heads, third_ship)
    send_borders(1, rows_way)
    gain_add(2)
    gain_send(3)

    own_rows = own_half

    def results(array, lanes, conv, do):
        def to_holder(i, carry):
            piece = OUT.at[array, pl.ds(pl.multiple_of(i * GROUP, GROUP), GROUP), 0:lanes]
            there = got_ref.at[array, block] if conv else goth_ref.at[array, block - TAPS]
            for number in range(s.share):
                where = holder(i, number)
                me = is_me(where)
                if do == "start":
                    @pl.when(me)
                    def _():
                        pltpu.make_async_copy(piece, there, out_recv.at[array, block]).start()

                @pl.when(jnp.logical_not(me))
                def _():
                    copy = remote(piece, there, out_send.at[array, i * s.share + number], out_recv.at[array, block], where)
                    copy.start() if do == "start" else copy.wait_send()
            return carry
        lax.fori_loop(0, tiles, to_holder, 0)

    def swap(buffer, lanes, which):
        rows = buffer.at[own_rows, 0:lanes]
        return remote(rows, rows, swap_send.at[which], swap_recv.at[which], sibling)

    def rotate(conv):
        group = conv_set if conv else head_set
        i = block if conv else block - TAPS
        lanes = group[4]
        n = slice(0, lanes)
        for way in (0, 1):
            for h in (0, 1):
                take(3, block, i, group, way, h, d0)
        OUT[0, :, n] = group[0][i].astype(BF16)
        TB[own_rows, n] = nn(OUT[0, :, n], RB[n, n]).astype(BF16)
        swap(TB, lanes, 0).start()
        results(0, lanes, conv, "start")
        swap(TB, lanes, 0).wait()
        rot = tn(LB[:, own_rows], TB[:, n])
        OUT[1, :, n] = rot.astype(BF16)

        def moments_in(j, carry):
            there = FB.at[:, j, :, n]
            remote(there, there, first_send.at[0], first_recv.at[j], sibling).wait_recv()
            return carry
        lax.fori_loop(0, tiles, moments_in, 0)
        first = FB[0].reshape(half, C)[:, n].astype(F32)
        second = FB[1].reshape(half, C)[:, n].astype(F32)
        _, _, direction = adam_parts(rot, first, second, step_ref, lanes)
        VB[own_rows, n] = nt(direction.astype(BF16), RB[n, n]).astype(BF16)
        swap(VB, lanes, 1).start()
        results(1, lanes, conv, "start")
        swap(VB, lanes, 1).wait()
        OUT[2, :, n] = nn(LB[own_rows, :], VB[:, n]).astype(BF16)
        results(2, lanes, conv, "start")

    pl.when(is_conv)(lambda: rotate(True))
    pl.when(is_head)(lambda: rotate(False))
    gain_add(3)
    gainsum_ref[...] = GG[...]

    wait_borders(1, rows_way, "recv")
    strip = sum(b for _, b in sizes)
    for side, a in ((0, 0), (1, 2)):
        for sc in range(3):
            lanes = slice(strip_at[sc], strip_at[sc] + sizes[sc][1])
            x = RIMS[1, side, lanes, :]
            before, after = shifted(1, x, sc, (sizes[sc][0] + 1) * side)
            for b, value in enumerate((before, x, after)):
                Z[3 * a + b, lanes, :] = value
        total = jnp.zeros((strip, C), F32)
        for b in range(3):
            k = TAPS - 1 - (3 * a + b)
            kernel = W[:, :, k * C : (k + 1) * C].reshape(C, C)
            total = total + nt(Z[3 * a + b, 0:strip, :], kernel)
        for sc in range(3):
            start = offs[sc] + side * (sizes[sc][0] - 1) * sizes[sc][1]
            lanes = slice(strip_at[sc], strip_at[sc] + sizes[sc][1])
            PRE[start : start + sizes[sc][1], :] += total[lanes]
    outs = (gfull_hbm, ghalf_hbm, gquarter_hbm)
    picture_stores = []
    for index, (sc, row, start, count) in enumerate(segments):
        PRE[start : start + count, :] = PRE[start : start + count, :] * valid_of(sc, row)
        picture_stores.append(pltpu.make_async_copy(
            PRE.at[start : start + count, :], outs[sc].at[row], store_sem.at[HEADS + index]))
        picture_stores[-1].start()

    for ch in range(chunks):
        rows = W.at[0 : n_sends + n_arrive + 1, :, chunk_lanes[ch]]
        remote(rows, rows, ag_send.at[ch], ag_recv.at[ch, 0], sibling).wait_send()
    all_moments("wait")
    wait_borders(1, rows_way + ends_way, "send")
    for stage, d in enumerate(sum_dims):
        for st in range(1, d.size):
            remote(GX.at[stage, 0], GX.at[stage, 0], gx_send.at[stage, st], gx_recv.at[stage, st], sibling).wait_send()

    def sent_block(b, i, conv):
        _, staged, landed, sb, _ = conv_set if conv else head_set
        core_copy(b, staged.at[i], landed.at[i]).wait_send()
        place = home_of(s, b)
        gone = (here.at(d0) != place[d0]) | (here.at(d1) != place[d1]) | (here.at(d2) != place[d2])
        for way in (0, 1):
            for h in (0, 1):
                @pl.when(gone)
                def _():
                    sent = sb.at[i, rows_of_part(way, h), :]
                    remote(sent, sent, rs_send.at[b, 2 * way + h], rs_send.at[b, 2 * way + h], sibling).wait_send()

    over_blocks(sent_block)

    def results_out(conv):
        for array in range(3):
            results(array, C if conv else HD, conv, "wait")

    pl.when(is_conv)(lambda: results_out(True))
    pl.when(is_head)(lambda: results_out(False))
    for array in range(3):
        def result_in(b, i, conv):
            there = got_ref.at[array, i] if conv else goth_ref.at[array, i]
            remote(there, there, out_send.at[0, 0], out_recv.at[array, b], sibling).wait_recv()
        over_blocks(result_in)

    def stored(t, carry):
        merged_store(t).wait()
        return carry

    lax.fori_loop(0, HEADS, stored, 0)
    for store in picture_stores:
        store.wait()


def train_call(s, shapes, args):
    C, HD, HEADS, sizes = shapes["C"], shapes["HD"], shapes["HEADS"], shapes["sizes"]
    counts = [a * b for a, b in sizes]
    n_pix = sum(counts)
    half = C // 2
    tiles = half // GROUP
    blocks = TAPS + HEADS
    strip = sum(b for _, b in sizes)
    own_sends, plan = gather_plan(s)
    n_arrive = len(plan)
    n_sends = len(own_sends) + sum(len(p[2]) for p in plan)
    chunks = len(CHUNK_TAPS) + len(CHUNK_HEADS)
    d0, d1, d2 = s.chips
    most = max(d1.size, d2.size) - 1
    lanes_all = TAPS * C + HEADS * HD
    heads_pad = -(-HEADS // 8) * 8
    cut = rest = half // 2
    eight = -(-sum(a for a, _ in sizes) // 8) * 8
    dma = pltpu.SemaphoreType.DMA
    vm = pltpu.VMEM
    longest = max(s.core.size, *(d.size for d in s.chips))
    scratch = [
        vm((s.groups, GROUP, lanes_all), BF16),
        vm((TAPS, n_pix, C), BF16),
        vm((n_pix, C), BF16),
        vm((2, 2, strip, C), BF16), vm((2, 2, eight, C), F32), vm((2, 4, 8, C), F32),
        vm((2, 2, strip, C), BF16), vm((2, 2, eight, C), F32), vm((2, 4, 8, C), F32),
        vm((counts[0], HD), F32),
        vm((counts[0], n_pix - counts[0]), BF16), vm((n_pix - counts[0], counts[0]), BF16),
        vm((n_pix, C), F32), vm((n_pix, C), F32),
        vm((n_pix, C), BF16), vm((n_pix, C), BF16),
        vm((heads_pad, HD), F32), vm((4, longest, heads_pad, HD), F32),
        vm((TAPS, half, C), F32), vm((HEADS, half, HD), F32),
        vm((TAPS, half, C), BF16), vm((HEADS, half, HD), BF16),
        vm((TAPS, half, C), BF16), vm((HEADS, half, HD), BF16),
        vm((TAPS, half, C), BF16), vm((HEADS, half, HD), BF16),
        vm((8, most, cut, C), BF16), vm((8, most, rest, C), BF16),
        vm((4, most, cut, C), BF16), vm((4, most, rest, C), BF16),
        vm((d0.size - 1, cut, C), BF16), vm((d0.size - 1, rest, C), BF16),
        vm((counts[0], HEADS * HD), BF16), vm((counts[0], HEADS * HD), BF16),
        vm((TAPS, GROUP, C), F32), vm((TAPS, GROUP, C), F32), vm((HEADS, GROUP, HD), F32), vm((HEADS, GROUP, HD), F32),
        vm((TAPS, 2, GROUP, C), BF16), vm((HEADS, 2, GROUP, HD), BF16), vm((2, tiles, GROUP, C), BF16),
        vm((C, C), F32), vm((C, C), F32), vm((C, C), BF16), vm((C, C), BF16),
        vm((C, C), BF16), vm((C, C), BF16), vm((3, half, C), BF16),
        dma((chunks,)), dma((chunks, n_arrive + 1)),
        dma((2, 10)), dma((2, 10)),
        dma((blocks,)), dma((blocks,)),
        dma((blocks, 4)), dma((4, 8, most)), dma((4, 4, most)), dma((4, d0.size - 1)),
        dma((4, longest)), dma((4, longest)),
        dma((5,)), dma((HEADS + sum(a for a, _ in sizes),)),
        dma((blocks,)), dma((tiles,)), dma((2,)), dma((2,)), dma((2,)),
        dma((3, tiles * s.share)), dma((3, blocks)),
    ]
    out_shape = (
        jax.ShapeDtypeStruct((counts[0], HEADS * HD), BF16),
        *(jax.ShapeDtypeStruct((a, b, C), F32) for a, b in sizes),
        jax.ShapeDtypeStruct((heads_pad, HD), F32),
        jax.ShapeDtypeStruct((3, TAPS, GROUP, C), BF16),
        jax.ShapeDtypeStruct((3, HEADS, GROUP, HD), BF16),
    )
    vmem = pl.BlockSpec(memory_space=pltpu.VMEM)
    smem = pl.BlockSpec(memory_space=pltpu.SMEM)
    hbm = pl.BlockSpec(memory_space=pl.ANY)

    def kernel(*refs):
        train_kernel(s, shapes, refs)

    return pl.pallas_call(
        kernel,
        name="train",
        out_shape=out_shape,
        in_specs=[vmem] * 5 + [smem] * 2 + [vmem] * 4 + [hbm] * 9,
        out_specs=[hbm] * 4 + [vmem] * 3,
        scratch_shapes=scratch,
        compiler_params=pltpu.CompilerParams(collective_id=0, has_side_effects=True, vmem_limit_bytes=VMEM_LIMIT),
        cost_estimate=pl.CostEstimate(flops=13 * 10**9, bytes_accessed=10**7, transcendentals=0),
    )(*args)


def finish_kernel(shapes, refs):
    inputs, outputs, rest = refs[:16], refs[16:34], refs[34:]
    step_ref, rest = rest[0], rest[1:]
    staged, made, load_sem, store_sem = rest[:16], rest[16:-2], rest[-2], rest[-1]
    HEADS = shapes["HEADS"]
    loads = [pltpu.make_async_copy(a, b, load_sem.at[i]) for i, (a, b) in enumerate(zip(inputs, staged))]
    for load in loads:
        load.start()
    held = (*staged[:4], *made)
    stores = [pltpu.make_async_copy(a, b, store_sem.at[i]) for i, (a, b) in enumerate(zip(held, outputs))]
    got, goth, cfirst, csecond, cmaster, hfirst, hsecond, hmaster, gains, gain, gfirst, gsecond = staged[4:]
    (cgrad, hgrad, cfirst_new, csecond_new, cmaster_new, ccopy, hfirst_new, hsecond_new, hmaster_new, hcopy,
     ggrad, gfirst_new, gsecond_new, gain_new) = made

    def rows(arrays, count, first, second, master, outs):
        grad_out, first_out, second_out, master_out, copy_out = outs
        for k in range(count):
            grad_out[k] = arrays[0, k].astype(F32)
            rot = arrays[1, k].astype(F32)
            first_out[k] = beta_one * first[k] + (1.0 - beta_one) * rot
            second_out[k] = beta_two * second[k] + (1.0 - beta_two) * rot * rot
            old = master[k]
            new = old - learn_rate * (arrays[2, k].astype(F32) + weight_decay * old)
            master_out[k] = new
            copy_out[k] = new.astype(BF16)

    def wait(*indices):
        for i in indices:
            loads[i].wait()

    def store(*indices):
        for i in indices:
            stores[i].start()

    wait(4, 6, 7, 8)
    rows(got, TAPS, cfirst, csecond, cmaster, (cgrad, cfirst_new, csecond_new, cmaster_new, ccopy))
    store(4, 6, 7, 8, 9)
    wait(5, 9, 10, 11)
    rows(goth, HEADS, hfirst, hsecond, hmaster, (hgrad, hfirst_new, hsecond_new, hmaster_new, hcopy))
    store(5, 10, 11, 12, 13)
    for i in range(4):
        wait(i)
        store(i)
    wait(12, 13, 14, 15)
    total = gains[0:HEADS, :]
    first_new, second_new, direction = adam_parts(total, gfirst[...], gsecond[...], step_ref, total.shape[1])
    ggrad[...] = total
    gfirst_new[...] = first_new
    gsecond_new[...] = second_new
    gain_new[...] = gain[...] - gain_rate * (direction + weight_decay * gain[...])
    store(14, 15, 16, 17)
    for copy in stores:
        copy.wait()


def finish_call(shapes, args, like):
    smem = pl.BlockSpec(memory_space=pltpu.SMEM)
    hbm = pl.BlockSpec(memory_space=pl.ANY)
    n = len(args) - 1

    def kernel(step_ref, *refs):
        finish_kernel(shapes, (*refs[: n + len(like)], step_ref, *refs[n + len(like) :]))

    return pl.pallas_call(
        kernel,
        name="finish",
        out_shape=like,
        in_specs=[smem] + [hbm] * n,
        out_specs=[hbm] * len(like),
        scratch_shapes=[
            *(pltpu.VMEM(x.shape, x.dtype) for x in args[1:]), *(pltpu.VMEM(x.shape, x.dtype) for x in like[4:]),
            pltpu.SemaphoreType.DMA((n,)), pltpu.SemaphoreType.DMA((len(like),)),
        ],
        compiler_params=pltpu.CompilerParams(vmem_limit_bytes=VMEM_LIMIT),
    )(*args)


def shapes_of(image_full, image_half, image_quarter, heads_copy):
    return {
        "C": image_full.shape[2], "HD": heads_copy.shape[2], "HEADS": heads_copy.shape[1],
        "sizes": [p.shape[:2] for p in (image_full, image_half, image_quarter)],
    }


def per_device(
    s, image_full, image_half, image_quarter, row_pads, tile_mask, aff_scale, aff_shift, conv_copy, heads_copy, gain,
    grad_out, step_count, conv_master, conv_first, conv_second, conv_left, conv_right, heads_master, heads_first,
    heads_second, heads_left, heads_right, gain_first, gain_second,
):
    shapes = shapes_of(image_full, image_half, image_quarter, heads_copy)
    C, HEADS, HD = shapes["C"], shapes["HEADS"], shapes["HD"]

    def grouped(x):
        x = x if s.share == 1 else lax.all_gather(x, "cols", axis=0, tiled=True)
        return turned(x)

    def turned(x):
        return x.transpose(1, 0, 2)

    merged, gfull, ghalf, gquarter, gains, got, goth = train_call(s, shapes, (
        grouped(conv_copy), grouped(heads_copy), image_full, image_half, image_quarter, row_pads, step_count,
        tile_mask, aff_scale.reshape(1, C), aff_shift.reshape(1, C), gain, grad_out.reshape(-1, HEADS * HD),
        grouped(conv_first), grouped(conv_second), grouped(heads_first), grouped(heads_second),
        conv_left, conv_right, heads_left, heads_right))
    if s.share > 1:
        rows = conv_first.shape[0]
        start = lax.rem(lax.axis_index("cols"), s.share) * rows
        got, goth = (lax.dynamic_slice_in_dim(x, start, rows, 2) for x in (got, goth))
    states = [turned(x) for x in (conv_first, conv_second, conv_master, heads_first, heads_second, heads_master)]
    conv = jax.ShapeDtypeStruct(states[0].shape, F32)
    head = jax.ShapeDtypeStruct(states[3].shape, F32)
    conv_low = jax.ShapeDtypeStruct(conv.shape, BF16)
    head_low = jax.ShapeDtypeStruct(head.shape, BF16)
    small = jax.ShapeDtypeStruct(gain.shape, F32)
    like = tuple(jax.ShapeDtypeStruct(x.shape, x.dtype) for x in (merged, gfull, ghalf, gquarter)) + (
        conv, head, conv, conv, conv, conv_low, head, head, head, head_low, small, small, small, small)
    outs = finish_call(shapes, (
        step_count, merged, gfull, ghalf, gquarter, got, goth, *states, gains, gain, gain_first, gain_second), like)
    return (outs[0].reshape(grad_out.shape), *outs[1:4], *[turned(x) for x in outs[4:14]], *outs[14:])


def solution(mesh):
    s = Slice(mesh, 512 // mesh.devices.size)
    pixels, rows, all_ = P("rows", "cols", None), P(("rows", "cols"), None, None), P()
    return jax.shard_map(
        functools.partial(per_device, s),
        mesh=mesh,
        in_specs=(
            pixels, pixels, pixels, all_, P("rows", "cols"), all_, all_, rows, rows, all_, pixels, all_,
            rows, rows, rows, all_, all_, rows, rows, rows, all_, all_, all_, all_,
        ),
        out_specs=(pixels,) * 4 + (rows,) * 10 + (all_,) * 4,
        check_vma=False,
    )
```
